32 devices in a mesh: group: 2 (over y), dm: 4 (over z), tm: 2 (over x), beam: 2 (over core).
Axes of the slice: x: 2, y: 2, z: 4, core: 2. Of those that a mesh axis runs over, the one named last changes fastest.
Arguments:
- raw: bfloat16 [16, 4194304], P(('group', 'dm', 'beam'), 'tm'), parts along dimension 0
- proto: float32 [4, 16384], replicated, may hold values from -4 to 4
- delays: int32 [8, 4, 64], replicated, may hold values from 0 to 3, as said below
- widths: int32 [8], replicated, may hold values from 1 to 8, as said below
- owners: int32 [8, 1], replicated, may hold values from 0 to 3; in each aligned block of 8 rows (0 to 7, 8 to 15, ...) at most 4 rows name the same one
Outputs:
- detect: bfloat16 [16, 8, 2, 4, 8, 256], P('dm', 'group', 'beam', None, None, 'tm'), parts along dimension 1
The draws below stay inside these ranges and needn't reach their ends.
There are 2 independent parts, one for each index of `group`. The reference program is written for one: setup_inputs(seed, part) draws one part's arguments, and reference() takes and returns one part's arrays. A program takes and returns all parts, laid end to end along the dimension named above; an argument that names none is the same for every part. Nothing has to cross between parts.
Inputs may be any that keep to these rules, and one draw needn't show every extreme that they name: `delays`: 3 occurs in every draw. `widths`: 8 occurs in every draw. `owners`: each owner holds at most 4 DM blocks, and some owner holds exactly 4.
All inputs are finite; a program needn't handle non-finite values.
Results may differ from the reference program's by a relative error of at most 0.014.
Values may be sent and summed in bfloat16 or wider, within the bound.
No kernel may reach another device: no remote copies, remote signals or barrier semaphores. Data moves between devices by JAX's collectives and lax.ppermute only.
A program may use at most 128 MiB of HBM per device.

```python
import math
import jax
import jax.numpy as jnp
import numpy as np
from jax import lax

NCH = 16384
DFT_A = 128
DFT_B = 128
TAPS = 4
NBLK = 64
CBW = 256
SPECTRA = 256
SAMPLES = 4194304
BEAM_SUB = 2
BEAMS = 8
PFB_BLK = 16
FD = 4
TT = 8
MAXT = 3
WMAX = 8
NBOX = 8
TRIALS = 4
NDMB = 8
CAP = 4
SLOTS = 16
HALO = 31
N_DM = 4


def draw_raw(key, part):
    key_noise = jax.random.fold_in(key, 11)
    key_level = jax.random.fold_in(key, 12)
    steps = jnp.arange(SPECTRA, dtype=jnp.float32) / max(SPECTRA - 1, 1)
    jitter = jax.random.uniform(key_level, (BEAMS, SPECTRA, 1), jnp.float32)
    values = jax.random.normal(key_noise, (BEAMS, SPECTRA, NCH), jnp.float32)
    level = jnp.power(10.0, 0.5 * steps[None, :, None] + 0.5 * jitter)
    return (values * jnp.sqrt(level)).reshape(BEAMS, SAMPLES).astype(jnp.bfloat16)


def draw_delays(key, part):
    block = jnp.arange(NDMB, dtype=jnp.int32)[:, None, None]
    trial = jnp.arange(TRIALS, dtype=jnp.int32)[None, :, None]
    channel = jnp.arange(NBLK, dtype=jnp.int32)[None, None, :]
    level = block * TRIALS + trial
    base = level * (NBLK - 1 - channel) * MAXT // max((NDMB * TRIALS - 1) * (NBLK - 1), 1)
    jitter = jax.random.randint(jax.random.fold_in(key, 21), (NDMB, TRIALS, NBLK), 0, 2)
    return jnp.minimum(base + jitter, MAXT).astype(jnp.int32)


def draw_widths(key, part):
    values = jax.random.randint(jax.random.fold_in(key, 31), (NBOX,), 1, WMAX + 1)
    where_top = jax.random.randint(jax.random.fold_in(key, 32), (), 0, NBOX)
    index = jnp.arange(NBOX, dtype=jnp.int32)
    return jnp.where(index == where_top, WMAX, values).astype(jnp.int32)


def shared_out(own_key, own, number, rows, amount, top, reach, skew):
    sequence = jax.random.permutation(own_key, amount)
    packed, usual = portions_of(amount, rows * top, reach, skew, True), portions_of(amount, rows * top, reach, skew, False)
    places = jnp.arange(amount)

    def named(tallies, rotation):
        used = int((tallies > 0).sum())
        fixed = max(1, used // 4)
        moved = fixed + (places - fixed + rotation * (used - fixed)) % max(1, amount - fixed)
        return jnp.zeros((amount,), jnp.int32).at[sequence[jnp.where(places < fixed, places, moved)]].set(jnp.asarray(tallies, jnp.int32))

    tallies = jnp.where(number % 4 == 0, named(packed, number // 4), named(usual, number - number // 4 - 1))
    mixed = jax.random.permutation(jax.random.fold_in(own, 3), amount)
    donor, taker = mixed[0:amount // 2 * 2:2], mixed[1:amount // 2 * 2:2]
    room = jnp.minimum(tallies[donor] - 1, reach - tallies[taker]) // 2
    room = jnp.where((donor == sequence[0]) | (taker == sequence[0]) | (tallies[taker] == 0), 0, jnp.maximum(room, 0))
    moved = jax.random.randint(jax.random.fold_in(own, 4), (amount // 2,), 0, 1 << 20) % (room + 1)
    tallies = tallies.at[donor].add(-moved).at[taker].add(moved)
    members = jnp.searchsorted(jnp.cumsum(tallies), jnp.arange(rows * top), side="right").astype(jnp.int32)
    table = members.reshape(top, rows).T
    table = table[jax.random.permutation(jax.random.fold_in(own, 1), rows)]
    rotation = jax.random.randint(jax.random.fold_in(own, 2), (rows, 1), 0, top)
    return jnp.take_along_axis(table, (jnp.arange(top)[None, :] + rotation) % top, axis=1)


def portions_of(number_of, total, bound, skew, full):
    weights = [(1 << 20) // math.isqrt(rank ** skew) + 1 for rank in range(1, number_of + 1)]
    largest = bound if full else min(bound, max(-(-total // number_of), total * weights[0] // sum(weights)))
    least = 1 if total - largest >= number_of - 1 else 0
    counts, rest = [largest] + [least] * (number_of - 1), total - largest - least * (number_of - 1)
    while rest > 0:
        candidates = [i for i in range(1, number_of) if counts[i] < largest] or [i for i in range(1, number_of) if counts[i] < bound]
        pool, budget = sum([weights[i] for i in candidates]), rest
        for i in candidates:
            more = min(bound - counts[i], max(1, budget * weights[i] // pool), rest)
            counts[i] = counts[i] + more
            rest = rest - more
    return np.array(counts)


def centred(rng, shape, scale, bound, held_as=jnp.bfloat16):
    values = jax.random.normal(rng, shape, jnp.float32) * scale
    return jnp.minimum(jnp.maximum(values, -bound), bound).astype(held_as)


def setup_inputs(seed: int = 0, part: int = 0) -> dict:
    seeds = jax.random.split(jax.random.key(seed), 6)
    part_keys = jax.random.split(jax.random.fold_in(seeds[5], part), 6)
    raw = draw_raw(jax.random.fold_in(jax.random.fold_in(seeds[5], part), 71), part)
    proto = centred(seeds[1], (TAPS, NCH), 1.0, 4.0, jnp.float32)
    delays = draw_delays(jax.random.fold_in(seeds[5], 71), part)
    widths = draw_widths(jax.random.fold_in(seeds[5], 71), part)
    owners_keys = jax.random.split(jax.random.fold_in(seeds[4], 1), NDMB // NDMB)
    owners_turns = jax.random.permutation(jax.random.fold_in(seeds[4], 3), NDMB // NDMB)
    owners = jax.vmap(lambda own, number: shared_out(jax.random.fold_in(seeds[4], 2), own, number, NDMB, N_DM, 1, CAP, 2))(owners_keys, owners_turns).reshape((NDMB, 1))
    return dict(raw=raw, proto=proto, delays=delays, widths=widths, owners=owners)


def dft_tables(size):
    index = jnp.arange(size, dtype=jnp.int32)
    product = index[:, None] * index[None, :] % size
    angle = product.astype(jnp.float32) * (2.0 * math.pi / size)
    return (jnp.cos(angle).astype(jnp.bfloat16), jnp.sin(angle).astype(jnp.bfloat16))

def twiddle_tables(rows, cols, total):
    first = jnp.arange(rows, dtype=jnp.int32)
    second = jnp.arange(cols, dtype=jnp.int32)
    product = first[:, None] * second[None, :] % total
    angle = product.astype(jnp.float32) * (2.0 * math.pi / total)
    return (jnp.cos(angle), jnp.sin(angle))

def spectra_power(window_frames, proto):
    count = window_frames.shape[0] - TAPS + 1
    hp = lax.Precision.HIGHEST
    acc = window_frames[0:count].astype(jnp.float32) * proto[0]
    for tap in range(1, TAPS):
        acc = acc + window_frames[tap:tap + count].astype(jnp.float32) * proto[tap]
    frames_bf = acc.astype(jnp.bfloat16).astype(jnp.float32).reshape(count, DFT_A, DFT_B)
    cos_a, sin_a = dft_tables(DFT_A)
    cos_b, sin_b = dft_tables(DFT_B)
    tw_cos, tw_sin = twiddle_tables(DFT_B, DFT_A, NCH)
    a_re = jnp.einsum('kab,fa->kbf', frames_bf, cos_a.astype(jnp.float32), precision=hp)
    a_im = -jnp.einsum('kab,fa->kbf', frames_bf, sin_a.astype(jnp.float32), precision=hp)
    t_re = (a_re * tw_cos + a_im * tw_sin).astype(jnp.bfloat16).astype(jnp.float32)
    t_im = (a_im * tw_cos - a_re * tw_sin).astype(jnp.bfloat16).astype(jnp.float32)
    cb = cos_b.astype(jnp.float32)
    sb = sin_b.astype(jnp.float32)
    c_re = jnp.einsum('kbf,gb->kgf', t_re, cb, precision=hp) + jnp.einsum('kbf,gb->kgf', t_im, sb, precision=hp)
    c_im = jnp.einsum('kbf,gb->kgf', t_im, cb, precision=hp) - jnp.einsum('kbf,gb->kgf', t_re, sb, precision=hp)
    power = (c_re * c_re + c_im * c_im) * (1.0 / (TAPS * NCH))
    return power.reshape(count, NCH)

def fine_masks(groups, width):
    block = jnp.arange(groups, dtype=jnp.int32)[:, None]
    inner = jnp.arange(width, dtype=jnp.int32)[None, :]
    fine = block * FD * (width - 1 - inner) // (groups * (width - 1))
    return jnp.stack([(fine == step).astype(jnp.float32) for step in range(FD)])

def beam_subbands(samples, proto, masks):
    frames = samples.reshape(SPECTRA, NCH)
    padded = jnp.concatenate([jnp.zeros((TAPS - 1, NCH), jnp.bfloat16), frames], 0)

    def block_power(index):
        start = (index * PFB_BLK).astype(jnp.int32)
        window = lax.dynamic_slice_in_dim(padded, start, PFB_BLK + TAPS - 1, 0)
        return spectra_power(window, proto)
    power = lax.map(block_power, jnp.arange(SPECTRA // PFB_BLK, dtype=jnp.int32)).reshape(SPECTRA, NCH)
    band = lax.optimization_barrier(jnp.sum(power, 0)) / SPECTRA
    ratio = power / (band + 1e-06)
    flat = (ratio - lax.optimization_barrier(jnp.mean(ratio, 1, keepdims=True))).astype(jnp.bfloat16)
    flat = jnp.concatenate([jnp.zeros((FD - 1, NCH), jnp.bfloat16), flat], 0)
    view = flat.reshape(SPECTRA + FD - 1, NBLK, CBW).astype(jnp.float32)
    total = jnp.zeros((NDMB, NBLK, SPECTRA), jnp.float32)
    for step in range(FD):
        part = view[FD - 1 - step:FD - 1 - step + SPECTRA]
        total = total + jnp.einsum('kci,gi->gck', part, masks[step], precision=lax.Precision.HIGHEST)
    return (total * (1.0 / math.sqrt(CBW))).astype(jnp.bfloat16)

def dedisperse(extended, delays, count):
    length = count + WMAX - 1
    total = 0.0
    for value in range(MAXT + 1):
        start = (MAXT - value) * TT
        window = extended[..., start:start + length].astype(jnp.float32)
        mask = (delays == value).astype(jnp.float32)
        total = total + jnp.einsum('rgck,gjc->rgjk', window, mask, precision=lax.Precision.HIGHEST)
    return total * (1.0 / math.sqrt(NBLK))

def boxcar(series, widths, count):
    lags = jnp.arange(WMAX, dtype=jnp.int32)
    weights = (lags[None, :] < widths[:, None]).astype(jnp.float32) / jnp.sqrt(widths.astype(jnp.float32))[:, None]
    stacked = jnp.stack([series[..., WMAX - 1 - lag:WMAX - 1 - lag + count] for lag in range(WMAX)], -2)
    return jnp.einsum('rgjik,wi->rgjwk', stacked, weights, precision=lax.Precision.HIGHEST)

def slot_table(owners, owner_count, capacity):
    owner = owners[:, 0]
    groups = owner.shape[0]
    index = jnp.arange(groups, dtype=jnp.int32)
    same = owner[:, None] == owner[None, :]
    earlier = index[None, :] < index[:, None]
    rank = lax.optimization_barrier(jnp.sum((same & earlier).astype(jnp.int32), 1))
    hit_owner = owner[None, None, :] == jnp.arange(owner_count, dtype=jnp.int32)[:, None, None]
    hit_slot = rank[None, None, :] == jnp.arange(capacity, dtype=jnp.int32)[None, :, None]
    return (hit_owner & hit_slot).astype(jnp.int32)

def reference(raw, proto, delays, widths, owners):
    masks = fine_masks(NDMB, CBW)

    def one_beam(samples):
        return beam_subbands(samples, proto, masks)
    subs = lax.map(one_beam, raw)
    extended = jnp.concatenate([jnp.zeros((BEAMS, NDMB, NBLK, HALO), jnp.bfloat16), subs], -1)
    series = dedisperse(extended, delays, SPECTRA)
    box = boxcar(series, widths, SPECTRA).astype(jnp.bfloat16)
    table = slot_table(owners, N_DM, CAP).astype(jnp.float32)
    placed = jnp.einsum('osg,rgjwk->osrjwk', table, box.astype(jnp.float32), precision=lax.Precision.HIGHEST)
    return placed.reshape(SLOTS, N_DM, BEAM_SUB, TRIALS, NBOX, SPECTRA).astype(jnp.bfloat16)
```

```python
import functools
import math

import jax
import jax.numpy as jnp
import numpy as np
from jax import lax
from jax.experimental import pallas as pl
from jax.experimental.pallas import tpu as pltpu
from jax.sharding import PartitionSpec as P

DFT_A = 128
NBLK = 64
FD = 4
TT = 8
MAXT = 3
WMAX = 8
LANES = 128
CHUNK = 16
LIMIT = 56 * 1024 * 1024


def ceil_to(value, unit):
    return -(-value // unit) * unit


def angle_tables(rows, cols, total):
    product = np.arange(rows)[:, None] * np.arange(cols)[None, :] % total
    angle = product.astype(np.float64) * (2.0 * math.pi / total)
    return np.cos(angle), np.sin(angle)


class Sizes:
    def __init__(self, taps, channels, spec, groups, n_dm, n_tm):
        self.taps, self.channels, self.spec, self.groups = taps, channels, spec, groups
        self.n_dm, self.n_tm = n_dm, n_tm
        self.side = channels // DFT_A
        self.half = DFT_A // 2 + 1
        self.rows = ceil_to(self.half, 8)
        self.rows16 = ceil_to(self.half, 16)
        self.hist = taps - 1
        self.raw_rows = self.hist * DFT_A
        self.bounds = n_tm - 1
        self.msg_rows = self.bounds * self.raw_rows + 2 * self.rows
        self.capacity = 2 * (groups // n_dm)


def dft_constants(z):
    cos_a, sin_a = angle_tables(DFT_A, DFT_A, DFT_A)
    first = np.zeros((2 * z.rows, DFT_A))
    first[: z.half] = cos_a[: z.half]
    first[z.rows : z.rows + z.half] = -sin_a[: z.half]
    tw_cos, tw_sin = np.zeros((2, z.rows, z.side))
    tw_cos[: z.half], tw_sin[: z.half] = angle_tables(z.half, z.side, z.channels)
    cos_b, sin_b = angle_tables(z.side, z.side, z.side)
    second = np.block([[cos_b, -sin_b], [sin_b, cos_b]])
    return (
        jnp.asarray(first, jnp.bfloat16),
        jnp.asarray(np.stack([tw_cos, tw_sin]), jnp.float32),
        jnp.asarray(second, jnp.bfloat16),
    )


def mask_constants(z):
    width = z.channels // NBLK
    fine = np.arange(z.groups)[:, None] * FD * (width - 1 - np.arange(width))[None, :] // (z.groups * (width - 1))
    parities = width // DFT_A
    masks = np.zeros((2, FD, parities, z.groups, z.rows16))
    for step in range(FD):
        for parity in range(parities):
            hit = fine[:, parity * DFT_A : (parity + 1) * DFT_A] == step
            masks[0, step, parity, :, : z.half] = hit[:, : z.half]
            masks[1, step, parity, :, 1 : z.half - 1] = hit[:, : z.half - 1 : -1]
    weight = np.zeros((z.rows, LANES))
    weight[: z.half] = 2.0 / z.channels
    weight[0] = weight[z.half - 1] = 1.0 / z.channels
    expand = np.zeros((NBLK, 2 * z.side))
    lane = np.arange(z.side)
    expand[lane // parities, lane] = 1
    expand[(z.side - 1 - lane) // parities, z.side + lane] = 1
    return (
        jnp.asarray(masks.reshape(-1, z.rows16), jnp.bfloat16),
        jnp.asarray(weight, jnp.float32),
        jnp.asarray(expand, jnp.bfloat16),
    )


def fill_frames(z, load, pr_ref, y_ref, count):
    for block in range(DFT_A // 16):
        rows = pl.ds(block * 16, 16)
        taps = [pr_ref[tap, rows, :] for tap in range(z.taps)]
        window = [load(k, block) for k in range(z.hist)]
        for k in range(count):
            window.append(load(k + z.hist, block))
            acc = window[0] * taps[0]
            for tap in range(1, z.taps):
                acc = acc + window[tap] * taps[tap]
            y_ref[rows, k * LANES : (k + 1) * LANES] = acc.astype(jnp.bfloat16)
            window.pop(0)


def transform(z, y_ref, first_ref, twiddle_ref, second_ref, a_ref, t_ref, count):
    a_ref[...] = jnp.dot(first_ref[...], y_ref[...], preferred_element_type=jnp.float32)
    pad = jnp.zeros((z.rows16 - z.rows, LANES), jnp.float32)
    for k in range(count):
        lanes = slice(k * LANES, (k + 1) * LANES)
        re, im = a_ref[: z.rows, lanes], a_ref[z.rows :, lanes]
        cos, sin = twiddle_ref[0], twiddle_ref[1]
        t_re = re * cos + im * sin
        t_im = im * cos - re * sin
        rows = slice(k * z.rows16, (k + 1) * z.rows16)
        t_ref[rows, :LANES] = jnp.concatenate([t_re, pad]).astype(jnp.bfloat16)
        t_ref[rows, LANES:] = jnp.concatenate([t_im, pad]).astype(jnp.bfloat16)
    c = jnp.dot(t_ref[...], second_ref[...], preferred_element_type=jnp.float32)
    out = []
    for k in range(count):
        part = c[k * z.rows16 : k * z.rows16 + z.rows]
        re, im = part[:, :LANES], part[:, LANES:]
        out.append(re * re + im * im)
    return out


def channelize(z, raw_ref, proto_ref, first_ref, twiddle_ref, second_ref,
               power_ref, pr_ref, band_ref, msg_ref, buf, y_ref, a_ref, t_ref, sems):
    chunks = z.spec // CHUNK
    span = CHUNK * z.channels
    front = z.hist * z.channels
    copies = [
        pltpu.make_async_copy(
            raw_ref.at[:, pl.ds(i * span, span)], buf.at[:, pl.ds(front + i * span, span)], sems.at[i]
        )
        for i in range(chunks)
    ]
    for copy in copies:
        copy.start()
    buf[:, :front] = jnp.zeros((1, front), jnp.bfloat16)
    for tap in range(z.taps):
        pr_ref[tap] = proto_ref[tap : tap + 1, :].reshape(DFT_A, LANES)
    early = lax.axis_index("tm") > 0
    band_ref[...] = jnp.zeros_like(band_ref)

    def step(i, carry):
        pltpu.make_async_copy(
            raw_ref.at[:, pl.ds(0, span)], buf.at[:, pl.ds(front, span)], sems.at[i]
        ).wait()
        base = i * span

        def load(k, block):
            start = pl.multiple_of(base + k * z.channels + block * 16 * LANES, 16 * LANES)
            return buf[:, pl.ds(start, 16 * LANES)].astype(jnp.float32).reshape(16, LANES)

        fill_frames(z, load, pr_ref, y_ref, CHUNK)
        power = transform(z, y_ref, first_ref, twiddle_ref, second_ref, a_ref, t_ref, CHUNK)
        late = power[z.hist]
        for k in range(z.hist + 1, CHUNK):
            late = late + power[k]
        head = power[0]
        for k in range(1, z.hist):
            head = head + power[k]
        skip = jnp.logical_and(i == 0, early)
        band_ref[...] = band_ref[...] + late + jnp.where(skip, 0.0, head)
        for k in range(CHUNK):
            power_ref[i * CHUNK + k] = power[k]
        return carry

    lax.fori_loop(0, chunks, step, 0)

    def spectrum(start):
        start = pl.multiple_of(start, z.channels)
        return buf[:, pl.ds(start, z.channels)].astype(jnp.float32).reshape(DFT_A, LANES).astype(jnp.bfloat16)

    row = 0
    if z.n_tm == 2:
        starts = [jnp.where(early, z.hist, z.spec) * z.channels]
    else:
        starts = [z.spec * z.channels, z.hist * z.channels]
    for start in starts:
        for k in range(z.hist):
            msg_ref[row : row + DFT_A] = spectrum(start + k * z.channels)
            row += DFT_A
    high = band_ref[...].astype(jnp.bfloat16)
    msg_ref[row : row + z.rows] = high
    msg_ref[row + z.rows : row + 2 * z.rows] = (band_ref[...] - high.astype(jnp.float32)).astype(jnp.bfloat16)


def search(z, power_ref, pr_ref, band_ref, own_ref, other_ref, first_ref, twiddle_ref, second_ref,
           masks_ref, weight_ref, expand_ref, delays_ref, owners_ref,
           out_ref, y_ref, a_ref, t_ref, bound_ref, inv_ref, sums_ref, mean_ref, f_ref, g_ref, sub_ref, del_ref):
    me = lax.axis_index("tm")
    groups, spec = z.groups, z.spec
    total = band_ref[...]
    lo = z.bounds * z.raw_rows
    total = total + (
        other_ref[lo : lo + z.rows].astype(jnp.float32) + other_ref[lo + z.rows : lo + 2 * z.rows].astype(jnp.float32)
    )
    swap = jnp.logical_and(me > 0, z.n_tm == 2)
    y_ref[:, z.hist * LANES :] = jnp.zeros((DFT_A, LANES), jnp.bfloat16)
    for b in range(z.bounds):

        def load(k, block, b=b):
            start = b * z.raw_rows + (k % z.hist) * DFT_A + block * 16
            own = own_ref[start : start + 16].astype(jnp.float32)
            other = other_ref[start : start + 16].astype(jnp.float32)
            return jnp.where(swap, other, own) if k < z.hist else jnp.where(swap, own, other)

        fill_frames(z, load, pr_ref, y_ref, z.hist)
        power = transform(z, y_ref, first_ref, twiddle_ref, second_ref, a_ref, t_ref, z.hist)
        for k in range(z.hist):
            total = total + power[k]
            bound_ref[b * z.hist + k] = power[k]
    scale = float(z.taps * z.channels)
    inv_ref[...] = 1.0 / (total * (1.0 / (z.spec * z.n_tm)) + 1e-6 * scale)
    mine = jnp.maximum(me - 1, 0) * z.hist

    def head_power(k):
        return jnp.where(me > 0, bound_ref[mine + k], power_ref[k])

    weighted = weight_ref[...] * inv_ref[...]

    def fold(value):
        value = value * weighted
        return jnp.sum(value.reshape(z.rows // 8, 8, LANES), 0)

    def sum_step(i, carry):
        for k in range(CHUNK):
            at = pl.multiple_of((i * CHUNK + k) * 8, 8)
            sums_ref[pl.ds(at, 8)] = fold(power_ref[i * CHUNK + k])
        return carry

    lax.fori_loop(0, spec // CHUNK, sum_step, 0)
    for k in range(z.hist):
        sums_ref[k * 8 : k * 8 + 8] = fold(head_power(k))
    acc = sums_ref[pl.ds(0, spec, stride=8)]
    for j in range(1, 8):
        acc = acc + sums_ref[pl.ds(j, spec, stride=8)]
    mean_ref[...] = jnp.broadcast_to(jnp.sum(acc, 1, keepdims=True), (spec, LANES))
    gap = (FD - 1) * LANES
    g_ref[:, :gap] = jnp.zeros((g_ref.shape[0], gap), jnp.float32)
    g_ref[:, gap + spec * LANES :] = jnp.zeros((g_ref.shape[0], gap), jnp.float32)
    f_ref[z.rows :] = jnp.zeros((z.rows16 - z.rows, CHUNK * LANES), jnp.float32)

    def flat_step(i, carry):
        for k in range(CHUNK):
            at = i * CHUNK + k
            power = power_ref[at]
            if k < z.hist:
                power = jnp.where(jnp.logical_and(me > 0, i == 0), bound_ref[mine + k], power)
            f_ref[: z.rows, k * LANES : (k + 1) * LANES] = power * inv_ref[...] - mean_ref[pl.ds(at, 1)]
        lanes = pl.ds(pl.multiple_of(gap + i * CHUNK * LANES, LANES), CHUNK * LANES)
        g_ref[:, lanes] = jnp.dot(masks_ref[...], f_ref[...].astype(jnp.bfloat16), preferred_element_type=jnp.float32)
        return carry

    lax.fori_loop(0, spec // CHUNK, flat_step, 0)
    parities = z.channels // NBLK // DFT_A
    lane = lax.broadcasted_iota(jnp.int32, (groups, LANES), 1)
    block = parities * groups

    def sub_step(k, carry):
        for m in range(2):
            acc = None
            for step in range(FD):
                lanes = pl.ds(pl.multiple_of((k + FD - 1 - step) * LANES, LANES), LANES)
                row = (m * FD + step) * block
                part = g_ref[row : row + groups, lanes]
                for parity in range(1, parities):
                    hit = (lane if m == 0 else LANES - 1 - lane) % parities == parity
                    part = jnp.where(hit, g_ref[row + parity * groups : row + (parity + 1) * groups, lanes], part)
                acc = part if acc is None else acc + part
            sub_ref[m, pl.ds(pl.multiple_of(k * groups, 8), groups)] = acc
        return carry

    length = spec + FD - 1
    lax.fori_loop(0, length, sub_step, 0)
    stop = ceil_to(length, 16)
    sub_ref[:, length * groups :] = jnp.zeros((2, (stop - length) * groups, LANES), jnp.float32)
    trials = delays_ref.shape[1]
    out_ref[...] = jnp.zeros_like(out_ref)
    wide = 2 * LANES
    del_ref[...] = jnp.zeros_like(del_ref)
    empty = jnp.zeros((wide - stop, wide), jnp.bfloat16)
    unit = 1.0 / (math.sqrt(z.channels // NBLK) * math.sqrt(NBLK))
    for g in range(groups):
        del_ref[:trials, :NBLK] = delays_ref[g].astype(jnp.float32)
        spread = jnp.dot(del_ref[:, :NBLK].astype(jnp.bfloat16), expand_ref[...], preferred_element_type=jnp.float32)
        hits = jnp.concatenate([jnp.where(spread == value, unit, 0.0) for value in range(MAXT + 1)])
        both = [sub_ref[m, pl.ds(g, stop, stride=groups)].astype(jnp.bfloat16) for m in range(2)]
        series = jnp.concatenate([jnp.concatenate(both, 1), empty])
        found = lax.dot_general(
            hits.astype(jnp.bfloat16), series, (((1,), (1,)), ((), ())), preferred_element_type=jnp.float32
        )
        dd = found[:8]
        for value in range(1, MAXT + 1):
            dd = dd + pltpu.roll(found[value * 8 : value * 8 + 8], value * TT, 1)
        owner = owners_ref[g, 0]
        rank = jnp.int32(0)
        for earlier in range(g):
            rank = rank + jnp.where(owners_ref[earlier, 0] == owner, 1, 0)
        out_ref[owner * z.n_tm + me, rank] = dd[:trials, :LANES]
        late = pltpu.roll(dd, wide - (spec - WMAX + 1), 1)

        @pl.when(me + 1 < z.n_tm)
        def _(late=late, owner=owner, rank=rank):
            out_ref[owner * z.n_tm + me + 1, rank] = late[:trials, :LANES]


def boxes(z, recv_ref, widths_ref, out_ref, d_ref):
    me = lax.axis_index("tm")
    trials = recv_ref.shape[2]
    rank = lax.broadcasted_iota(jnp.int32, (8, LANES), 0)
    count = widths_ref.shape[0]
    width = jnp.zeros((8, LANES), jnp.int32)
    for w in range(count):
        width = jnp.where(rank == w, widths_ref[w], width)
    norm = 1.0 / jnp.sqrt(width.astype(jnp.float32))
    weights = [jnp.where(width > lag, norm, 0.0) for lag in range(WMAX)]
    prior = WMAX - 1
    zero = jnp.zeros((8, LANES), jnp.float32)
    before = jnp.maximum(me - 1, 0)
    rows = z.capacity * trials
    for d in range(z.n_dm):
        own = recv_ref[d * z.n_tm + me].reshape(rows, LANES)
        past = recv_ref[d * z.n_tm + before].reshape(rows, LANES)
        past = jnp.where(me > 0, past, 0.0)
        wide = jnp.concatenate([own, jnp.zeros_like(own)], 1)
        wide = pltpu.roll(wide, prior, 1) + jnp.concatenate([past, jnp.zeros_like(past)], 1)
        for lag in range(WMAX):
            shift = prior - lag
            d_ref[lag] = (pltpu.roll(wide, 2 * LANES - shift, 1) if shift else wide)[:, :LANES]
        for s in range(z.capacity):
            for j in range(trials):
                acc = None
                for lag in range(WMAX):
                    part = d_ref[lag, s * trials + j : s * trials + j + 1, :] * weights[lag]
                    acc = part if acc is None else acc + part
                out_ref[s, d, 0, j] = acc[:count].astype(jnp.bfloat16)


def vmem_spec():
    return pl.BlockSpec(memory_space=pltpu.VMEM)


def smem_spec():
    return pl.BlockSpec(memory_space=pltpu.SMEM)


def shards(n_dm, n_tm, raw, proto, delays, widths, owners):
    taps, channels = proto.shape
    groups, trials, _ = delays.shape
    z = Sizes(taps, channels, raw.shape[1] // channels, groups, n_dm, n_tm)
    first, twiddle, second = dft_constants(z)
    masks, weight, expand = mask_constants(z)
    params = pltpu.CompilerParams(vmem_limit_bytes=LIMIT)
    own_rows = z.raw_rows * (1 if n_tm == 2 else 2) + 2 * z.rows
    f32, bf16 = jnp.float32, jnp.bfloat16
    power, pr, band, msg = pl.pallas_call(
        functools.partial(channelize, z),
        out_shape=(
            jax.ShapeDtypeStruct((z.spec, z.rows, LANES), f32),
            jax.ShapeDtypeStruct((taps, DFT_A, LANES), f32),
            jax.ShapeDtypeStruct((z.rows, LANES), f32),
            jax.ShapeDtypeStruct((own_rows, LANES), bf16),
        ),
        in_specs=[pl.BlockSpec(memory_space=pl.ANY)] + [vmem_spec()] * 4,
        out_specs=[vmem_spec()] * 4,
        scratch_shapes=[
            pltpu.VMEM((1, (z.spec + z.hist) * channels), bf16),
            pltpu.VMEM((DFT_A, CHUNK * LANES), bf16),
            pltpu.VMEM((2 * z.rows, CHUNK * LANES), f32),
            pltpu.VMEM((CHUNK * z.rows16, 2 * LANES), bf16),
            pltpu.SemaphoreType.DMA((z.spec // CHUNK,)),
        ],
        compiler_params=params,
        name="channelize",
    )(raw, proto, first, twiddle, second)
    if n_tm == 2:
        own, other = msg, lax.ppermute(msg, "tm", [(0, 1), (1, 0)])
    else:
        every = lax.all_gather(msg, "tm")
        lasts = every[:-1, : z.raw_rows].reshape(-1, LANES)
        firsts = every[1:, z.raw_rows : 2 * z.raw_rows].reshape(-1, LANES)
        parts = every[:, 2 * z.raw_rows :].astype(f32).reshape(n_tm, 2, z.rows, LANES)
        rest = jnp.sum(parts, (0, 1)) - band
        high = rest.astype(bf16)
        pair = jnp.concatenate([high, (rest - high.astype(f32)).astype(bf16)])
        own, other = jnp.concatenate([lasts, pair]), jnp.concatenate([firsts, pair])
    length = ceil_to(z.spec + FD - 1, 16)
    out = pl.pallas_call(
        functools.partial(search, z),
        out_shape=jax.ShapeDtypeStruct((n_dm * n_tm, z.capacity, trials, LANES), f32),
        in_specs=[vmem_spec()] * 12 + [smem_spec()],
        out_specs=vmem_spec(),
        scratch_shapes=[
            pltpu.VMEM((DFT_A, (z.hist + 1) * LANES), bf16),
            pltpu.VMEM((2 * z.rows, (z.hist + 1) * LANES), f32),
            pltpu.VMEM((z.hist * z.rows16, 2 * LANES), bf16),
            pltpu.VMEM((z.bounds * z.hist, z.rows, LANES), f32),
            pltpu.VMEM((z.rows, LANES), f32),
            pltpu.VMEM((z.spec * 8, LANES), f32),
            pltpu.VMEM((z.spec, LANES), f32),
            pltpu.VMEM((z.rows16, CHUNK * LANES), f32),
            pltpu.VMEM((masks.shape[0], (z.spec + 2 * (FD - 1)) * LANES), f32),
            pltpu.VMEM((2, length * groups, LANES), f32),
            pltpu.VMEM((8, LANES), f32),
        ],
        compiler_params=params,
        name="search",
    )(power, pr, band, own, other, first, twiddle, second, masks, weight, expand, delays, owners)
    recv = lax.all_to_all(out, ("dm", "tm"), split_axis=0, concat_axis=0, tiled=True)
    return pl.pallas_call(
        functools.partial(boxes, z),
        out_shape=jax.ShapeDtypeStruct((z.capacity, n_dm, 1, trials, widths.shape[0], z.spec), bf16),
        in_specs=[vmem_spec(), smem_spec()],
        out_specs=vmem_spec(),
        scratch_shapes=[pltpu.VMEM((WMAX, z.capacity * trials, LANES), f32)],
        compiler_params=params,
        name="boxes",
    )(recv, widths)


def solution(mesh):
    sizes = dict(mesh.shape)
    return jax.shard_map(
        functools.partial(shards, sizes["dm"], sizes["tm"]),
        mesh=mesh,
        in_specs=(P(("group", "dm", "beam"), "tm"), P(), P(), P(), P()),
        out_specs=P("dm", "group", "beam", None, None, "tm"),
        check_vma=False,
    )
```

```python
import functools
import math

import jax
import jax.numpy as jnp
import numpy as np
from jax import lax
from jax.experimental import pallas as pl
from jax.experimental.pallas import tpu as pltpu
from jax.sharding import PartitionSpec as P

DFT_A = 128
NBLK = 64
FD = 4
TT = 8
MAXT = 3
WMAX = 8
LANES = 128
CHUNK = 16
LIMIT = 32 * 1024 * 1024


def ceil_to(value, unit):
    return -(-value // unit) * unit


def angle_tables(rows, cols, total):
    product = np.arange(rows)[:, None] * np.arange(cols)[None, :] % total
    angle = product.astype(np.float64) * (2.0 * math.pi / total)
    return np.cos(angle), np.sin(angle)


class Sizes:
    def __init__(self, taps, channels, spec, groups, n_dm, n_tm):
        self.taps, self.channels, self.spec, self.groups = taps, channels, spec, groups
        self.n_dm, self.n_tm = n_dm, n_tm
        self.side = channels // DFT_A
        self.half = DFT_A // 2 + 1
        self.rows = ceil_to(self.half, 8)
        self.rows16 = ceil_to(self.half, 16)
        self.hist = taps - 1
        self.raw_rows = self.hist * DFT_A
        self.bounds = n_tm - 1
        self.msg_rows = self.bounds * self.raw_rows + 2 * self.rows
        self.capacity = 2 * (groups // n_dm)


def dft_constants(z):
    cos_a, sin_a = angle_tables(DFT_A, DFT_A, DFT_A)
    first = np.zeros((2 * z.rows, DFT_A))
    first[: z.half] = cos_a[: z.half]
    first[z.rows : z.rows + z.half] = -sin_a[: z.half]
    tw_cos, tw_sin = np.zeros((2, z.rows, z.side))
    tw_cos[: z.half], tw_sin[: z.half] = angle_tables(z.half, z.side, z.channels)
    cos_b, sin_b = angle_tables(z.side, z.side, z.side)
    second = np.block([[cos_b, -sin_b], [sin_b, cos_b]])
    return (
        jnp.asarray(first, jnp.bfloat16),
        jnp.asarray(np.stack([tw_cos, tw_sin]), jnp.float32),
        jnp.asarray(second, jnp.bfloat16),
    )


def mask_constants(z):
    width = z.channels // NBLK
    fine = np.arange(z.groups)[:, None] * FD * (width - 1 - np.arange(width))[None, :] // (z.groups * (width - 1))
    parities = width // DFT_A
    masks = np.zeros((2, FD, parities, z.groups, z.rows16))
    for step in range(FD):
        for parity in range(parities):
            hit = fine[:, parity * DFT_A : (parity + 1) * DFT_A] == step
            masks[0, step, parity, :, : z.half] = hit[:, : z.half]
            masks[1, step, parity, :, 1 : z.half - 1] = hit[:, : z.half - 1 : -1]
    weight = np.zeros((z.rows, LANES))
    weight[: z.half] = 2.0 / z.channels
    weight[0] = weight[z.half - 1] = 1.0 / z.channels
    expand = np.zeros((NBLK, 2 * z.side))
    lane = np.arange(z.side)
    expand[lane // parities, lane] = 1
    expand[(z.side - 1 - lane) // parities, z.side + lane] = 1
    return (
        jnp.asarray(masks.reshape(-1, z.rows16), jnp.bfloat16),
        jnp.asarray(weight, jnp.float32),
        jnp.asarray(expand, jnp.bfloat16),
    )


def fill_frames(z, history, load, pr_ref, y_ref, count, save=None):
    for block in range(DFT_A // 16):
        rows = pl.ds(block * 16, 16)
        taps = [pr_ref[tap, rows, :] for tap in range(z.taps)]
        window = [history(k, block) for k in range(z.hist)]
        for k in range(count):
            window.append(load(k, block))
            acc = window[0] * taps[0]
            for tap in range(1, z.taps):
                acc = acc + window[tap] * taps[tap]
            y_ref[rows, k * LANES : (k + 1) * LANES] = acc.astype(jnp.bfloat16)
            window.pop(0)
        if save is not None:
            for k in range(z.hist):
                save(k, block, window[k])


def transform(z, y_ref, first_ref, twiddle_ref, second_ref, t_refs, count):
    pad = jnp.zeros((z.rows16 - z.rows, LANES), jnp.float32)
    part = count // len(t_refs)
    out = []
    for index, t_ref in enumerate(t_refs):
        for at in range(0, part, 2):
            pair = min(2, part - at)
            lane = (index * part + at) * LANES
            a = jnp.dot(first_ref[...], y_ref[:, lane : lane + pair * LANES], preferred_element_type=jnp.float32)
            for k in range(pair):
                re = a[: z.rows, k * LANES : (k + 1) * LANES]
                im = a[z.rows :, k * LANES : (k + 1) * LANES]
                cos, sin = twiddle_ref[0], twiddle_ref[1]
                t_re = re * cos + im * sin
                t_im = im * cos - re * sin
                rows = slice((at + k) * z.rows16, (at + k + 1) * z.rows16)
                t_ref[rows, :LANES] = jnp.concatenate([t_re, pad]).astype(jnp.bfloat16)
                t_ref[rows, LANES:] = jnp.concatenate([t_im, pad]).astype(jnp.bfloat16)
        c = jnp.dot(t_ref[...], second_ref[...], preferred_element_type=jnp.float32)
        for k in range(part):
            rows = c[k * z.rows16 : k * z.rows16 + z.rows]
            re, im = rows[:, :LANES], rows[:, LANES:]
            out.append(re * re + im * im)
    return out


def channelize(z, raw_ref, proto_ref, first_in, twiddle_in, second_in, masks_in, weight_in, expand_ref, delays_ref, owners_in,
               power_ref, pr_ref, band_ref, msg_ref, first_ref, twiddle_ref, second_ref, masks_ref, weight_ref, hits_ref, owners_ref,
               buf, tap_ref, spread_ref, trial_ref, hist_ref, y0_ref, y1_ref, t0_ref, t1_ref, t2_ref, t3_ref, sems, sides):
    chunks = z.spec // CHUNK
    span = CHUNK * z.channels

    def raw_copy(i):
        part = pl.ds(i * span, span)
        return pltpu.make_async_copy(raw_ref.at[:, part], buf.at[:, part], sems.at[i])

    raw_copy(0).start()
    pairs = [
        (proto_ref, tap_ref), (first_in, first_ref), (twiddle_in, twiddle_ref), (second_in, second_ref),
        (delays_ref, trial_ref), (expand_ref, spread_ref), (masks_in, masks_ref), (weight_in, weight_ref),
    ]
    copies = [pltpu.make_async_copy(source, target, sides.at[i]) for i, (source, target) in enumerate(pairs)]
    copies[0].start()
    for copy in copies[1:]:
        copy.start()
    for i in range(1, chunks):
        raw_copy(i).start()
    hist_ref[...] = jnp.zeros_like(hist_ref)
    band_ref[...] = jnp.zeros_like(band_ref)
    for g in range(z.groups):
        owners_ref[g] = owners_in[g]
    early = lax.axis_index("tm") > 0
    copies[0].wait()
    for tap in range(z.taps):
        pr_ref[tap] = tap_ref[tap : tap + 1, :].reshape(DFT_A, LANES)
    for copy in copies[1:]:
        copy.wait()
    unit = 1.0 / (math.sqrt(z.channels // NBLK) * math.sqrt(NBLK))
    trials = trial_ref.shape[1]
    tall = jnp.concatenate(
        [
            jnp.concatenate([trial_ref[g].astype(jnp.float32), jnp.zeros((8 - trials, NBLK), jnp.float32)])
            for g in range(z.groups)
        ]
    )
    spread = jnp.dot(tall.astype(jnp.bfloat16), spread_ref[...], preferred_element_type=jnp.float32)
    for g in range(z.groups):
        mine = spread[g * 8 : g * 8 + 8]
        hits = jnp.concatenate([jnp.where(mine == value, unit, 0.0) for value in range(MAXT + 1)])
        hits_ref[g] = hits.astype(jnp.bfloat16)

    def frames(i, y_ref):
        base = i * span

        def load(k, block):
            start = pl.multiple_of(base + k * z.channels + block * 16 * LANES, 16 * LANES)
            return buf[:, pl.ds(start, 16 * LANES)].astype(jnp.float32).reshape(16, LANES)

        def history(k, block):
            return hist_ref[k, block * 16 : block * 16 + 16, :]

        def save(k, block, value):
            hist_ref[k, block * 16 : block * 16 + 16, :] = value

        fill_frames(z, history, load, pr_ref, y_ref, CHUNK, save)

    def powers(i, y_ref, t_refs):
        power = transform(z, y_ref, first_ref, twiddle_ref, second_ref, t_refs, CHUNK)
        late = power[z.hist]
        for k in range(z.hist + 1, CHUNK):
            late = late + power[k]
        head = power[0]
        for k in range(1, z.hist):
            head = head + power[k]
        skip = jnp.logical_and(i == 0, early)
        band_ref[...] = band_ref[...] + late + jnp.where(skip, 0.0, head)
        for k in range(CHUNK):
            power_ref[i * CHUNK + k] = power[k]

    def arrived(i):
        raw_copy(i).wait()

    arrived(0)
    frames(0, y0_ref)

    def step(j, carry):
        i = 2 * j
        arrived(i + 1)
        arrived(i + 2)
        frames(i + 1, y1_ref)
        powers(i, y0_ref, [t0_ref, t1_ref])
        frames(i + 2, y0_ref)
        powers(i + 1, y1_ref, [t2_ref, t3_ref])
        return carry

    lax.fori_loop(0, chunks // 2 - 1, step, 0)
    arrived(chunks - 1)
    frames(chunks - 1, y1_ref)
    powers(chunks - 2, y0_ref, [t0_ref, t1_ref])
    powers(chunks - 1, y1_ref, [t2_ref, t3_ref])

    def spectrum(start):
        start = pl.multiple_of(start, z.channels)
        return buf[:, pl.ds(start, z.channels)].astype(jnp.float32).reshape(DFT_A, LANES).astype(jnp.bfloat16)

    row = 0
    tail = (z.spec - z.hist) * z.channels
    starts = [jnp.where(early, 0, tail)] if z.n_tm == 2 else [tail, 0]
    for start in starts:
        for k in range(z.hist):
            msg_ref[row : row + DFT_A] = spectrum(start + k * z.channels)
            row += DFT_A
    high = band_ref[...].astype(jnp.bfloat16)
    msg_ref[row : row + z.rows] = high
    msg_ref[row + z.rows : row + 2 * z.rows] = (band_ref[...] - high.astype(jnp.float32)).astype(jnp.bfloat16)


def search(z, power_ref, pr_ref, band_ref, own_ref, other_ref, first_ref, twiddle_ref, second_ref,
           masks_ref, weight_ref, hits_ref, owners_ref,
           out_ref, y_ref, t_ref, bound_ref, inv_ref, weighted_ref, sums_ref, mean_ref, sub_ref):
    me = lax.axis_index("tm")
    groups, spec = z.groups, z.spec
    chunks = spec // CHUNK
    total = band_ref[...]
    lo = z.bounds * z.raw_rows
    total = total + (
        other_ref[lo : lo + z.rows].astype(jnp.float32) + other_ref[lo + z.rows : lo + 2 * z.rows].astype(jnp.float32)
    )
    swap = jnp.logical_and(me > 0, z.n_tm == 2)
    y_ref[:, z.hist * LANES :] = jnp.zeros((DFT_A, LANES), jnp.bfloat16)
    for b in range(z.bounds):

        def take(k, block, first, b=b):
            start = b * z.raw_rows + k * DFT_A + block * 16
            own = own_ref[start : start + 16].astype(jnp.float32)
            other = other_ref[start : start + 16].astype(jnp.float32)
            return jnp.where(swap, other, own) if first else jnp.where(swap, own, other)

        fill_frames(
            z, lambda k, block: take(k, block, True), lambda k, block: take(k, block, False), pr_ref, y_ref, z.hist
        )
        power = transform(z, y_ref, first_ref, twiddle_ref, second_ref, [t_ref], z.hist)
        for k in range(z.hist):
            total = total + power[k]
            bound_ref[b * z.hist + k] = power[k]
    scale = float(z.taps * z.channels)
    inv_ref[...] = 1.0 / (total * (1.0 / (z.spec * z.n_tm)) + 1e-6 * scale)
    weighted_ref[...] = weight_ref[...] * inv_ref[...]
    mine = jnp.maximum(me - 1, 0) * z.hist

    def power_of(i, k):
        value = power_ref[i * CHUNK + k]
        if k < z.hist:
            value = jnp.where(jnp.logical_and(me > 0, i == 0), bound_ref[mine + k], value)
        return value

    def means(i):
        for k in range(CHUNK):
            value = power_of(i, k) * weighted_ref[...]
            sums_ref[k * 8 : k * 8 + 8] = jnp.sum(value.reshape(z.rows // 8, 8, LANES), 0)
        acc = sums_ref[pl.ds(0, CHUNK, stride=8)]
        for j in range(1, 8):
            acc = acc + sums_ref[pl.ds(j, CHUNK, stride=8)]
        at = pl.multiple_of(i * CHUNK, CHUNK)
        mean_ref[pl.ds(at, CHUNK)] = jnp.broadcast_to(jnp.sum(acc, 1, keepdims=True), (CHUNK, LANES))

    parities = z.channels // NBLK // DFT_A
    lane = lax.broadcasted_iota(jnp.int32, (groups, LANES), 1)
    pad = jnp.zeros((z.rows16 - z.rows, LANES), jnp.float32)

    def picked(m, step, value):
        row = (m * FD + step) * parities * groups
        part = value[row : row + groups]
        for parity in range(1, parities):
            hit = (lane if m == 0 else LANES - 1 - lane) % parities == parity
            part = jnp.where(hit, value[row + parity * groups : row + (parity + 1) * groups], part)
        return part

    def flat_step(i, carry):
        flats = []
        open_sums = [list(carry[m]) for m in range(2)]
        for k in range(CHUNK):
            flat = power_of(i, k) * inv_ref[...] - mean_ref[pl.ds(i * CHUNK + k, 1)]
            flats.append(jnp.concatenate([flat, pad]).astype(jnp.bfloat16))
            if k % 2 == 0:
                continue
            found = jnp.dot(masks_ref[...], jnp.concatenate(flats[-2:], 1), preferred_element_type=jnp.float32)
            for half in range(2):
                value = found[:, half * LANES : (half + 1) * LANES]
                at = pl.multiple_of((i * CHUNK + k - 1 + half) * groups, 8)
                for m in range(2):
                    parts = [picked(m, step, value) for step in range(FD)]
                    sub_ref[m, pl.ds(at, groups)] = open_sums[m][0] + parts[0]
                    later = open_sums[m][1:] + [None]
                    open_sums[m] = [
                        parts[step + 1] if later[step] is None else later[step] + parts[step + 1]
                        for step in range(FD - 1)
                    ]
        means(jnp.minimum(i + 1, chunks - 1))
        return tuple(tuple(value) for value in open_sums)

    means(0)
    empty = jnp.zeros((groups, LANES), jnp.float32)
    carry = lax.fori_loop(0, chunks, flat_step, ((empty,) * (FD - 1),) * 2)
    length = spec + FD - 1
    stop = ceil_to(length, 16)
    for m in range(2):
        for step in range(FD - 1):
            sub_ref[m, (spec + step) * groups : (spec + step + 1) * groups] = carry[m][step]
    sub_ref[:, length * groups :] = jnp.zeros((2, (stop - length) * groups, LANES), jnp.float32)
    trials = out_ref.shape[2]
    out_ref[...] = jnp.zeros_like(out_ref)
    wide = 2 * LANES
    blank = jnp.zeros((wide - stop, wide), jnp.bfloat16)
    for g in range(groups):
        both = [sub_ref[m, pl.ds(g, stop, stride=groups)].astype(jnp.bfloat16) for m in range(2)]
        series = jnp.concatenate([jnp.concatenate(both, 1), blank])
        found = lax.dot_general(hits_ref[g], series, (((1,), (1,)), ((), ())), preferred_element_type=jnp.float32)
        dd = found[:8]
        for value in range(1, MAXT + 1):
            dd = dd + pltpu.roll(found[value * 8 : value * 8 + 8], value * TT, 1)
        owner = owners_ref[g]
        rank = jnp.int32(0)
        for earlier in range(g):
            rank = rank + jnp.where(owners_ref[earlier] == owner, 1, 0)
        late = pltpu.roll(dd, wide - (spec - WMAX + 1), 1)
        out_ref[owner * z.n_tm + jnp.minimum(me + 1, z.n_tm - 1), rank] = late[:trials, :LANES]
        out_ref[owner * z.n_tm + me, rank] = dd[:trials, :LANES]


def boxes(z, recv_ref, widths_ref, out_ref, d_ref):
    me = lax.axis_index("tm")
    trials = recv_ref.shape[2]
    rank = lax.broadcasted_iota(jnp.int32, (8, LANES), 0)
    count = widths_ref.shape[0]
    width = jnp.zeros((8, LANES), jnp.int32)
    for w in range(count):
        width = jnp.where(rank == w, widths_ref[w], width)
    norm = 1.0 / jnp.sqrt(width.astype(jnp.float32))
    weights = [jnp.where(width > lag, norm, 0.0) for lag in range(WMAX)]
    prior = WMAX - 1
    zero = jnp.zeros((8, LANES), jnp.float32)
    before = jnp.maximum(me - 1, 0)
    rows = z.capacity * trials
    for d in range(z.n_dm):
        own = recv_ref[d * z.n_tm + me].reshape(rows, LANES)
        past = recv_ref[d * z.n_tm + before].reshape(rows, LANES)
        past = jnp.where(me > 0, past, 0.0)
        wide = jnp.concatenate([own, jnp.zeros_like(own)], 1)
        wide = pltpu.roll(wide, prior, 1) + jnp.concatenate([past, jnp.zeros_like(past)], 1)
        for lag in range(WMAX):
            shift = prior - lag
            d_ref[lag] = (pltpu.roll(wide, 2 * LANES - shift, 1) if shift else wide)[:, :LANES]
        for s in range(z.capacity):
            for j in range(trials):
                acc = None
                for lag in range(WMAX):
                    part = d_ref[lag, s * trials + j : s * trials + j + 1, :] * weights[lag]
                    acc = part if acc is None else acc + part
                out_ref[s, d, 0, j] = acc[:count].astype(jnp.bfloat16)


def vmem_spec():
    return pl.BlockSpec(memory_space=pltpu.VMEM)


def smem_spec():
    return pl.BlockSpec(memory_space=pltpu.SMEM)


def any_spec():
    return pl.BlockSpec(memory_space=pl.ANY)


def kept(*values):
    return [pltpu.with_memory_space_constraint(value, pltpu.VMEM) for value in values]


def shards(n_dm, n_tm, raw, proto, delays, widths, owners):
    taps, channels = proto.shape
    groups, trials, _ = delays.shape
    z = Sizes(taps, channels, raw.shape[1] // channels, groups, n_dm, n_tm)
    first, twiddle, second = dft_constants(z)
    masks, weight, expand = mask_constants(z)
    params = pltpu.CompilerParams(vmem_limit_bytes=LIMIT)
    own_rows = z.raw_rows * (1 if n_tm == 2 else 2) + 2 * z.rows
    f32, bf16 = jnp.float32, jnp.bfloat16
    chunks = z.spec // CHUNK
    half = CHUNK // 2 * z.rows16
    power, pr, band, msg, first, twiddle, second, masks, weight, hits, owner = pl.pallas_call(
        functools.partial(channelize, z),
        out_shape=(
            pltpu.VMEM((z.spec, z.rows, LANES), f32),
            pltpu.VMEM((taps, DFT_A, LANES), f32),
            pltpu.VMEM((z.rows, LANES), f32),
            pltpu.VMEM((own_rows, LANES), bf16),
            pltpu.VMEM(first.shape, bf16),
            pltpu.VMEM(twiddle.shape, f32),
            pltpu.VMEM(second.shape, bf16),
            pltpu.VMEM(masks.shape, bf16),
            pltpu.VMEM(weight.shape, f32),
            pltpu.VMEM((groups, (MAXT + 1) * 8, 2 * LANES), bf16),
            pltpu.SMEM((groups,), jnp.int32),
        ),
        in_specs=[any_spec()] * 9 + [smem_spec()],
        out_specs=[vmem_spec()] * 10 + [smem_spec()],
        scratch_shapes=[
            pltpu.VMEM((1, z.spec * channels), bf16),
            pltpu.VMEM(proto.shape, f32),
            pltpu.VMEM(expand.shape, bf16),
            pltpu.VMEM(delays.shape, jnp.int32),
            pltpu.VMEM((z.hist, DFT_A, LANES), f32),
            pltpu.VMEM((DFT_A, CHUNK * LANES), bf16),
            pltpu.VMEM((DFT_A, CHUNK * LANES), bf16),
            pltpu.VMEM((half, 2 * LANES), bf16),
            pltpu.VMEM((half, 2 * LANES), bf16),
            pltpu.VMEM((half, 2 * LANES), bf16),
            pltpu.VMEM((half, 2 * LANES), bf16),
            pltpu.SemaphoreType.DMA((chunks,)),
            pltpu.SemaphoreType.DMA((8,)),
        ],
        compiler_params=params,
        name="channelize",
    )(raw, proto, first, twiddle, second, masks, weight, expand, delays, owners.reshape(groups))
    if n_tm == 2:
        own, other = msg, lax.ppermute(msg, "tm", [(0, 1), (1, 0)])
    else:
        every = lax.all_gather(msg, "tm")
        lasts = every[:-1, : z.raw_rows].reshape(-1, LANES)
        firsts = every[1:, z.raw_rows : 2 * z.raw_rows].reshape(-1, LANES)
        parts = every[:, 2 * z.raw_rows :].astype(f32).reshape(n_tm, 2, z.rows, LANES)
        rest = jnp.sum(parts, (0, 1)) - band
        high = rest.astype(bf16)
        pair = jnp.concatenate([high, (rest - high.astype(f32)).astype(bf16)])
        own, other = jnp.concatenate([lasts, pair]), jnp.concatenate([firsts, pair])
    length = ceil_to(z.spec + FD - 1, 16)
    out = pl.pallas_call(
        functools.partial(search, z),
        out_shape=pltpu.VMEM((n_dm * n_tm, z.capacity, trials, LANES), f32),
        in_specs=[vmem_spec()] * 11 + [smem_spec()],
        out_specs=vmem_spec(),
        scratch_shapes=[
            pltpu.VMEM((DFT_A, (z.hist + 1) * LANES), bf16),
            pltpu.VMEM((z.hist * z.rows16, 2 * LANES), bf16),
            pltpu.VMEM((z.bounds * z.hist, z.rows, LANES), f32),
            pltpu.VMEM((z.rows, LANES), f32),
            pltpu.VMEM((z.rows, LANES), f32),
            pltpu.VMEM((CHUNK * 8, LANES), f32),
            pltpu.VMEM((z.spec, LANES), f32),
            pltpu.VMEM((2, length * groups, LANES), f32),
        ],
        compiler_params=params,
        name="search",
    )(
        *kept(power, pr, band, own, other, first, twiddle, second, masks, weight, hits),
        pltpu.with_memory_space_constraint(owner, pltpu.SMEM),
    )
    recv = lax.all_to_all(out, ("dm", "tm"), split_axis=0, concat_axis=0, tiled=True)
    return pl.pallas_call(
        functools.partial(boxes, z),
        out_shape=jax.ShapeDtypeStruct((z.capacity, n_dm, 1, trials, widths.shape[0], z.spec), bf16),
        in_specs=[vmem_spec(), smem_spec()],
        out_specs=vmem_spec(),
        scratch_shapes=[pltpu.VMEM((WMAX, z.capacity * trials, LANES), f32)],
        compiler_params=params,
        name="boxes",
    )(*kept(recv), widths)


def solution(mesh):
    sizes = dict(mesh.shape)
    return jax.shard_map(
        functools.partial(shards, sizes["dm"], sizes["tm"]),
        mesh=mesh,
        in_specs=(P(("group", "dm", "beam"), "tm"), P(), P(), P(), P()),
        out_specs=P("dm", "group", "beam", None, None, "tm"),
        check_vma=False,
    )
```

```python
import functools
import math

import jax
import jax.numpy as jnp
import numpy as np
from jax import lax
from jax.experimental import pallas as pl
from jax.experimental.pallas import tpu as pltpu
from jax.sharding import PartitionSpec as P

DFT_A = 128
NBLK = 64
FD = 4
TT = 8
MAXT = 3
WMAX = 8
LANES = 128
CHUNK = 16
LIMIT = 32 * 1024 * 1024


def ceil_to(value, unit):
    return -(-value // unit) * unit


def angle_tables(rows, cols, total):
    product = np.arange(rows)[:, None] * np.arange(cols)[None, :] % total
    angle = product.astype(np.float64) * (2.0 * math.pi / total)
    return np.cos(angle), np.sin(angle)


class Sizes:
    def __init__(self, taps, channels, spec, groups, n_dm, n_tm):
        self.taps, self.channels, self.spec, self.groups = taps, channels, spec, groups
        self.n_dm, self.n_tm = n_dm, n_tm
        self.side = channels // DFT_A
        self.half = DFT_A // 2 + 1
        self.rows = ceil_to(self.half, 8)
        self.rows16 = ceil_to(self.half, 16)
        self.hist = taps - 1
        self.raw_rows = self.hist * DFT_A
        self.bounds = n_tm - 1
        self.msg_rows = self.bounds * self.raw_rows + 2 * self.rows
        self.capacity = 2 * (groups // n_dm)


def dft_constants(z):
    cos_a, sin_a = angle_tables(DFT_A, DFT_A, DFT_A)
    first = np.zeros((2 * z.rows, DFT_A))
    first[: z.half] = cos_a[: z.half]
    first[z.rows : z.rows + z.half] = -sin_a[: z.half]
    tw_cos, tw_sin = np.zeros((2, z.rows, z.side))
    tw_cos[: z.half], tw_sin[: z.half] = angle_tables(z.half, z.side, z.channels)
    cos_b, sin_b = angle_tables(z.side, z.side, z.side)
    second = np.block([[cos_b, -sin_b], [sin_b, cos_b]])
    return (
        jnp.asarray(first, jnp.bfloat16),
        jnp.asarray(np.stack([tw_cos, tw_sin]), jnp.float32),
        jnp.asarray(second, jnp.bfloat16),
    )


def mask_constants(z):
    width = z.channels // NBLK
    fine = np.arange(z.groups)[:, None] * FD * (width - 1 - np.arange(width))[None, :] // (z.groups * (width - 1))
    parities = width // DFT_A
    masks = np.zeros((2, FD, parities, z.groups, z.rows16))
    for step in range(FD):
        for parity in range(parities):
            hit = fine[:, parity * DFT_A : (parity + 1) * DFT_A] == step
            masks[0, step, parity, :, : z.half] = hit[:, : z.half]
            masks[1, step, parity, :, 1 : z.half - 1] = hit[:, : z.half - 1 : -1]
    weight = np.zeros((z.rows, LANES))
    weight[: z.half] = 2.0 / z.channels
    weight[0] = weight[z.half - 1] = 1.0 / z.channels
    expand = np.zeros((NBLK, 2 * z.side))
    lane = np.arange(z.side)
    expand[lane // parities, lane] = 1
    expand[(z.side - 1 - lane) // parities, z.side + lane] = 1
    return (
        jnp.asarray(masks.reshape(-1, z.rows16), jnp.bfloat16),
        jnp.asarray(weight, jnp.float32),
        jnp.asarray(expand, jnp.bfloat16),
    )


def fill_frames(z, history, load, pr_ref, y_ref, count, save=None):
    for block in range(DFT_A // 16):
        rows = pl.ds(block * 16, 16)
        taps = [pr_ref[tap, rows, :] for tap in range(z.taps)]
        window = [history(k, block) for k in range(z.hist)]
        for k in range(count):
            window.append(load(k, block))
            acc = window[0] * taps[0]
            for tap in range(1, z.taps):
                acc = acc + window[tap] * taps[tap]
            y_ref[rows, k * LANES : (k + 1) * LANES] = acc.astype(jnp.bfloat16)
            window.pop(0)
        if save is not None:
            for k in range(z.hist):
                save(k, block, window[k])


def transform(z, y_ref, first_ref, twiddle_ref, second_ref, t_refs, count):
    pad = jnp.zeros((z.rows16 - z.rows, LANES), jnp.float32)
    part = count // len(t_refs)
    out = []
    for index, t_ref in enumerate(t_refs):
        for at in range(0, part, 2):
            pair = min(2, part - at)
            lane = (index * part + at) * LANES
            a = jnp.dot(first_ref[...], y_ref[:, lane : lane + pair * LANES], preferred_element_type=jnp.float32)
            for k in range(pair):
                re = a[: z.rows, k * LANES : (k + 1) * LANES]
                im = a[z.rows :, k * LANES : (k + 1) * LANES]
                cos, sin = twiddle_ref[0], twiddle_ref[1]
                t_re = re * cos + im * sin
                t_im = im * cos - re * sin
                rows = slice((at + k) * z.rows16, (at + k + 1) * z.rows16)
                t_ref[rows, :LANES] = jnp.concatenate([t_re, pad]).astype(jnp.bfloat16)
                t_ref[rows, LANES:] = jnp.concatenate([t_im, pad]).astype(jnp.bfloat16)
        c = jnp.dot(t_ref[...], second_ref[...], preferred_element_type=jnp.float32)
        for k in range(part):
            rows = c[k * z.rows16 : k * z.rows16 + z.rows]
            re, im = rows[:, :LANES], rows[:, LANES:]
            out.append(re * re + im * im)
    return out


def channelize(z, raw_ref, proto_ref, first_in, twiddle_in, second_in, masks_in, weight_in, expand_ref, delays_ref, owners_in, widths_in,
               power_ref, pr_ref, band_ref, msg_ref, first_ref, twiddle_ref, second_ref, masks_ref, weight_ref, hits_ref, owners_ref, widths_ref,
               buf, tap_ref, spread_ref, trial_ref, hist_ref, y0_ref, y1_ref, t0_ref, t1_ref, t2_ref, t3_ref, sems, sides):
    chunks = z.spec // CHUNK
    span = CHUNK * z.channels

    def raw_copy(i):
        part = pl.ds(i * span, span)
        return pltpu.make_async_copy(raw_ref.at[:, part], buf.at[:, part], sems.at[i])

    raw_copy(0).start()
    pairs = [
        (proto_ref, tap_ref), (first_in, first_ref), (twiddle_in, twiddle_ref), (second_in, second_ref),
        (delays_ref, trial_ref), (expand_ref, spread_ref), (masks_in, masks_ref), (weight_in, weight_ref),
        (owners_in, owners_ref), (widths_in, widths_ref),
    ]
    copies = [pltpu.make_async_copy(source, target, sides.at[i]) for i, (source, target) in enumerate(pairs)]
    for copy in copies:
        copy.start()
    for i in range(1, chunks):
        raw_copy(i).start()
    hist_ref[...] = jnp.zeros_like(hist_ref)
    band_ref[...] = jnp.zeros_like(band_ref)
    early = lax.axis_index("tm") > 0
    copies[0].wait()
    for tap in range(z.taps):
        pr_ref[tap] = tap_ref[tap : tap + 1, :].reshape(DFT_A, LANES)
    for copy in copies[1:]:
        copy.wait()
    unit = 1.0 / (math.sqrt(z.channels // NBLK) * math.sqrt(NBLK))
    trials = trial_ref.shape[1]
    tall = jnp.concatenate(
        [
            jnp.concatenate([trial_ref[g].astype(jnp.float32), jnp.zeros((8 - trials, NBLK), jnp.float32)])
            for g in range(z.groups)
        ]
    )
    spread = jnp.dot(tall.astype(jnp.bfloat16), spread_ref[...], preferred_element_type=jnp.float32)
    for g in range(z.groups):
        mine = spread[g * 8 : g * 8 + 8]
        hits = jnp.concatenate([jnp.where(mine == value, unit, 0.0) for value in range(MAXT + 1)])
        hits_ref[g] = hits.astype(jnp.bfloat16)

    def frames(i, y_ref):
        base = i * span

        def load(k, block):
            start = pl.multiple_of(base + k * z.channels + block * 16 * LANES, 16 * LANES)
            return buf[:, pl.ds(start, 16 * LANES)].astype(jnp.float32).reshape(16, LANES)

        def history(k, block):
            return hist_ref[k, block * 16 : block * 16 + 16, :]

        def save(k, block, value):
            hist_ref[k, block * 16 : block * 16 + 16, :] = value

        fill_frames(z, history, load, pr_ref, y_ref, CHUNK, save)

    def powers(i, y_ref, t_refs):
        power = transform(z, y_ref, first_ref, twiddle_ref, second_ref, t_refs, CHUNK)
        late = power[z.hist]
        for k in range(z.hist + 1, CHUNK):
            late = late + power[k]
        head = power[0]
        for k in range(1, z.hist):
            head = head + power[k]
        skip = jnp.logical_and(i == 0, early)
        band_ref[...] = band_ref[...] + late + jnp.where(skip, 0.0, head)
        for k in range(CHUNK):
            power_ref[i * CHUNK + k] = power[k]

    def arrived(i):
        raw_copy(i).wait()

    arrived(0)
    frames(0, y0_ref)

    def step(j, carry):
        i = 2 * j
        arrived(i + 1)
        arrived(i + 2)
        frames(i + 1, y1_ref)
        powers(i, y0_ref, [t0_ref, t1_ref])
        frames(i + 2, y0_ref)
        powers(i + 1, y1_ref, [t2_ref, t3_ref])
        return carry

    lax.fori_loop(0, chunks // 2 - 1, step, 0)
    arrived(chunks - 1)
    frames(chunks - 1, y1_ref)
    powers(chunks - 2, y0_ref, [t0_ref, t1_ref])
    powers(chunks - 1, y1_ref, [t2_ref, t3_ref])

    def spectrum(start):
        start = pl.multiple_of(start, z.channels)
        return buf[:, pl.ds(start, z.channels)].astype(jnp.float32).reshape(DFT_A, LANES).astype(jnp.bfloat16)

    row = 0
    tail = (z.spec - z.hist) * z.channels
    starts = [jnp.where(early, 0, tail)] if z.n_tm == 2 else [tail, 0]
    for start in starts:
        for k in range(z.hist):
            msg_ref[row : row + DFT_A] = spectrum(start + k * z.channels)
            row += DFT_A
    high = band_ref[...].astype(jnp.bfloat16)
    msg_ref[row : row + z.rows] = high
    msg_ref[row + z.rows : row + 2 * z.rows] = (band_ref[...] - high.astype(jnp.float32)).astype(jnp.bfloat16)


def search(z, power_ref, pr_ref, band_ref, own_ref, other_ref, first_ref, twiddle_ref, second_ref,
           masks_ref, weight_ref, hits_ref, owners_ref,
           out_ref, y_ref, t_ref, bound_ref, inv_ref, weighted_ref, sums_ref, mean_ref, sub_ref):
    me = lax.axis_index("tm")
    groups, spec = z.groups, z.spec
    chunks = spec // CHUNK
    total = band_ref[...]
    lo = z.bounds * z.raw_rows
    total = total + (
        other_ref[lo : lo + z.rows].astype(jnp.float32) + other_ref[lo + z.rows : lo + 2 * z.rows].astype(jnp.float32)
    )
    swap = jnp.logical_and(me > 0, z.n_tm == 2)
    y_ref[:, z.hist * LANES :] = jnp.zeros((DFT_A, LANES), jnp.bfloat16)
    for b in range(z.bounds):

        def take(k, block, first, b=b):
            start = b * z.raw_rows + k * DFT_A + block * 16
            own = own_ref[start : start + 16].astype(jnp.float32)
            other = other_ref[start : start + 16].astype(jnp.float32)
            return jnp.where(swap, other, own) if first else jnp.where(swap, own, other)

        fill_frames(
            z, lambda k, block: take(k, block, True), lambda k, block: take(k, block, False), pr_ref, y_ref, z.hist
        )
        power = transform(z, y_ref, first_ref, twiddle_ref, second_ref, [t_ref], z.hist)
        for k in range(z.hist):
            total = total + power[k]
            bound_ref[b * z.hist + k] = power[k]
    scale = float(z.taps * z.channels)
    inv_ref[...] = 1.0 / (total * (1.0 / (z.spec * z.n_tm)) + 1e-6 * scale)
    weighted_ref[...] = weight_ref[...] * inv_ref[...]
    mine = jnp.maximum(me - 1, 0) * z.hist

    def power_of(i, k):
        value = power_ref[i * CHUNK + k]
        if k < z.hist:
            value = jnp.where(jnp.logical_and(me > 0, i == 0), bound_ref[mine + k], value)
        return value

    def means(i):
        for k in range(CHUNK):
            value = power_of(i, k) * weighted_ref[...]
            sums_ref[k * 8 : k * 8 + 8] = jnp.sum(value.reshape(z.rows // 8, 8, LANES), 0)
        acc = sums_ref[pl.ds(0, CHUNK, stride=8)]
        for j in range(1, 8):
            acc = acc + sums_ref[pl.ds(j, CHUNK, stride=8)]
        at = pl.multiple_of(i * CHUNK, CHUNK)
        mean_ref[pl.ds(at, CHUNK)] = jnp.broadcast_to(jnp.sum(acc, 1, keepdims=True), (CHUNK, LANES))

    parities = z.channels // NBLK // DFT_A
    lane = lax.broadcasted_iota(jnp.int32, (groups, LANES), 1)
    pad = jnp.zeros((z.rows16 - z.rows, LANES), jnp.float32)

    def picked(m, step, value):
        row = (m * FD + step) * parities * groups
        part = value[row : row + groups]
        for parity in range(1, parities):
            hit = (lane if m == 0 else LANES - 1 - lane) % parities == parity
            part = jnp.where(hit, value[row + parity * groups : row + (parity + 1) * groups], part)
        return part

    def flat_step(i, carry):
        flats = []
        open_sums = [list(carry[m]) for m in range(2)]
        for k in range(CHUNK):
            flat = power_of(i, k) * inv_ref[...] - mean_ref[pl.ds(i * CHUNK + k, 1)]
            flats.append(jnp.concatenate([flat, pad]).astype(jnp.bfloat16))
            if k % 2 == 0:
                continue
            found = jnp.dot(masks_ref[...], jnp.concatenate(flats[-2:], 1), preferred_element_type=jnp.float32)
            for half in range(2):
                value = found[:, half * LANES : (half + 1) * LANES]
                at = pl.multiple_of((i * CHUNK + k - 1 + half) * groups, 8)
                for m in range(2):
                    parts = [picked(m, step, value) for step in range(FD)]
                    sub_ref[m, pl.ds(at, groups)] = open_sums[m][0] + parts[0]
                    later = open_sums[m][1:] + [None]
                    open_sums[m] = [
                        parts[step + 1] if later[step] is None else later[step] + parts[step + 1]
                        for step in range(FD - 1)
                    ]
        means(jnp.minimum(i + 1, chunks - 1))
        return tuple(tuple(value) for value in open_sums)

    means(0)
    empty = jnp.zeros((groups, LANES), jnp.float32)
    carry = lax.fori_loop(0, chunks, flat_step, ((empty,) * (FD - 1),) * 2)
    length = spec + FD - 1
    stop = ceil_to(length, 16)
    for m in range(2):
        for step in range(FD - 1):
            sub_ref[m, (spec + step) * groups : (spec + step + 1) * groups] = carry[m][step]
    sub_ref[:, length * groups :] = jnp.zeros((2, (stop - length) * groups, LANES), jnp.float32)
    trials = out_ref.shape[2]
    out_ref[...] = jnp.zeros_like(out_ref)
    wide = 2 * LANES
    blank = jnp.zeros((wide - stop, wide), jnp.bfloat16)
    for g in range(groups):
        both = [sub_ref[m, pl.ds(g, stop, stride=groups)].astype(jnp.bfloat16) for m in range(2)]
        series = jnp.concatenate([jnp.concatenate(both, 1), blank])
        found = lax.dot_general(hits_ref[g], series, (((1,), (1,)), ((), ())), preferred_element_type=jnp.float32)
        dd = found[:8]
        for value in range(1, MAXT + 1):
            dd = dd + pltpu.roll(found[value * 8 : value * 8 + 8], value * TT, 1)
        owner = owners_ref[g]
        rank = jnp.int32(0)
        for earlier in range(g):
            rank = rank + jnp.where(owners_ref[earlier] == owner, 1, 0)
        late = pltpu.roll(dd, wide - (spec - WMAX + 1), 1)
        out_ref[owner * z.n_tm + jnp.minimum(me + 1, z.n_tm - 1), rank] = late[:trials, :LANES]
        out_ref[owner * z.n_tm + me, rank] = dd[:trials, :LANES]


def boxes(z, recv_ref, widths_ref, out_ref, d_ref):
    me = lax.axis_index("tm")
    trials = recv_ref.shape[2]
    rank = lax.broadcasted_iota(jnp.int32, (8, LANES), 0)
    count = widths_ref.shape[0]
    width = jnp.zeros((8, LANES), jnp.int32)
    for w in range(count):
        width = jnp.where(rank == w, widths_ref[w], width)
    norm = 1.0 / jnp.sqrt(width.astype(jnp.float32))
    weights = [jnp.where(width > lag, norm, 0.0) for lag in range(WMAX)]
    prior = WMAX - 1
    zero = jnp.zeros((8, LANES), jnp.float32)
    before = jnp.maximum(me - 1, 0)
    rows = z.capacity * trials
    for d in range(z.n_dm):
        own = recv_ref[d * z.n_tm + me].reshape(rows, LANES)
        past = recv_ref[d * z.n_tm + before].reshape(rows, LANES)
        past = jnp.where(me > 0, past, 0.0)
        wide = jnp.concatenate([own, jnp.zeros_like(own)], 1)
        wide = pltpu.roll(wide, prior, 1) + jnp.concatenate([past, jnp.zeros_like(past)], 1)
        for lag in range(WMAX):
            shift = prior - lag
            d_ref[lag] = (pltpu.roll(wide, 2 * LANES - shift, 1) if shift else wide)[:, :LANES]
        for s in range(z.capacity):
            for j in range(trials):
                acc = None
                for lag in range(WMAX):
                    part = d_ref[lag, s * trials + j : s * trials + j + 1, :] * weights[lag]
                    acc = part if acc is None else acc + part
                out_ref[s, d, 0, j] = acc[:count].astype(jnp.bfloat16)


def vmem_spec():
    return pl.BlockSpec(memory_space=pltpu.VMEM)


def smem_spec():
    return pl.BlockSpec(memory_space=pltpu.SMEM)


def hbm_spec():
    return pl.BlockSpec(memory_space=pltpu.HBM)


def kept(*values, space=pltpu.VMEM):
    return [pltpu.with_memory_space_constraint(value, space) for value in values]


def shards(n_dm, n_tm, raw, proto, delays, widths, owners):
    taps, channels = proto.shape
    groups, trials, _ = delays.shape
    z = Sizes(taps, channels, raw.shape[1] // channels, groups, n_dm, n_tm)
    first, twiddle, second = dft_constants(z)
    masks, weight, expand = mask_constants(z)
    params = pltpu.CompilerParams(vmem_limit_bytes=LIMIT)
    own_rows = z.raw_rows * (1 if n_tm == 2 else 2) + 2 * z.rows
    f32, bf16 = jnp.float32, jnp.bfloat16
    chunks = z.spec // CHUNK
    half = CHUNK // 2 * z.rows16
    power, pr, band, msg, first, twiddle, second, masks, weight, hits, owner, width = pl.pallas_call(
        functools.partial(channelize, z),
        out_shape=(
            pltpu.VMEM((z.spec, z.rows, LANES), f32),
            pltpu.VMEM((taps, DFT_A, LANES), f32),
            pltpu.VMEM((z.rows, LANES), f32),
            pltpu.VMEM((own_rows, LANES), bf16),
            pltpu.VMEM(first.shape, bf16),
            pltpu.VMEM(twiddle.shape, f32),
            pltpu.VMEM(second.shape, bf16),
            pltpu.VMEM(masks.shape, bf16),
            pltpu.VMEM(weight.shape, f32),
            pltpu.VMEM((groups, (MAXT + 1) * 8, 2 * LANES), bf16),
            pltpu.SMEM((groups,), jnp.int32),
            pltpu.SMEM(widths.shape, jnp.int32),
        ),
        in_specs=[hbm_spec()] * 11,
        out_specs=[vmem_spec()] * 10 + [smem_spec()] * 2,
        scratch_shapes=[
            pltpu.VMEM((1, z.spec * channels), bf16),
            pltpu.VMEM(proto.shape, f32),
            pltpu.VMEM(expand.shape, bf16),
            pltpu.VMEM(delays.shape, jnp.int32),
            pltpu.VMEM((z.hist, DFT_A, LANES), f32),
            pltpu.VMEM((DFT_A, CHUNK * LANES), bf16),
            pltpu.VMEM((DFT_A, CHUNK * LANES), bf16),
            pltpu.VMEM((half, 2 * LANES), bf16),
            pltpu.VMEM((half, 2 * LANES), bf16),
            pltpu.VMEM((half, 2 * LANES), bf16),
            pltpu.VMEM((half, 2 * LANES), bf16),
            pltpu.SemaphoreType.DMA((chunks,)),
            pltpu.SemaphoreType.DMA((10,)),
        ],
        compiler_params=params,
        name="channelize",
    )(
        *kept(
            raw, proto, first, twiddle, second, masks, weight, expand, delays, owners.reshape(groups), widths,
            space=pltpu.HBM,
        )
    )
    if n_tm == 2:
        own, other = msg, lax.ppermute(msg, "tm", [(0, 1), (1, 0)])
    else:
        every = lax.all_gather(msg, "tm")
        lasts = every[:-1, : z.raw_rows].reshape(-1, LANES)
        firsts = every[1:, z.raw_rows : 2 * z.raw_rows].reshape(-1, LANES)
        parts = every[:, 2 * z.raw_rows :].astype(f32).reshape(n_tm, 2, z.rows, LANES)
        rest = jnp.sum(parts, (0, 1)) - band
        high = rest.astype(bf16)
        pair = jnp.concatenate([high, (rest - high.astype(f32)).astype(bf16)])
        own, other = jnp.concatenate([lasts, pair]), jnp.concatenate([firsts, pair])
    length = ceil_to(z.spec + FD - 1, 16)
    out = pl.pallas_call(
        functools.partial(search, z),
        out_shape=pltpu.VMEM((n_dm * n_tm, z.capacity, trials, LANES), f32),
        in_specs=[vmem_spec()] * 11 + [smem_spec()],
        out_specs=vmem_spec(),
        scratch_shapes=[
            pltpu.VMEM((DFT_A, (z.hist + 1) * LANES), bf16),
            pltpu.VMEM((z.hist * z.rows16, 2 * LANES), bf16),
            pltpu.VMEM((z.bounds * z.hist, z.rows, LANES), f32),
            pltpu.VMEM((z.rows, LANES), f32),
            pltpu.VMEM((z.rows, LANES), f32),
            pltpu.VMEM((CHUNK * 8, LANES), f32),
            pltpu.VMEM((z.spec, LANES), f32),
            pltpu.VMEM((2, length * groups, LANES), f32),
        ],
        compiler_params=params,
        name="search",
    )(
        *kept(power, pr, band, own, other, first, twiddle, second, masks, weight, hits),
        *kept(owner, space=pltpu.SMEM),
    )
    recv = lax.all_to_all(out, ("dm", "tm"), split_axis=0, concat_axis=0, tiled=True)
    return pl.pallas_call(
        functools.partial(boxes, z),
        out_shape=jax.ShapeDtypeStruct((z.capacity, n_dm, 1, trials, widths.shape[0], z.spec), bf16),
        in_specs=[vmem_spec(), smem_spec()],
        out_specs=vmem_spec(),
        scratch_shapes=[pltpu.VMEM((WMAX, z.capacity * trials, LANES), f32)],
        compiler_params=params,
        name="boxes",
    )(*kept(recv), *kept(width, space=pltpu.SMEM))


def solution(mesh):
    sizes = dict(mesh.shape)
    return jax.shard_map(
        functools.partial(shards, sizes["dm"], sizes["tm"]),
        mesh=mesh,
        in_specs=(P(("group", "dm", "beam"), "tm"), P(), P(), P(), P()),
        out_specs=P("dm", "group", "beam", None, None, "tm"),
        check_vma=False,
    )
```

```python
import functools
import math

import jax
import jax.numpy as jnp
import numpy as np
from jax import lax
from jax.experimental import pallas as pl
from jax.experimental.pallas import tpu as pltpu
from jax.sharding import PartitionSpec as P

DFT_A = 128
NBLK = 64
FD = 4
TT = 8
MAXT = 3
WMAX = 8
LANES = 128
CHUNK = 16
LIMIT = 32 * 1024 * 1024


def ceil_to(value, unit):
    return -(-value // unit) * unit


def angle_tables(rows, cols, total):
    product = np.arange(rows)[:, None] * np.arange(cols)[None, :] % total
    angle = product.astype(np.float64) * (2.0 * math.pi / total)
    return np.cos(angle), np.sin(angle)


class Sizes:
    def __init__(self, taps, channels, spec, groups, n_dm, n_tm):
        self.taps, self.channels, self.spec, self.groups = taps, channels, spec, groups
        self.n_dm, self.n_tm = n_dm, n_tm
        self.side = channels // DFT_A
        self.half = DFT_A // 2 + 1
        self.rows = ceil_to(self.half, 8)
        self.rows16 = ceil_to(self.half, 16)
        self.hist = taps - 1
        self.raw_rows = self.hist * DFT_A
        self.bounds = n_tm - 1
        self.msg_rows = self.bounds * self.raw_rows + 2 * self.rows
        self.capacity = 2 * (groups // n_dm)


def constants(z):
    cos_a, sin_a = angle_tables(DFT_A, DFT_A, DFT_A)
    first = np.zeros((2 * z.rows, DFT_A))
    first[: z.half] = cos_a[: z.half]
    first[z.rows : z.rows + z.half] = -sin_a[: z.half]
    tw_cos, tw_sin = np.zeros((2, z.rows16, z.side))
    tw_cos[: z.half], tw_sin[: z.half] = angle_tables(z.half, z.side, z.channels)
    cos_b, sin_b = angle_tables(z.side, z.side, z.side)
    width = z.channels // NBLK
    fine = np.arange(z.groups)[:, None] * FD * (width - 1 - np.arange(width))[None, :] // (z.groups * (width - 1))
    parities = width // DFT_A
    masks = np.zeros((2, FD, parities, z.groups, LANES))
    for step in range(FD):
        for parity in range(parities):
            hit = fine[:, parity * DFT_A : (parity + 1) * DFT_A] == step
            masks[0, step, parity, :, : z.half] = hit[:, : z.half]
            masks[1, step, parity, :, 1 : z.half - 1] = hit[:, : z.half - 1 : -1]
    weight = np.zeros((z.rows16, LANES))
    weight[: z.half] = 2.0 / z.channels
    weight[0] = weight[z.half - 1] = 1.0 / z.channels
    expand = np.zeros((NBLK, 2 * z.side))
    lane = np.arange(z.side)
    expand[lane // parities, lane] = 1
    expand[(z.side - 1 - lane) // parities, z.side + lane] = 1
    tables = {
        "first": first,
        "cos": tw_cos,
        "sin": tw_sin,
        "second": np.concatenate([cos_b, sin_b]),
        "second_im": np.concatenate([-sin_b, cos_b]),
        "masks": masks.reshape(-1, LANES),
        "weight": weight,
        "expand": expand[:, : z.side],
        "expand_im": expand[:, z.side :],
    }
    places, row = {}, 0
    for name, table in tables.items():
        places[name] = (row, row + table.shape[0])
        row += table.shape[0]
    return jnp.asarray(np.concatenate(list(tables.values())), jnp.bfloat16), places


def table(z, ref, name):
    first, last = z.places[name]
    return ref[first:last]


def wide_table(z, ref, name):
    return jnp.concatenate([table(z, ref, name), table(z, ref, name + "_im")], 1)


def fill_frames(z, history, load, pr_ref, y_ref, count, save=None):
    for block in range(DFT_A // 16):
        rows = pl.ds(block * 16, 16)
        taps = [
            jnp.concatenate(
                [
                    pr_ref[tap, :, (2 * block + part) * 8 * LANES : (2 * block + part + 1) * 8 * LANES].reshape(8, LANES)
                    for part in range(2)
                ]
            )
            for tap in range(z.taps)
        ]
        window = [history(k, block) for k in range(z.hist)]
        for k in range(count):
            window.append(load(k, block))
            acc = window[0] * taps[0]
            for tap in range(1, z.taps):
                acc = acc + window[tap] * taps[tap]
            y_ref[rows, k * LANES : (k + 1) * LANES] = acc.astype(jnp.bfloat16)
            window.pop(0)
        if save is not None:
            for k in range(z.hist):
                save(k, block, window[k])


def transform(z, y_ref, tab_ref, t_refs, count):
    pad = jnp.zeros((z.rows16 - z.rows, LANES), jnp.float32)
    cos, sin = table(z, tab_ref, "cos"), table(z, tab_ref, "sin")
    part = count // len(t_refs)
    out = []
    for index, t_ref in enumerate(t_refs):
        for at in range(0, part, 2):
            pair = min(2, part - at)
            lane = (index * part + at) * LANES
            a = jnp.dot(table(z, tab_ref, "first"), y_ref[:, lane : lane + pair * LANES], preferred_element_type=jnp.float32)
            for k in range(pair):
                lanes = slice(k * LANES, (k + 1) * LANES)
                re = jnp.concatenate([a[: z.rows, lanes], pad]).astype(jnp.bfloat16)
                im = jnp.concatenate([a[z.rows :, lanes], pad]).astype(jnp.bfloat16)
                rows = slice((at + k) * z.rows16, (at + k + 1) * z.rows16)
                t_ref[rows, :LANES] = re * cos + im * sin
                t_ref[rows, LANES:] = im * cos - re * sin
        c = jnp.dot(t_ref[...], wide_table(z, tab_ref, "second"), preferred_element_type=jnp.float32)
        for k in range(part):
            rows = c[k * z.rows16 : k * z.rows16 + z.rows]
            re, im = rows[:, :LANES], rows[:, LANES:]
            out.append(re * re + im * im)
    return out


def channelize(z, raw_ref, proto_ref, tab_in, delays_ref, owners_in, widths_in,
               power_ref, pr_ref, band_ref, msg_ref, tab_ref, hits_ref, owners_ref, widths_ref,
               buf, trial_ref, hist_ref, y0_ref, y1_ref, t0_ref, t1_ref, t2_ref, t3_ref, sems):
    chunks = z.spec // CHUNK
    span = CHUNK * z.channels

    def raw_copy(i, side):
        part = pl.ds(pl.multiple_of(i * span, span), span)
        return pltpu.make_async_copy(raw_ref.at[:, part], buf.at[:, part], sems.at[side])

    tab_copy = pltpu.make_async_copy(tab_in, tab_ref, sems.at[2])
    delays_copy = pltpu.make_async_copy(delays_ref, trial_ref, sems.at[2])
    owners_copy = pltpu.make_async_copy(owners_in, owners_ref, sems.at[3])
    widths_copy = pltpu.make_async_copy(widths_in, widths_ref, sems.at[3])
    raw_copy(0, 0).start()
    for tap in range(z.taps):
        pltpu.make_async_copy(proto_ref.at[tap : tap + 1], pr_ref.at[tap], sems.at[3]).start()
    tab_copy.start()
    raw_copy(1, 1).start()
    hist_ref[...] = jnp.zeros_like(hist_ref)
    band_ref[...] = jnp.zeros_like(band_ref)
    early = lax.axis_index("tm") > 0

    def frames(i, y_ref):
        base = i * span

        def load(k, block):
            parts = []
            for part in range(2):
                start = pl.multiple_of(base + k * z.channels + (2 * block + part) * 8 * LANES, 8 * LANES)
                parts.append(buf[:, pl.ds(start, 8 * LANES)].astype(jnp.float32).reshape(8, LANES))
            return jnp.concatenate(parts)

        def history(k, block):
            return hist_ref[k, block * 16 : block * 16 + 16, :]

        def save(k, block, value):
            hist_ref[k, block * 16 : block * 16 + 16, :] = value

        fill_frames(z, history, load, pr_ref, y_ref, CHUNK, save)

    def powers(i, y_ref, t_refs):
        power = transform(z, y_ref, tab_ref, t_refs, CHUNK)
        late = power[z.hist]
        for k in range(z.hist + 1, CHUNK):
            late = late + power[k]
        head = power[0]
        for k in range(1, z.hist):
            head = head + power[k]
        skip = jnp.logical_and(i == 0, early)
        band_ref[...] = band_ref[...] + late + jnp.where(skip, 0.0, head)
        for k in range(CHUNK):
            power_ref[i * CHUNK + k] = power[k]

    pltpu.make_async_copy(pr_ref, pr_ref, sems.at[3]).wait()
    owners_copy.start()
    raw_copy(0, 0).wait()
    raw_copy(2, 0).start()
    frames(0, y0_ref)
    tab_copy.wait()
    delays_copy.start()

    def step(j, carry):
        i = 2 * j
        raw_copy(i + 1, 1).wait()
        raw_copy(i + 2, 0).wait()
        raw_copy(i + 3, 1).start()

        @pl.when(i + 4 < chunks)
        def _():
            raw_copy(i + 4, 0).start()

        frames(i + 1, y1_ref)
        powers(i, y0_ref, [t0_ref, t1_ref])
        frames(i + 2, y0_ref)
        powers(i + 1, y1_ref, [t2_ref, t3_ref])
        return carry

    lax.fori_loop(0, chunks // 2 - 1, step, 0)
    raw_copy(chunks - 1, 1).wait()
    owners_copy.wait()
    widths_copy.start()
    delays_copy.wait()
    frames(chunks - 1, y1_ref)
    powers(chunks - 2, y0_ref, [t0_ref, t1_ref])
    powers(chunks - 1, y1_ref, [t2_ref, t3_ref])
    unit = 1.0 / (math.sqrt(z.channels // NBLK) * math.sqrt(NBLK))
    trials = trial_ref.shape[1]
    tall = jnp.concatenate(
        [
            jnp.concatenate([trial_ref[g].astype(jnp.float32), jnp.zeros((8 - trials, NBLK), jnp.float32)])
            for g in range(z.groups)
        ]
    )
    spread = jnp.dot(
        tall.astype(jnp.bfloat16), wide_table(z, tab_ref, "expand"), preferred_element_type=jnp.float32
    )
    for g in range(z.groups):
        mine = spread[g * 8 : g * 8 + 8]
        hits = jnp.concatenate([jnp.where(mine == value, unit, 0.0) for value in range(MAXT + 1)])
        hits_ref[g] = hits.astype(jnp.bfloat16)

    def spectrum(start):
        start = pl.multiple_of(start, z.channels)
        return buf[:, pl.ds(start, z.channels)].astype(jnp.float32).reshape(DFT_A, LANES).astype(jnp.bfloat16)

    row = 0
    tail = (z.spec - z.hist) * z.channels
    starts = [jnp.where(early, 0, tail)] if z.n_tm == 2 else [tail, 0]
    for start in starts:
        for k in range(z.hist):
            msg_ref[row : row + DFT_A] = spectrum(start + k * z.channels)
            row += DFT_A
    high = band_ref[...].astype(jnp.bfloat16)
    msg_ref[row : row + z.rows] = high
    msg_ref[row + z.rows : row + 2 * z.rows] = (band_ref[...] - high.astype(jnp.float32)).astype(jnp.bfloat16)
    widths_copy.wait()


def search(z, power_ref, pr_ref, band_ref, own_ref, other_ref, tab_ref, hits_ref, owners_ref,
           out_ref, y_ref, t_ref, bound_ref, inv_ref, weighted_ref, sums_ref, mean_ref, sub_ref):
    me = lax.axis_index("tm")
    groups, spec = z.groups, z.spec
    chunks = spec // CHUNK
    total = band_ref[...]
    lo = z.bounds * z.raw_rows
    total = total + (
        other_ref[lo : lo + z.rows].astype(jnp.float32) + other_ref[lo + z.rows : lo + 2 * z.rows].astype(jnp.float32)
    )
    swap = jnp.logical_and(me > 0, z.n_tm == 2)
    y_ref[:, z.hist * LANES :] = jnp.zeros((DFT_A, LANES), jnp.bfloat16)
    for b in range(z.bounds):

        def take(k, block, first, b=b):
            start = b * z.raw_rows + k * DFT_A + block * 16
            own = own_ref[start : start + 16].astype(jnp.float32)
            other = other_ref[start : start + 16].astype(jnp.float32)
            return jnp.where(swap, other, own) if first else jnp.where(swap, own, other)

        fill_frames(
            z, lambda k, block: take(k, block, True), lambda k, block: take(k, block, False), pr_ref, y_ref, z.hist
        )
        power = transform(z, y_ref, tab_ref, [t_ref], z.hist)
        for k in range(z.hist):
            total = total + power[k]
            bound_ref[b * z.hist + k] = power[k]
    scale = float(z.taps * z.channels)
    inv_ref[...] = 1.0 / (total * (1.0 / (z.spec * z.n_tm)) + 1e-6 * scale)
    weighted_ref[...] = table(z, tab_ref, "weight").astype(jnp.float32)[: z.rows] * inv_ref[...]
    mine = jnp.maximum(me - 1, 0) * z.hist

    def power_of(i, k):
        value = power_ref[i * CHUNK + k]
        if k < z.hist:
            value = jnp.where(jnp.logical_and(me > 0, i == 0), bound_ref[mine + k], value)
        return value

    def means(i):
        for k in range(CHUNK):
            value = power_of(i, k) * weighted_ref[...]
            sums_ref[k * 8 : k * 8 + 8] = jnp.sum(value.reshape(z.rows // 8, 8, LANES), 0)
        acc = sums_ref[pl.ds(0, CHUNK, stride=8)]
        for j in range(1, 8):
            acc = acc + sums_ref[pl.ds(j, CHUNK, stride=8)]
        at = pl.multiple_of(i * CHUNK, CHUNK)
        mean_ref[pl.ds(at, CHUNK)] = jnp.broadcast_to(jnp.sum(acc, 1, keepdims=True), (CHUNK, LANES))

    parities = z.channels // NBLK // DFT_A
    lane = lax.broadcasted_iota(jnp.int32, (groups, LANES), 1)
    pad = jnp.zeros((z.rows16 - z.rows, LANES), jnp.float32)

    def picked(m, step, value):
        row = (m * FD + step) * parities * groups
        part = value[row : row + groups]
        for parity in range(1, parities):
            hit = (lane if m == 0 else LANES - 1 - lane) % parities == parity
            part = jnp.where(hit, value[row + parity * groups : row + (parity + 1) * groups], part)
        return part

    def flat_step(i, carry):
        flats = []
        open_sums = [list(carry[m]) for m in range(2)]
        for k in range(CHUNK):
            flat = power_of(i, k) * inv_ref[...] - mean_ref[pl.ds(i * CHUNK + k, 1)]
            flats.append(jnp.concatenate([flat, pad]).astype(jnp.bfloat16))
            if k % 2 == 0:
                continue
            masks = table(z, tab_ref, "masks")[:, : z.rows16]
            found = jnp.dot(masks, jnp.concatenate(flats[-2:], 1), preferred_element_type=jnp.float32)
            for half in range(2):
                value = found[:, half * LANES : (half + 1) * LANES]
                at = pl.multiple_of((i * CHUNK + k - 1 + half) * groups, 8)
                for m in range(2):
                    parts = [picked(m, step, value) for step in range(FD)]
                    sub_ref[m, pl.ds(at, groups)] = open_sums[m][0] + parts[0]
                    later = open_sums[m][1:] + [None]
                    open_sums[m] = [
                        parts[step + 1] if later[step] is None else later[step] + parts[step + 1]
                        for step in range(FD - 1)
                    ]
        means(jnp.minimum(i + 1, chunks - 1))
        return tuple(tuple(value) for value in open_sums)

    means(0)
    empty = jnp.zeros((groups, LANES), jnp.float32)
    carry = lax.fori_loop(0, chunks, flat_step, ((empty,) * (FD - 1),) * 2)
    length = spec + FD - 1
    stop = ceil_to(length, 16)
    for m in range(2):
        for step in range(FD - 1):
            sub_ref[m, (spec + step) * groups : (spec + step + 1) * groups] = carry[m][step]
    sub_ref[:, length * groups :] = jnp.zeros((2, (stop - length) * groups, LANES), jnp.float32)
    trials = out_ref.shape[2]
    out_ref[...] = jnp.zeros_like(out_ref)
    wide = 2 * LANES
    blank = jnp.zeros((wide - stop, wide), jnp.bfloat16)
    for g in range(groups):
        both = [sub_ref[m, pl.ds(g, stop, stride=groups)].astype(jnp.bfloat16) for m in range(2)]
        series = jnp.concatenate([jnp.concatenate(both, 1), blank])
        found = lax.dot_general(hits_ref[g], series, (((1,), (1,)), ((), ())), preferred_element_type=jnp.float32)
        dd = found[:8]
        for value in range(1, MAXT + 1):
            dd = dd + pltpu.roll(found[value * 8 : value * 8 + 8], value * TT, 1)
        owner = owners_ref[g]
        rank = jnp.int32(0)
        for earlier in range(g):
            rank = rank + jnp.where(owners_ref[earlier] == owner, 1, 0)
        late = pltpu.roll(dd, wide - (spec - WMAX + 1), 1)
        out_ref[owner * z.n_tm + jnp.minimum(me + 1, z.n_tm - 1), rank] = late[:trials, :LANES]
        out_ref[owner * z.n_tm + me, rank] = dd[:trials, :LANES]


def boxes(z, recv_ref, widths_ref, out_ref, d_ref):
    me = lax.axis_index("tm")
    trials = recv_ref.shape[2]
    rank = lax.broadcasted_iota(jnp.int32, (8, LANES), 0)
    count = widths_ref.shape[0]
    width = jnp.zeros((8, LANES), jnp.int32)
    for w in range(count):
        width = jnp.where(rank == w, widths_ref[w], width)
    norm = 1.0 / jnp.sqrt(width.astype(jnp.float32))
    weights = [jnp.where(width > lag, norm, 0.0) for lag in range(WMAX)]
    prior = WMAX - 1
    zero = jnp.zeros((8, LANES), jnp.float32)
    before = jnp.maximum(me - 1, 0)
    rows = z.capacity * trials
    for d in range(z.n_dm):
        own = recv_ref[d * z.n_tm + me].reshape(rows, LANES)
        past = recv_ref[d * z.n_tm + before].reshape(rows, LANES)
        past = jnp.where(me > 0, past, 0.0)
        wide = jnp.concatenate([own, jnp.zeros_like(own)], 1)
        wide = pltpu.roll(wide, prior, 1) + jnp.concatenate([past, jnp.zeros_like(past)], 1)
        for lag in range(WMAX):
            shift = prior - lag
            d_ref[lag] = (pltpu.roll(wide, 2 * LANES - shift, 1) if shift else wide)[:, :LANES]
        for s in range(z.capacity):
            for j in range(trials):
                acc = None
                for lag in range(WMAX):
                    part = d_ref[lag, s * trials + j : s * trials + j + 1, :] * weights[lag]
                    acc = part if acc is None else acc + part
                out_ref[s, d, 0, j] = acc[:count].astype(jnp.bfloat16)


def vmem_spec():
    return pl.BlockSpec(memory_space=pltpu.VMEM)


def smem_spec():
    return pl.BlockSpec(memory_space=pltpu.SMEM)


def hbm_spec():
    return pl.BlockSpec(memory_space=pltpu.HBM)


def kept(*values, space=pltpu.VMEM):
    return [pltpu.with_memory_space_constraint(value, space) for value in values]


def shards(n_dm, n_tm, raw, proto, delays, widths, owners):
    taps, channels = proto.shape
    groups, trials, _ = delays.shape
    z = Sizes(taps, channels, raw.shape[1] // channels, groups, n_dm, n_tm)
    tables, z.places = constants(z)
    params = pltpu.CompilerParams(vmem_limit_bytes=LIMIT)
    own_rows = z.raw_rows * (1 if n_tm == 2 else 2) + 2 * z.rows
    f32, bf16 = jnp.float32, jnp.bfloat16
    half = CHUNK // 2 * z.rows16
    power, pr, band, msg, tables, hits, owner, width = pl.pallas_call(
        functools.partial(channelize, z),
        out_shape=(
            pltpu.VMEM((z.spec, z.rows, LANES), f32),
            pltpu.VMEM((taps, 1, channels), f32),
            pltpu.VMEM((z.rows, LANES), f32),
            pltpu.VMEM((own_rows, LANES), bf16),
            pltpu.VMEM(tables.shape, bf16),
            pltpu.VMEM((groups, (MAXT + 1) * 8, 2 * LANES), bf16),
            pltpu.SMEM((groups,), jnp.int32),
            pltpu.SMEM(widths.shape, jnp.int32),
        ),
        in_specs=[hbm_spec()] * 6,
        out_specs=[vmem_spec()] * 6 + [smem_spec()] * 2,
        scratch_shapes=[
            pltpu.VMEM((1, z.spec * channels), bf16),
            pltpu.VMEM(delays.shape, jnp.int32),
            pltpu.VMEM((z.hist, DFT_A, LANES), f32),
            pltpu.VMEM((DFT_A, CHUNK * LANES), bf16),
            pltpu.VMEM((DFT_A, CHUNK * LANES), bf16),
            pltpu.VMEM((half, 2 * LANES), bf16),
            pltpu.VMEM((half, 2 * LANES), bf16),
            pltpu.VMEM((half, 2 * LANES), bf16),
            pltpu.VMEM((half, 2 * LANES), bf16),
            pltpu.SemaphoreType.DMA((4,)),
        ],
        compiler_params=params,
        name="channelize",
    )(
        *kept(raw, proto, tables, delays, owners.reshape(groups), widths, space=pltpu.HBM)
    )
    if n_tm == 2:
        own, other = msg, lax.ppermute(msg, "tm", [(0, 1), (1, 0)])
    else:
        every = lax.all_gather(msg, "tm")
        lasts = every[:-1, : z.raw_rows].reshape(-1, LANES)
        firsts = every[1:, z.raw_rows : 2 * z.raw_rows].reshape(-1, LANES)
        parts = every[:, 2 * z.raw_rows :].astype(f32).reshape(n_tm, 2, z.rows, LANES)
        rest = jnp.sum(parts, (0, 1)) - band
        high = rest.astype(bf16)
        pair = jnp.concatenate([high, (rest - high.astype(f32)).astype(bf16)])
        own, other = jnp.concatenate([lasts, pair]), jnp.concatenate([firsts, pair])
    length = ceil_to(z.spec + FD - 1, 16)
    out = pl.pallas_call(
        functools.partial(search, z),
        out_shape=pltpu.VMEM((n_dm * n_tm, z.capacity, trials, LANES), f32),
        in_specs=[vmem_spec()] * 7 + [smem_spec()],
        out_specs=vmem_spec(),
        scratch_shapes=[
            pltpu.VMEM((DFT_A, (z.hist + 1) * LANES), bf16),
            pltpu.VMEM((z.hist * z.rows16, 2 * LANES), bf16),
            pltpu.VMEM((z.bounds * z.hist, z.rows, LANES), f32),
            pltpu.VMEM((z.rows, LANES), f32),
            pltpu.VMEM((z.rows, LANES), f32),
            pltpu.VMEM((CHUNK * 8, LANES), f32),
            pltpu.VMEM((z.spec, LANES), f32),
            pltpu.VMEM((2, length * groups, LANES), f32),
        ],
        compiler_params=params,
        name="search",
    )(
        *kept(power, pr, band, own, other, tables, hits),
        *kept(owner, space=pltpu.SMEM),
    )
    recv = lax.all_to_all(out, ("dm", "tm"), split_axis=0, concat_axis=0, tiled=True)
    return pl.pallas_call(
        functools.partial(boxes, z),
        out_shape=jax.ShapeDtypeStruct((z.capacity, n_dm, 1, trials, widths.shape[0], z.spec), bf16),
        in_specs=[vmem_spec(), smem_spec()],
        out_specs=vmem_spec(),
        scratch_shapes=[pltpu.VMEM((WMAX, z.capacity * trials, LANES), f32)],
        compiler_params=params,
        name="boxes",
    )(*kept(recv), *kept(width, space=pltpu.SMEM))


def solution(mesh):
    sizes = dict(mesh.shape)
    return jax.shard_map(
        functools.partial(shards, sizes["dm"], sizes["tm"]),
        mesh=mesh,
        in_specs=(P(("group", "dm", "beam"), "tm"), P(), P(), P(), P()),
        out_specs=P("dm", "group", "beam", None, None, "tm"),
        check_vma=False,
    )
```

```python
import functools
import math

import jax
import jax.numpy as jnp
import numpy as np
from jax import lax
from jax.experimental import pallas as pl
from jax.experimental.pallas import tpu as pltpu
from jax.sharding import PartitionSpec as P

DFT_A = 128
NBLK = 64
FD = 4
TT = 8
MAXT = 3
WMAX = 8
LANES = 128
CHUNK = 16
LIMIT = 32 * 1024 * 1024


def ceil_to(value, unit):
    return -(-value // unit) * unit


def angle_tables(rows, cols, total):
    product = np.arange(rows)[:, None] * np.arange(cols)[None, :] % total
    angle = product.astype(np.float64) * (2.0 * math.pi / total)
    return np.cos(angle), np.sin(angle)


class Sizes:
    def __init__(self, taps, channels, spec, groups, n_dm, n_tm):
        self.taps, self.channels, self.spec, self.groups = taps, channels, spec, groups
        self.n_dm, self.n_tm = n_dm, n_tm
        self.side = channels // DFT_A
        self.half = DFT_A // 2 + 1
        self.rows = ceil_to(self.half, 8)
        self.rows16 = ceil_to(self.half, 16)
        self.hist = taps - 1
        self.raw_rows = self.hist * DFT_A
        self.bounds = n_tm - 1
        self.msg_rows = self.bounds * self.raw_rows + self.rows
        self.capacity = 2 * (groups // n_dm)
        self.low_chunks = (spec - (WMAX - 1) - MAXT * TT - (FD - 1)) // CHUNK
        self.high_rows = ceil_to(spec + FD - 1 - self.low_chunks * CHUNK, 16)


def constants(z):
    cos_a, sin_a = angle_tables(DFT_A, DFT_A, DFT_A)
    first = np.zeros((2 * z.rows, DFT_A))
    first[: z.half] = cos_a[: z.half]
    first[z.rows : z.rows + z.half] = -sin_a[: z.half]
    tw_cos, tw_sin = np.zeros((2, z.rows16, z.side))
    tw_cos[: z.half], tw_sin[: z.half] = angle_tables(z.half, z.side, z.channels)
    cos_b, sin_b = angle_tables(z.side, z.side, z.side)
    width = z.channels // NBLK
    fine = np.arange(z.groups)[:, None] * FD * (width - 1 - np.arange(width))[None, :] // (z.groups * (width - 1))
    parities = width // DFT_A
    masks = np.zeros((2, FD, parities, z.groups, LANES))
    for step in range(FD):
        for parity in range(parities):
            hit = fine[:, parity * DFT_A : (parity + 1) * DFT_A] == step
            masks[0, step, parity, :, : z.half] = hit[:, : z.half]
            masks[1, step, parity, :, 1 : z.half - 1] = hit[:, : z.half - 1 : -1]
    weight = np.zeros((z.rows16, LANES))
    weight[: z.half] = 2.0 / z.channels
    weight[0] = weight[z.half - 1] = 1.0 / z.channels
    expand = np.zeros((NBLK, 2 * z.side))
    lane = np.arange(z.side)
    expand[lane // parities, lane] = 1
    expand[(z.side - 1 - lane) // parities, z.side + lane] = 1
    tables = {
        "first": first,
        "cos": tw_cos,
        "sin": tw_sin,
        "second": np.concatenate([cos_b, sin_b]),
        "second_im": np.concatenate([-sin_b, cos_b]),
        "masks": masks.reshape(-1, LANES),
        "weight": weight,
        "expand": expand[:, : z.side],
        "expand_im": expand[:, z.side :],
    }
    places, row = {}, 0
    for name, table in tables.items():
        places[name] = (row, row + table.shape[0])
        row += table.shape[0]
    return jnp.asarray(np.concatenate(list(tables.values())), jnp.bfloat16), places


def table(z, ref, name):
    first, last = z.places[name]
    return ref[first:last]


def wide_table(z, ref, name):
    return jnp.concatenate([table(z, ref, name), table(z, ref, name + "_im")], 1)


def fill_frames(z, history, load, pr_ref, y_ref, count, save=None):
    for block in range(DFT_A // 16):
        rows = pl.ds(block * 16, 16)
        taps = [
            jnp.concatenate(
                [
                    pr_ref[tap, :, (2 * block + part) * 8 * LANES : (2 * block + part + 1) * 8 * LANES].reshape(8, LANES)
                    for part in range(2)
                ]
            )
            for tap in range(z.taps)
        ]
        window = [history(k, block) for k in range(z.hist)]
        for k in range(count):
            window.append(load(k, block))
            acc = window[0] * taps[0]
            for tap in range(1, z.taps):
                acc = acc + window[tap] * taps[tap]
            y_ref[rows, k * LANES : (k + 1) * LANES] = acc.astype(jnp.bfloat16)
            window.pop(0)
        if save is not None:
            for k in range(z.hist):
                save(k, block, window[k])


def transform(z, y_ref, tab_ref, t_refs, count):
    pad = jnp.zeros((z.rows16 - z.rows, LANES), jnp.float32)
    cos, sin = table(z, tab_ref, "cos"), table(z, tab_ref, "sin")
    part = count // len(t_refs)
    out = []
    for index, t_ref in enumerate(t_refs):
        for at in range(0, part, 2):
            pair = min(2, part - at)
            lane = (index * part + at) * LANES
            a = jnp.dot(table(z, tab_ref, "first"), y_ref[:, lane : lane + pair * LANES], preferred_element_type=jnp.float32)
            for k in range(pair):
                lanes = slice(k * LANES, (k + 1) * LANES)
                re = jnp.concatenate([a[: z.rows, lanes], pad]).astype(jnp.bfloat16)
                im = jnp.concatenate([a[z.rows :, lanes], pad]).astype(jnp.bfloat16)
                rows = slice((at + k) * z.rows16, (at + k + 1) * z.rows16)
                t_ref[rows, :LANES] = re * cos + im * sin
                t_ref[rows, LANES:] = im * cos - re * sin
        c = jnp.dot(t_ref[...], wide_table(z, tab_ref, "second"), preferred_element_type=jnp.float32)
        for k in range(part):
            rows = c[k * z.rows16 : k * z.rows16 + z.rows]
            re, im = rows[:, :LANES], rows[:, LANES:]
            out.append(re * re + im * im)
    return out


def channelize(z, raw_ref, proto_ref, tab_in, delays_ref, owners_in, widths_in,
               power_ref, pr_ref, band_ref, msg_ref, tab_ref, hits_ref, owners_ref, widths_ref,
               buf, trial_ref, hist_ref, y0_ref, y1_ref, t0_ref, t1_ref, t2_ref, t3_ref, sems):
    chunks = z.spec // CHUNK
    span = CHUNK * z.channels

    def raw_copy(i, side):
        part = pl.ds(pl.multiple_of(i * span, span), span)
        return pltpu.make_async_copy(raw_ref.at[:, part], buf.at[:, part], sems.at[side])

    tab_copy = pltpu.make_async_copy(tab_in, tab_ref, sems.at[2])
    delays_copy = pltpu.make_async_copy(delays_ref, trial_ref, sems.at[2])
    owners_copy = pltpu.make_async_copy(owners_in, owners_ref, sems.at[3])
    widths_copy = pltpu.make_async_copy(widths_in, widths_ref, sems.at[3])
    raw_copy(0, 0).start()
    for tap in range(z.taps):
        pltpu.make_async_copy(proto_ref.at[tap : tap + 1], pr_ref.at[tap], sems.at[3]).start()
    tab_copy.start()
    raw_copy(1, 1).start()
    hist_ref[...] = jnp.zeros_like(hist_ref)
    band_ref[...] = jnp.zeros_like(band_ref)
    early = lax.axis_index("tm") > 0

    def frames(i, y_ref):
        base = i * span

        def load(k, block):
            parts = []
            for part in range(2):
                start = pl.multiple_of(base + k * z.channels + (2 * block + part) * 8 * LANES, 8 * LANES)
                parts.append(buf[:, pl.ds(start, 8 * LANES)].astype(jnp.float32).reshape(8, LANES))
            return jnp.concatenate(parts)

        def history(k, block):
            return hist_ref[k, block * 16 : block * 16 + 16, :]

        def save(k, block, value):
            hist_ref[k, block * 16 : block * 16 + 16, :] = value

        fill_frames(z, history, load, pr_ref, y_ref, CHUNK, save)

    def powers(i, y_ref, t_refs):
        power = transform(z, y_ref, tab_ref, t_refs, CHUNK)
        late = power[z.hist]
        for k in range(z.hist + 1, CHUNK):
            late = late + power[k]
        head = power[0]
        for k in range(1, z.hist):
            head = head + power[k]
        skip = jnp.logical_and(i == 0, early)
        band_ref[...] = band_ref[...] + late + jnp.where(skip, 0.0, head)
        for k in range(CHUNK):
            power_ref[i * CHUNK + k] = power[k]

    pltpu.make_async_copy(pr_ref, pr_ref, sems.at[3]).wait()
    owners_copy.start()
    raw_copy(0, 0).wait()
    raw_copy(2, 0).start()
    frames(0, y0_ref)
    tab_copy.wait()
    delays_copy.start()

    def step(j, carry):
        i = 2 * j
        raw_copy(i + 1, 1).wait()
        raw_copy(i + 2, 0).wait()
        raw_copy(i + 3, 1).start()

        @pl.when(i + 4 < chunks)
        def _():
            raw_copy(i + 4, 0).start()

        frames(i + 1, y1_ref)
        powers(i, y0_ref, [t0_ref, t1_ref])
        frames(i + 2, y0_ref)
        powers(i + 1, y1_ref, [t2_ref, t3_ref])
        return carry

    lax.fori_loop(0, chunks // 2 - 1, step, 0)
    raw_copy(chunks - 1, 1).wait()
    owners_copy.wait()
    widths_copy.start()
    delays_copy.wait()
    frames(chunks - 1, y1_ref)
    powers(chunks - 2, y0_ref, [t0_ref, t1_ref])
    powers(chunks - 1, y1_ref, [t2_ref, t3_ref])
    unit = 1.0 / (math.sqrt(z.channels // NBLK) * math.sqrt(NBLK))
    trials = trial_ref.shape[1]
    tall = jnp.concatenate(
        [
            jnp.concatenate([trial_ref[g].astype(jnp.float32), jnp.zeros((8 - trials, NBLK), jnp.float32)])
            for g in range(z.groups)
        ]
    )
    spread = jnp.dot(
        tall.astype(jnp.bfloat16), wide_table(z, tab_ref, "expand"), preferred_element_type=jnp.float32
    )
    for g in range(z.groups):
        mine = spread[g * 8 : g * 8 + 8]
        hits = jnp.concatenate([jnp.where(mine == value, unit, 0.0) for value in range(MAXT + 1)])
        hits_ref[g] = hits.astype(jnp.bfloat16)

    def spectrum(start):
        start = pl.multiple_of(start, z.channels)
        return buf[:, pl.ds(start, z.channels)].astype(jnp.float32).reshape(DFT_A, LANES).astype(jnp.bfloat16)

    row = 0
    tail = (z.spec - z.hist) * z.channels
    starts = [jnp.where(early, 0, tail)] if z.n_tm == 2 else [tail, 0]
    for start in starts:
        for k in range(z.hist):
            msg_ref[row : row + DFT_A] = spectrum(start + k * z.channels)
            row += DFT_A
    high = band_ref[...].astype(jnp.bfloat16)
    msg_ref[row : row + z.rows] = high
    msg_ref[row + z.rows : row + 2 * z.rows] = (band_ref[...] - high.astype(jnp.float32)).astype(jnp.bfloat16)
    widths_copy.wait()


def boundary(z, power_ref, pr_ref, band_ref, own_ref, other_ref, tab_ref, y_ref, t_ref, bound_ref, inv_ref):
    me = lax.axis_index("tm")
    total = band_ref[...]
    lo = z.bounds * z.raw_rows
    total = total + (
        other_ref[lo : lo + z.rows].astype(jnp.float32) + other_ref[lo + z.rows : lo + 2 * z.rows].astype(jnp.float32)
    )
    swap = jnp.logical_and(me > 0, z.n_tm == 2)
    y_ref[:, z.hist * LANES :] = jnp.zeros((DFT_A, LANES), jnp.bfloat16)
    for b in range(z.bounds):

        def take(k, block, first, b=b):
            start = b * z.raw_rows + k * DFT_A + block * 16
            own = own_ref[start : start + 16].astype(jnp.float32)
            other = other_ref[start : start + 16].astype(jnp.float32)
            return jnp.where(swap, other, own) if first else jnp.where(swap, own, other)

        fill_frames(
            z, lambda k, block: take(k, block, True), lambda k, block: take(k, block, False), pr_ref, y_ref, z.hist
        )
        power = transform(z, y_ref, tab_ref, [t_ref], z.hist)
        for k in range(z.hist):
            total = total + power[k]
            bound_ref[b * z.hist + k] = power[k]
    scale = float(z.taps * z.channels)
    inv_ref[...] = 1.0 / (total * (1.0 / (z.spec * z.n_tm)) + 1e-6 * scale)


def subbands(z, first, last, power_ref, bound_ref, inv_ref, tab_ref, weighted_ref, sums_ref, mean_ref, sub_ref):
    me = lax.axis_index("tm")
    groups = z.groups
    weighted_ref[...] = table(z, tab_ref, "weight").astype(jnp.float32)[: z.rows] * inv_ref[...]
    mine = jnp.maximum(me - 1, 0) * z.hist

    def power_of(i, k):
        value = power_ref[i * CHUNK + k]
        if first == 0 and k < z.hist:
            value = jnp.where(jnp.logical_and(me > 0, i == 0), bound_ref[mine + k], value)
        return value

    def means(i):
        for k in range(CHUNK):
            value = power_of(i, k) * weighted_ref[...]
            sums_ref[k * 8 : k * 8 + 8] = jnp.sum(value.reshape(z.rows // 8, 8, LANES), 0)
        acc = sums_ref[pl.ds(0, CHUNK, stride=8)]
        for j in range(1, 8):
            acc = acc + sums_ref[pl.ds(j, CHUNK, stride=8)]
        at = pl.multiple_of(i * CHUNK, CHUNK)
        mean_ref[pl.ds(at, CHUNK)] = jnp.broadcast_to(jnp.sum(acc, 1, keepdims=True), (CHUNK, LANES))

    parities = z.channels // NBLK // DFT_A
    lane = lax.broadcasted_iota(jnp.int32, (groups, LANES), 1)
    pad = jnp.zeros((z.rows16 - z.rows, LANES), jnp.float32)

    def picked(m, step, value):
        row = (m * FD + step) * parities * groups
        part = value[row : row + groups]
        for parity in range(1, parities):
            hit = (lane if m == 0 else LANES - 1 - lane) % parities == parity
            part = jnp.where(hit, value[row + parity * groups : row + (parity + 1) * groups], part)
        return part

    def flat_step(i, carry):
        flats = []
        open_sums = [list(carry[m]) for m in range(2)]
        for k in range(CHUNK):
            flat = power_of(i, k) * inv_ref[...] - mean_ref[pl.ds(i * CHUNK + k, 1)]
            flats.append(jnp.concatenate([flat, pad]).astype(jnp.bfloat16))
            if k % 2 == 0:
                continue
            masks = table(z, tab_ref, "masks")[:, : z.rows16]
            found = jnp.dot(masks, jnp.concatenate(flats[-2:], 1), preferred_element_type=jnp.float32)
            for half in range(2):
                value = found[:, half * LANES : (half + 1) * LANES]
                at = pl.multiple_of(((i - first) * CHUNK + k - 1 + half) * groups, 8)
                for m in range(2):
                    parts = [picked(m, step, value) for step in range(FD)]
                    sub_ref[m, pl.ds(at, groups)] = open_sums[m][0] + parts[0]
                    later = open_sums[m][1:] + [None]
                    open_sums[m] = [
                        parts[step + 1] if later[step] is None else later[step] + parts[step + 1]
                        for step in range(FD - 1)
                    ]
        means(jnp.minimum(i + 1, last - 1))
        return tuple(tuple(value) for value in open_sums)

    means(first)
    empty = jnp.zeros((groups, LANES), jnp.float32)
    return lax.fori_loop(first, last, flat_step, ((empty,) * (FD - 1),) * 2)


def delayed(z, hits, series):
    lane = lax.broadcasted_iota(jnp.int32, (8, LANES), 1)
    found = lax.dot_general(hits, series, (((1,), (1,)), ((), ())), preferred_element_type=jnp.float32)
    total = found[:8]
    for value in range(1, MAXT + 1):
        moved = pltpu.roll(found[value * 8 : value * 8 + 8], value * TT, 1)
        total = total + jnp.where(lane >= value * TT, moved, 0.0)
    return total


def tails(z, power_ref, pr_ref, band_ref, own_ref, other_ref, tab_ref, hits_ref,
          prev_ref, high_ref, bound_ref, inv_ref, y_ref, t_ref, late_ref, weighted_ref, sums_ref, mean_ref):
    groups = z.groups
    boundary(z, power_ref, pr_ref, band_ref, own_ref, other_ref, tab_ref, y_ref, t_ref, bound_ref, inv_ref)
    carry = subbands(
        z, z.low_chunks, z.spec // CHUNK, power_ref, bound_ref, inv_ref, tab_ref, weighted_ref, sums_ref, mean_ref, high_ref
    )
    count = z.high_rows
    done = z.spec - z.low_chunks * CHUNK
    for m in range(2):
        for step in range(FD - 1):
            high_ref[m, (done + step) * groups : (done + step + 1) * groups] = carry[m][step]
    high_ref[:, (done + FD - 1) * groups :] = jnp.zeros((2, (count - done - FD + 1) * groups, LANES), jnp.float32)
    blank = jnp.zeros((LANES - count, 2 * LANES), jnp.bfloat16)
    trials = late_ref.shape[1]
    lane = lax.broadcasted_iota(jnp.int32, (8, LANES), 1)
    start = done - (WMAX - 1)
    for g in range(groups):
        both = [high_ref[m, pl.ds(g, count, stride=groups)].astype(jnp.bfloat16) for m in range(2)]
        dd = delayed(z, hits_ref[g], jnp.concatenate([jnp.concatenate(both, 1), blank]))
        late = pltpu.roll(dd, LANES - start, 1)
        late_ref[g] = jnp.where(lane < WMAX - 1 + MAXT * TT + FD - 1, late, 0.0)[:trials]
    prev_ref[...] = late_ref[...].reshape(groups * trials, LANES).astype(jnp.bfloat16)


def bulk(z, power_ref, bound_ref, inv_ref, tab_ref, hits_ref, high_ref,
         main_ref, weighted_ref, sums_ref, mean_ref, low_ref, join_ref):
    groups = z.groups
    carry = subbands(z, 0, z.low_chunks, power_ref, bound_ref, inv_ref, tab_ref, weighted_ref, sums_ref, mean_ref, low_ref)
    join_ref[...] = jnp.zeros_like(join_ref)
    for m in range(2):
        for step in range(FD - 1):
            join_ref[m, step * groups : (step + 1) * groups] = carry[m][step]
    low = z.low_chunks * CHUNK
    trials = main_ref.shape[1]
    for g in range(groups):
        both = []
        for m in range(2):
            edge = high_ref[m, pl.ds(g, 8, stride=groups)] + join_ref[m, pl.ds(g, 8, stride=groups)]
            rest = high_ref[m, pl.ds(8 * groups + g, z.spec - low - 8, stride=groups)]
            both.append(jnp.concatenate([low_ref[m, pl.ds(g, low, stride=groups)], edge, rest]).astype(jnp.bfloat16))
        main_ref[g] = delayed(z, hits_ref[g], jnp.concatenate(both, 1))[:trials]


def parcels(z, main_ref, prev_ref, owners_ref, stay_ref, leave_ref, late_ref, all_ref):
    me = lax.axis_index("dm")
    all_ref[...] = jnp.zeros_like(all_ref)
    late_ref[...] = prev_ref[...].astype(jnp.float32).reshape(late_ref.shape)
    for g in range(z.groups):
        owner = owners_ref[g]
        rank = jnp.int32(0)
        for earlier in range(g):
            rank = rank + jnp.where(owners_ref[earlier] == owner, 1, 0)
        all_ref[owner ^ me, 0, rank] = main_ref[g]
        all_ref[owner ^ me, 1, rank] = late_ref[g]
    for r in range(z.n_dm):
        value = all_ref[r].reshape(stay_ref.shape[2:]).astype(jnp.bfloat16)
        (leave_ref if r % 2 else stay_ref)[r // 2, 0] = value


def relay(held_ref, got_ref, stay_ref, leave_ref):
    count = held_ref.shape[1]
    for r in range(held_ref.shape[0]):
        target = leave_ref if r % 2 else stay_ref
        target[r // 2, :count] = held_ref[r]
        target[r // 2, count:] = got_ref[r]


def boxes(z, widths_ref, *refs):
    held_ref, got_ref, out_ref, d_ref = refs
    early = lax.axis_index("tm") == 0
    me = lax.axis_index("dm")
    trials = out_ref.shape[3]
    near = held_ref.shape[1]
    rank = lax.broadcasted_iota(jnp.int32, (8, LANES), 0)
    count = widths_ref.shape[0]
    width = jnp.zeros((8, LANES), jnp.int32)
    for w in range(count):
        width = jnp.where(rank == w, widths_ref[w], width)
    norm = 1.0 / jnp.sqrt(width.astype(jnp.float32))
    weights = [jnp.where(width > lag, norm, 0.0) for lag in range(WMAX)]
    prior = WMAX - 1
    rows = z.capacity * trials
    for r in range(z.n_dm):
        ref, at = (held_ref, r) if r < near else (got_ref, r - near)
        own = ref[0, at, :rows].astype(jnp.float32)
        past = jnp.where(early, 0.0, ref[0, at, rows:].astype(jnp.float32))
        wide = jnp.concatenate([own, jnp.zeros_like(own)], 1)
        wide = pltpu.roll(wide, prior, 1) + jnp.concatenate([past, jnp.zeros_like(past)], 1)
        for lag in range(WMAX):
            shift = prior - lag
            d_ref[r, lag] = (pltpu.roll(wide, 2 * LANES - shift, 1) if shift else wide)[:, :LANES]
        for s in range(z.capacity):
            for j in range(trials):
                acc = None
                for lag in range(WMAX):
                    part = d_ref[r, lag, s * trials + j : s * trials + j + 1, :] * weights[lag]
                    acc = part if acc is None else acc + part
                out_ref[s, me ^ r, 0, j] = acc[:count].astype(jnp.bfloat16)


def vmem_spec():
    return pl.BlockSpec(memory_space=pltpu.VMEM)


def smem_spec():
    return pl.BlockSpec(memory_space=pltpu.SMEM)


def hbm_spec():
    return pl.BlockSpec(memory_space=pltpu.HBM)


def kept(*values, space=pltpu.VMEM):
    return [pltpu.with_memory_space_constraint(value, space) for value in values]


def shards(n_dm, n_tm, raw, proto, delays, widths, owners):
    taps, channels = proto.shape
    groups, trials, _ = delays.shape
    z = Sizes(taps, channels, raw.shape[1] // channels, groups, n_dm, n_tm)
    tables, z.places = constants(z)
    params = pltpu.CompilerParams(vmem_limit_bytes=LIMIT)
    own_rows = z.raw_rows * (1 if n_tm == 2 else 2) + 2 * z.rows
    f32, bf16 = jnp.float32, jnp.bfloat16
    half = CHUNK // 2 * z.rows16
    power, pr, band, msg, tables, hits, owner, width = pl.pallas_call(
        functools.partial(channelize, z),
        out_shape=(
            pltpu.VMEM((z.spec, z.rows, LANES), f32),
            pltpu.VMEM((taps, 1, channels), f32),
            pltpu.VMEM((z.rows, LANES), f32),
            pltpu.VMEM((own_rows, LANES), bf16),
            pltpu.VMEM(tables.shape, bf16),
            pltpu.VMEM((groups, (MAXT + 1) * 8, 2 * LANES), bf16),
            pltpu.SMEM((groups,), jnp.int32),
            pltpu.SMEM(widths.shape, jnp.int32),
        ),
        in_specs=[hbm_spec()] * 6,
        out_specs=[vmem_spec()] * 6 + [smem_spec()] * 2,
        scratch_shapes=[
            pltpu.VMEM((1, z.spec * channels), bf16),
            pltpu.VMEM(delays.shape, jnp.int32),
            pltpu.VMEM((z.hist, DFT_A, LANES), f32),
            pltpu.VMEM((DFT_A, CHUNK * LANES), bf16),
            pltpu.VMEM((DFT_A, CHUNK * LANES), bf16),
            pltpu.VMEM((half, 2 * LANES), bf16),
            pltpu.VMEM((half, 2 * LANES), bf16),
            pltpu.VMEM((half, 2 * LANES), bf16),
            pltpu.VMEM((half, 2 * LANES), bf16),
            pltpu.SemaphoreType.DMA((4,)),
        ],
        compiler_params=params,
        name="channelize",
    )(
        *kept(raw, proto, tables, delays, owners.reshape(groups), widths, space=pltpu.HBM)
    )
    if n_tm == 2:
        own, other = msg, lax.ppermute(msg, "tm", [(0, 1), (1, 0)])
    else:
        every = lax.all_gather(msg, "tm")
        lasts = every[:-1, : z.raw_rows].reshape(-1, LANES)
        firsts = every[1:, z.raw_rows : 2 * z.raw_rows].reshape(-1, LANES)
        parts = every[:, 2 * z.raw_rows :].astype(f32).reshape(n_tm, 2, z.rows, LANES)
        rest = jnp.sum(parts, (0, 1)) - band
        high = rest.astype(bf16)
        pair = jnp.concatenate([high, (rest - high.astype(f32)).astype(bf16)])
        own, other = jnp.concatenate([lasts, pair]), jnp.concatenate([firsts, pair])
    work = [
        pltpu.VMEM((z.rows, LANES), f32),
        pltpu.VMEM((CHUNK * 8, LANES), f32),
        pltpu.VMEM((z.spec, LANES), f32),
    ]
    prev, high, bound, inv = pl.pallas_call(
        functools.partial(tails, z),
        out_shape=(
            pltpu.VMEM((groups * trials, LANES), bf16),
            pltpu.VMEM((2, z.high_rows * groups, LANES), f32),
            pltpu.VMEM((z.bounds * z.hist, z.rows, LANES), f32),
            pltpu.VMEM((z.rows, LANES), f32),
        ),
        in_specs=[vmem_spec()] * 7,
        out_specs=[vmem_spec()] * 4,
        scratch_shapes=[
            pltpu.VMEM((DFT_A, (z.hist + 1) * LANES), bf16),
            pltpu.VMEM((z.hist * z.rows16, 2 * LANES), bf16),
            pltpu.VMEM((groups, trials, LANES), f32),
        ]
        + work,
        compiler_params=params,
        name="tails",
    )(*kept(power, pr, band, own, other, tables, hits))
    before = lax.ppermute(prev, "tm", [(i, (i + 1) % n_tm) for i in range(n_tm)])
    main = pl.pallas_call(
        functools.partial(bulk, z),
        out_shape=pltpu.VMEM((groups, trials, LANES), f32),
        in_specs=[vmem_spec()] * 6,
        out_specs=vmem_spec(),
        scratch_shapes=work
        + [
            pltpu.VMEM((2, z.low_chunks * CHUNK * groups, LANES), f32),
            pltpu.VMEM((2, 8 * groups, LANES), f32),
        ],
        compiler_params=params,
        cost_estimate=pl.CostEstimate(flops=10**9, bytes_accessed=8 * 10**6, transcendentals=0),
        name="bulk",
    )(*kept(power, bound, inv, tables, hits, high))
    slots = (2, z.capacity, trials, LANES)
    parcel = (2 * z.capacity * trials, LANES)
    held, leaving = pl.pallas_call(
        functools.partial(parcels, z),
        out_shape=(pltpu.VMEM((n_dm // 2, 1, *parcel), bf16),) * 2,
        in_specs=[vmem_spec()] * 2 + [smem_spec()],
        out_specs=[vmem_spec()] * 2,
        scratch_shapes=[pltpu.VMEM((groups, trials, LANES), f32), pltpu.VMEM((n_dm, *slots), f32)],
        compiler_params=params,
        name="parcels",
    )(*kept(main, before), *kept(owner, space=pltpu.SMEM))
    bit = 1
    while True:
        got = lax.ppermute(leaving, "dm", [(i, i ^ bit) for i in range(n_dm)])
        bit *= 2
        if bit == n_dm:
            break
        held, leaving = pl.pallas_call(
            relay,
            out_shape=(pltpu.VMEM((n_dm // 2 // bit, bit, *parcel), bf16),) * 2,
            in_specs=[vmem_spec()] * 2,
            out_specs=[vmem_spec()] * 2,
            compiler_params=params,
            name="relay",
        )(*kept(held, got))
    return pl.pallas_call(
        functools.partial(boxes, z),
        out_shape=jax.ShapeDtypeStruct((z.capacity, n_dm, 1, trials, widths.shape[0], z.spec), bf16),
        in_specs=[smem_spec()] + [vmem_spec()] * 2,
        out_specs=vmem_spec(),
        scratch_shapes=[pltpu.VMEM((n_dm, WMAX, z.capacity * trials, LANES), f32)],
        compiler_params=params,
        name="boxes",
    )(*kept(width, space=pltpu.SMEM), *kept(held, got))


def solution(mesh):
    sizes = dict(mesh.shape)
    return jax.shard_map(
        functools.partial(shards, sizes["dm"], sizes["tm"]),
        mesh=mesh,
        in_specs=(P(("group", "dm", "beam"), "tm"), P(), P(), P(), P()),
        out_specs=P("dm", "group", "beam", None, None, "tm"),
        check_vma=False,
    )
```

```python
import functools
import math

import jax
import jax.numpy as jnp
import numpy as np
from jax import lax
from jax.experimental import pallas as pl
from jax.experimental.pallas import tpu as pltpu
from jax.sharding import PartitionSpec as P

DFT_A = 128
NBLK = 64
FD = 4
TT = 8
MAXT = 3
WMAX = 8
LANES = 128
CHUNK = 16
LIMIT = 32 * 1024 * 1024


def ceil_to(value, unit):
    return -(-value // unit) * unit


def angle_tables(rows, cols, total):
    product = np.arange(rows)[:, None] * np.arange(cols)[None, :] % total
    angle = product.astype(np.float64) * (2.0 * math.pi / total)
    return np.cos(angle), np.sin(angle)


class Sizes:
    def __init__(self, taps, channels, spec, groups, n_dm, n_tm):
        self.taps, self.channels, self.spec, self.groups = taps, channels, spec, groups
        self.n_dm, self.n_tm = n_dm, n_tm
        self.side = channels // DFT_A
        self.rows = DFT_A // 2
        self.deep = self.rows + 16
        self.band_rows = self.rows + 8
        self.hist = taps - 1
        self.raw_rows = self.hist * DFT_A
        self.bounds = n_tm - 1
        self.capacity = 2 * (groups // n_dm)
        self.low_chunks = (spec - (WMAX - 1) - MAXT * TT - (FD - 1)) // CHUNK
        self.high_rows = ceil_to(spec + FD - 1 - self.low_chunks * CHUNK, 16)


def constants(z):
    cos_a, sin_a = angle_tables(DFT_A, DFT_A, DFT_A)
    first = np.concatenate([cos_a[: z.rows], -sin_a[: z.rows]])
    first[z.rows] = cos_a[z.rows]
    tw_cos, tw_sin = angle_tables(z.rows + 1, z.side, z.channels)
    edge = np.zeros((16, z.side))
    edge[0], edge[1] = tw_cos[z.rows], -tw_sin[z.rows]
    tw_cos, tw_sin = tw_cos[: z.rows], tw_sin[: z.rows]
    hidden = tw_cos.copy()
    hidden[0] = 0
    cos_b, sin_b = angle_tables(z.side, z.side, z.side)
    width = z.channels // NBLK
    fine = np.arange(z.groups)[:, None] * FD * (width - 1 - np.arange(width))[None, :] // (z.groups * (width - 1))
    parities = width // DFT_A
    masks = np.zeros((2, FD, parities, z.groups, LANES))
    for step in range(FD):
        for parity in range(parities):
            hit = fine[:, parity * DFT_A : (parity + 1) * DFT_A] == step
            masks[0, step, parity, :, : z.rows] = hit[:, : z.rows]
            masks[0, step, parity, :, z.rows : z.deep] = hit[:, z.rows, None]
            masks[1, step, parity, :, 1 : z.rows] = hit[:, : z.rows : -1]
    weight = np.full((z.deep, LANES), 2.0 / z.channels)
    weight[0] = weight[z.rows] = 1.0 / z.channels
    expand = np.zeros((NBLK, 2 * z.side))
    lane = np.arange(z.side)
    expand[lane // parities, lane] = 1
    expand[(z.side - 1 - lane) // parities, z.side + lane] = 1
    tables = {
        "first": first,
        "cos": tw_cos,
        "hidden": hidden,
        "edge": edge,
        "sin": tw_sin,
        "second": np.concatenate([cos_b, sin_b]),
        "second_im": np.concatenate([-sin_b, cos_b]),
        "masks": masks.reshape(-1, LANES),
        "weight": weight,
        "expand": expand[:, : z.side],
        "expand_im": expand[:, z.side :],
    }
    places, row = {}, 0
    for name, table in tables.items():
        places[name] = (row, row + table.shape[0])
        row += table.shape[0]
    return jnp.asarray(np.concatenate(list(tables.values())), jnp.bfloat16), places


def table(z, ref, name):
    first, last = z.places[name]
    return ref[first:last]


def wide_table(z, ref, name):
    return jnp.concatenate([table(z, ref, name), table(z, ref, name + "_im")], 1)


def fill_frames(z, history, load, pr_ref, y_ref, count, save=None):
    for block in range(DFT_A // 16):
        rows = pl.ds(block * 16, 16)
        taps = [
            jnp.concatenate(
                [
                    pr_ref[tap, :, (2 * block + part) * 8 * LANES : (2 * block + part + 1) * 8 * LANES].reshape(8, LANES)
                    for part in range(2)
                ]
            )
            for tap in range(z.taps)
        ]
        window = [history(k, block) for k in range(z.hist)]
        for k in range(count):
            window.append(load(k, block))
            acc = window[0] * taps[0]
            for tap in range(1, z.taps):
                acc = acc + window[tap] * taps[tap]
            y_ref[rows, k * LANES : (k + 1) * LANES] = acc.astype(jnp.bfloat16)
            window.pop(0)
        if save is not None:
            for k in range(z.hist):
                save(k, block, window[k])


def transform(z, y_ref, tab_ref, t_refs, edge_ref, count):
    cos, hidden, sin = (table(z, tab_ref, name) for name in ("cos", "hidden", "sin"))
    part = count // len(t_refs)
    out = []
    for index, t_ref in enumerate(t_refs):
        for at in range(0, part, 2):
            pair = min(2, part - at)
            lane = (index * part + at) * LANES
            a = jnp.dot(
                table(z, tab_ref, "first"), y_ref[:, lane : lane + pair * LANES], preferred_element_type=jnp.float32
            )
            for k in range(pair):
                lanes = slice(k * LANES, (k + 1) * LANES)
                edge_ref[index * part + at + k : index * part + at + k + 1] = a[z.rows : z.rows + 1, lanes]
                re, im = a[: z.rows, lanes].astype(jnp.bfloat16), a[z.rows :, lanes].astype(jnp.bfloat16)
                rows = slice((at + k) * z.rows, (at + k + 1) * z.rows)
                t_ref[rows, :LANES] = re * cos + im * sin
                t_ref[rows, LANES:] = im * hidden - re * sin
        last = index + 1 == len(t_refs)
        if last:
            turn = table(z, tab_ref, "edge").astype(jnp.float32)
            rows = slice(part * z.rows, part * z.rows + 16)
            t_ref[rows, :LANES] = (edge_ref[...] * turn[0:1]).astype(jnp.bfloat16)
            t_ref[rows, LANES:] = (edge_ref[...] * turn[1:2]).astype(jnp.bfloat16)
        c = jnp.dot(
            t_ref[: part * z.rows + (16 if last else 0)], wide_table(z, tab_ref, "second"),
            preferred_element_type=jnp.float32,
        )
        for k in range(part):
            rows = c[k * z.rows : (k + 1) * z.rows]
            re, im = rows[:, :LANES], rows[:, LANES:]
            out.append(re * re + im * im)
    re, im = c[part * z.rows :, :LANES], c[part * z.rows :, LANES:]
    return out, re * re + im * im


def channelize(z, raw_ref, proto_ref, tab_in, delays_ref, owners_in, widths_in,
               power_ref, edges_ref, pr_ref, band_ref, msg_ref, tab_ref, trial_ref, owners_ref, widths_ref,
               buf, hist_ref, y0_ref, y1_ref, t0_ref, t1_ref, t2_ref, t3_ref, e0_ref, e1_ref, sum_ref, sems):
    chunks = z.spec // CHUNK
    span = CHUNK * z.channels

    def raw_copy(first, last, side):
        part = pl.ds(first * span, (last - first) * span)
        return pltpu.make_async_copy(raw_ref.at[:, part], buf.at[:, part], sems.at[side])

    tab_copy = pltpu.make_async_copy(tab_in, tab_ref, sems.at[2])
    delays_copy = pltpu.make_async_copy(delays_ref, trial_ref, sems.at[2])
    owners_copy = pltpu.make_async_copy(owners_in, owners_ref, sems.at[3])
    widths_copy = pltpu.make_async_copy(widths_in, widths_ref, sems.at[3])
    early_copies = [raw_copy(0, 1, 0), raw_copy(1, 3, 1), raw_copy(3, 5, 4), raw_copy(5, chunks, 0)]
    early_copies[0].start()
    for tap in range(z.taps):
        pltpu.make_async_copy(proto_ref.at[tap : tap + 1], pr_ref.at[tap], sems.at[3]).start()
    tab_copy.start()
    early_copies[1].start()
    hist_ref[...] = jnp.zeros_like(hist_ref)
    band_ref[...] = jnp.zeros_like(band_ref)
    sum_ref[...] = jnp.zeros_like(sum_ref)
    early = lax.axis_index("tm") > 0
    place = lax.broadcasted_iota(jnp.int32, (16, LANES), 0)

    def frames(i, y_ref):
        base = i * span

        def load(k, block):
            parts = []
            for part in range(2):
                start = pl.multiple_of(base + k * z.channels + (2 * block + part) * 8 * LANES, 8 * LANES)
                parts.append(buf[:, pl.ds(start, 8 * LANES)].astype(jnp.float32).reshape(8, LANES))
            return jnp.concatenate(parts)

        def history(k, block):
            return hist_ref[k, block * 16 : block * 16 + 16, :]

        def save(k, block, value):
            hist_ref[k, block * 16 : block * 16 + 16, :] = value

        fill_frames(z, history, load, pr_ref, y_ref, CHUNK, save)

    def powers(i, y_ref, t_refs, e_ref):
        power, edges = transform(z, y_ref, tab_ref, t_refs, e_ref, CHUNK)
        late = power[z.hist]
        for k in range(z.hist + 1, CHUNK):
            late = late + power[k]
        head = power[0]
        for k in range(1, z.hist):
            head = head + power[k]
        skip = jnp.logical_and(i == 0, early)
        band_ref[: z.rows] = band_ref[: z.rows] + late + jnp.where(skip, 0.0, head)
        sum_ref[...] = sum_ref[...] + jnp.where(jnp.logical_and(skip, place < z.hist), 0.0, edges)
        edges_ref[pl.ds(pl.multiple_of(i * CHUNK, CHUNK), CHUNK)] = edges
        for k in range(CHUNK):
            power_ref[i * CHUNK + k] = power[k]

    pltpu.make_async_copy(pr_ref, pr_ref, sems.at[3]).wait()
    owners_copy.start()
    early_copies[0].wait()
    early_copies[2].start()
    frames(0, y0_ref)
    early_copies[3].start()
    tab_copy.wait()
    delays_copy.start()

    def step(j, carry):
        i = 2 * j
        for turn in range(3):

            @pl.when(j == turn)
            def _(turn=turn):
                early_copies[turn + 1].wait()

        frames(i + 1, y1_ref)
        powers(i, y0_ref, [t0_ref, t1_ref], e0_ref)
        frames(i + 2, y0_ref)
        powers(i + 1, y1_ref, [t2_ref, t3_ref], e1_ref)
        return carry

    lax.fori_loop(0, chunks // 2 - 1, step, 0)
    owners_copy.wait()
    widths_copy.start()
    delays_copy.wait()
    frames(chunks - 1, y1_ref)
    powers(chunks - 2, y0_ref, [t0_ref, t1_ref], e0_ref)
    powers(chunks - 1, y1_ref, [t2_ref, t3_ref], e1_ref)
    def spectrum(start):
        start = pl.multiple_of(start, z.channels)
        return buf[:, pl.ds(start, z.channels)].astype(jnp.float32).reshape(DFT_A, LANES).astype(jnp.bfloat16)

    row = 0
    tail = (z.spec - z.hist) * z.channels
    starts = [jnp.where(early, 0, tail)] if z.n_tm == 2 else [tail, 0]
    for start in starts:
        for k in range(z.hist):
            msg_ref[row : row + DFT_A] = spectrum(start + k * z.channels)
            row += DFT_A
    total = jnp.sum(sum_ref[...], 0, keepdims=True)
    rest = jnp.concatenate([total, jnp.zeros((15, LANES), jnp.float32)])
    band_ref[z.rows :] = rest[: z.band_rows - z.rows]
    msg_ref[row : row + z.deep] = jnp.concatenate([band_ref[: z.rows], rest]).astype(jnp.bfloat16)
    widths_copy.wait()


def coarse(z, tab_ref, trial_ref, hits_ref):
    unit = 1.0 / (math.sqrt(z.channels // NBLK) * math.sqrt(NBLK))
    trials = trial_ref.shape[1]
    tall = jnp.concatenate(
        [
            jnp.concatenate([trial_ref[g].astype(jnp.float32), jnp.zeros((8 - trials, NBLK), jnp.float32)])
            for g in range(z.groups)
        ]
    )
    spread = jnp.dot(
        tall.astype(jnp.bfloat16), wide_table(z, tab_ref, "expand"), preferred_element_type=jnp.float32
    )
    for g in range(z.groups):
        mine = spread[g * 8 : g * 8 + 8]
        hits = jnp.concatenate([jnp.where(mine == value, unit, 0.0) for value in range(MAXT + 1)])
        hits_ref[g] = hits.astype(jnp.bfloat16)


def boundary(z, pr_ref, band_ref, own_ref, other_ref, tab_ref, y_ref, t_ref, e_ref, bound_ref, sides_ref, inv_ref):
    me = lax.axis_index("tm")
    lo = z.bounds * z.raw_rows
    rest = other_ref[lo : lo + z.deep].astype(jnp.float32)
    total = band_ref[: z.rows] + rest[: z.rows]
    edge = band_ref[z.rows :] + rest[z.rows : z.band_rows]
    e_ref[...] = jnp.zeros_like(e_ref)
    swap = jnp.logical_and(me > 0, z.n_tm == 2)
    y_ref[:, z.hist * LANES :] = jnp.zeros((DFT_A, LANES), jnp.bfloat16)
    for b in range(z.bounds):

        def take(k, block, first, b=b):
            start = b * z.raw_rows + k * DFT_A + block * 16
            own = own_ref[start : start + 16].astype(jnp.float32)
            other = other_ref[start : start + 16].astype(jnp.float32)
            return jnp.where(swap, other, own) if first else jnp.where(swap, own, other)

        fill_frames(
            z, lambda k, block: take(k, block, True), lambda k, block: take(k, block, False), pr_ref, y_ref, z.hist
        )
        power, edges = transform(z, y_ref, tab_ref, [t_ref], e_ref, z.hist)
        sides_ref[b] = edges
        edge = edge + jnp.sum(edges, 0, keepdims=True)
        for k in range(z.hist):
            total = total + power[k]
            bound_ref[b * z.hist + k] = power[k]
    scale = float(z.taps * z.channels)
    total = jnp.concatenate([total, edge])
    inv_ref[...] = 1.0 / (total * (1.0 / (z.spec * z.n_tm)) + 1e-6 * scale)


def subbands(
    z, first, last, power_ref, edges_ref, bound_ref, sides_ref, inv_ref, tab_ref, weighted_ref, sums_ref, mean_ref, sub_ref
):
    me = lax.axis_index("tm")
    groups = z.groups
    weighted_ref[...] = table(z, tab_ref, "weight").astype(jnp.float32)[: z.band_rows] * inv_ref[...]
    before = jnp.maximum(me - 1, 0)
    mine = before * z.hist
    place = lax.broadcasted_iota(jnp.int32, (CHUNK, LANES), 0)

    def edges_of(i):
        value = edges_ref[pl.ds(pl.multiple_of(i * CHUNK, CHUNK), CHUNK)]
        if first == 0:
            inside = jnp.logical_and(jnp.logical_and(me > 0, i == 0), place < z.hist)
            value = jnp.where(inside, sides_ref[before], value)
        return value

    def power_of(i, k):
        value = power_ref[i * CHUNK + k]
        if first == 0 and k < z.hist:
            value = jnp.where(jnp.logical_and(me > 0, i == 0), bound_ref[mine + k], value)
        return value

    def means(i):
        for k in range(CHUNK):
            value = power_of(i, k) * weighted_ref[: z.rows]
            sums_ref[k * 8 : k * 8 + 8] = jnp.sum(value.reshape(z.rows // 8, 8, LANES), 0)
        acc = edges_of(i) * weighted_ref[z.rows : z.rows + 1]
        for j in range(8):
            acc = acc + sums_ref[pl.ds(j, CHUNK, stride=8)]
        at = pl.multiple_of(i * CHUNK, CHUNK)
        mean_ref[pl.ds(at, CHUNK)] = jnp.broadcast_to(jnp.sum(acc, 1, keepdims=True), (CHUNK, LANES))

    parities = z.channels // NBLK // DFT_A
    lane = lax.broadcasted_iota(jnp.int32, (groups, LANES), 1)

    def picked(m, step, value):
        row = (m * FD + step) * parities * groups
        part = value[row : row + groups]
        for parity in range(1, parities):
            hit = (lane if m == 0 else LANES - 1 - lane) % parities == parity
            part = jnp.where(hit, value[row + parity * groups : row + (parity + 1) * groups], part)
        return part

    def flat_step(i, carry):
        flats = []
        at = pl.multiple_of(i * CHUNK, CHUNK)
        edges = edges_of(i) * inv_ref[z.rows : z.rows + 1] - mean_ref[pl.ds(at, CHUNK)]
        open_sums = [list(carry[m]) for m in range(2)]
        for k in range(CHUNK):
            flat = power_of(i, k) * inv_ref[: z.rows] - mean_ref[pl.ds(i * CHUNK + k, 1)]
            edge = jnp.where(place == k, edges, 0.0)
            flats.append(jnp.concatenate([flat, edge]).astype(jnp.bfloat16))
            if k % 2 == 0:
                continue
            masks = table(z, tab_ref, "masks")[:, : z.deep]
            found = jnp.dot(masks, jnp.concatenate(flats[-2:], 1), preferred_element_type=jnp.float32)
            for half in range(2):
                value = found[:, half * LANES : (half + 1) * LANES]
                at = pl.multiple_of(((i - first) * CHUNK + k - 1 + half) * groups, 8)
                for m in range(2):
                    parts = [picked(m, step, value) for step in range(FD)]
                    sub_ref[m, pl.ds(at, groups)] = open_sums[m][0] + parts[0]
                    later = open_sums[m][1:] + [None]
                    open_sums[m] = [
                        parts[step + 1] if later[step] is None else later[step] + parts[step + 1]
                        for step in range(FD - 1)
                    ]
        means(jnp.minimum(i + 1, last - 1))
        return tuple(tuple(value) for value in open_sums)

    means(first)
    empty = jnp.zeros((groups, LANES), jnp.float32)
    return lax.fori_loop(first, last, flat_step, ((empty,) * (FD - 1),) * 2)


def delayed(z, hits, series):
    lane = lax.broadcasted_iota(jnp.int32, (8, LANES), 1)
    found = lax.dot_general(hits, series, (((1,), (1,)), ((), ())), preferred_element_type=jnp.float32)
    total = found[:8]
    for value in range(1, MAXT + 1):
        moved = pltpu.roll(found[value * 8 : value * 8 + 8], value * TT, 1)
        total = total + jnp.where(lane >= value * TT, moved, 0.0)
    return total


def tails(z, power_ref, edges_ref, pr_ref, band_ref, own_ref, other_ref, tab_ref, hits_ref,
          prev_ref, high_ref, bound_ref, sides_ref, inv_ref, y_ref, t_ref, e_ref, late_ref, weighted_ref, sums_ref, mean_ref):
    groups = z.groups
    boundary(z, pr_ref, band_ref, own_ref, other_ref, tab_ref, y_ref, t_ref, e_ref, bound_ref, sides_ref, inv_ref)
    carry = subbands(
        z, z.low_chunks, z.spec // CHUNK, power_ref, edges_ref, bound_ref, sides_ref, inv_ref, tab_ref,
        weighted_ref, sums_ref, mean_ref, high_ref,
    )
    count = z.high_rows
    done = z.spec - z.low_chunks * CHUNK
    for m in range(2):
        for step in range(FD - 1):
            high_ref[m, (done + step) * groups : (done + step + 1) * groups] = carry[m][step]
    high_ref[:, (done + FD - 1) * groups :] = jnp.zeros((2, (count - done - FD + 1) * groups, LANES), jnp.float32)
    blank = jnp.zeros((LANES - count, 2 * LANES), jnp.bfloat16)
    trials = late_ref.shape[1]
    lane = lax.broadcasted_iota(jnp.int32, (8, LANES), 1)
    start = done - (WMAX - 1)
    for g in range(groups):
        both = [high_ref[m, pl.ds(g, count, stride=groups)].astype(jnp.bfloat16) for m in range(2)]
        dd = delayed(z, hits_ref[g], jnp.concatenate([jnp.concatenate(both, 1), blank]))
        late = pltpu.roll(dd, LANES - start, 1)
        late_ref[g] = jnp.where(lane < WMAX - 1 + MAXT * TT + FD - 1, late, 0.0)[:trials]
    prev_ref[...] = late_ref[...].reshape(groups * trials, LANES).astype(jnp.bfloat16)


def bulk(z, power_ref, edges_ref, bound_ref, sides_ref, inv_ref, tab_ref, hits_ref, high_ref,
         main_ref, weighted_ref, sums_ref, mean_ref, low_ref, join_ref):
    groups = z.groups
    carry = subbands(
        z, 0, z.low_chunks, power_ref, edges_ref, bound_ref, sides_ref, inv_ref, tab_ref,
        weighted_ref, sums_ref, mean_ref, low_ref,
    )
    join_ref[...] = jnp.zeros_like(join_ref)
    for m in range(2):
        for step in range(FD - 1):
            join_ref[m, step * groups : (step + 1) * groups] = carry[m][step]
    low = z.low_chunks * CHUNK
    trials = main_ref.shape[1]
    for g in range(groups):
        both = []
        for m in range(2):
            edge = high_ref[m, pl.ds(g, 8, stride=groups)] + join_ref[m, pl.ds(g, 8, stride=groups)]
            rest = high_ref[m, pl.ds(8 * groups + g, z.spec - low - 8, stride=groups)]
            both.append(jnp.concatenate([low_ref[m, pl.ds(g, low, stride=groups)], edge, rest]).astype(jnp.bfloat16))
        main_ref[g] = delayed(z, hits_ref[g], jnp.concatenate(both, 1))[:trials]


def parcels(z, main_ref, prev_ref, owners_ref, stay_ref, leave_ref, late_ref, all_ref):
    me = lax.axis_index("dm")
    all_ref[...] = jnp.zeros_like(all_ref)
    late_ref[...] = prev_ref[...].astype(jnp.float32).reshape(late_ref.shape)
    for g in range(z.groups):
        owner = owners_ref[g]
        rank = jnp.int32(0)
        for earlier in range(g):
            rank = rank + jnp.where(owners_ref[earlier] == owner, 1, 0)
        all_ref[owner ^ me, 0, rank] = main_ref[g]
        all_ref[owner ^ me, 1, rank] = late_ref[g]
    for r in range(z.n_dm):
        value = all_ref[r].reshape(stay_ref.shape[2:]).astype(jnp.bfloat16)
        (leave_ref if r % 2 else stay_ref)[r // 2, 0] = value


def relay(held_ref, got_ref, stay_ref, leave_ref):
    count = held_ref.shape[1]
    for r in range(held_ref.shape[0]):
        target = leave_ref if r % 2 else stay_ref
        target[r // 2, :count] = held_ref[r]
        target[r // 2, count:] = got_ref[r]


def boxes(z, widths_ref, *refs):
    held_ref, got_ref, out_ref, d_ref = refs
    early = lax.axis_index("tm") == 0
    me = lax.axis_index("dm")
    trials = out_ref.shape[3]
    near = held_ref.shape[1]
    rank = lax.broadcasted_iota(jnp.int32, (8, LANES), 0)
    count = widths_ref.shape[0]
    width = jnp.zeros((8, LANES), jnp.int32)
    for w in range(count):
        width = jnp.where(rank == w, widths_ref[w], width)
    norm = 1.0 / jnp.sqrt(width.astype(jnp.float32))
    weights = [jnp.where(width > lag, norm, 0.0) for lag in range(WMAX)]
    prior = WMAX - 1
    rows = z.capacity * trials
    for r in range(z.n_dm):
        ref, at = (held_ref, r) if r < near else (got_ref, r - near)
        own = ref[0, at, :rows].astype(jnp.float32)
        past = jnp.where(early, 0.0, ref[0, at, rows:].astype(jnp.float32))
        wide = jnp.concatenate([own, jnp.zeros_like(own)], 1)
        wide = pltpu.roll(wide, prior, 1) + jnp.concatenate([past, jnp.zeros_like(past)], 1)
        for lag in range(WMAX):
            shift = prior - lag
            d_ref[r, lag] = (pltpu.roll(wide, 2 * LANES - shift, 1) if shift else wide)[:, :LANES]
        for s in range(z.capacity):
            for j in range(trials):
                acc = None
                for lag in range(WMAX):
                    part = d_ref[r, lag, s * trials + j : s * trials + j + 1, :] * weights[lag]
                    acc = part if acc is None else acc + part
                out_ref[s, me ^ r, 0, j] = acc[:count].astype(jnp.bfloat16)


def vmem_spec():
    return pl.BlockSpec(memory_space=pltpu.VMEM)


def smem_spec():
    return pl.BlockSpec(memory_space=pltpu.SMEM)


def hbm_spec():
    return pl.BlockSpec(memory_space=pltpu.HBM)


def kept(*values, space=pltpu.VMEM):
    return [pltpu.with_memory_space_constraint(value, space) for value in values]


def shards(n_dm, n_tm, raw, proto, delays, widths, owners):
    taps, channels = proto.shape
    groups, trials, _ = delays.shape
    z = Sizes(taps, channels, raw.shape[1] // channels, groups, n_dm, n_tm)
    tables, z.places = constants(z)
    params = pltpu.CompilerParams(vmem_limit_bytes=LIMIT)
    own_rows = z.raw_rows * (1 if n_tm == 2 else 2) + z.deep
    f32, bf16 = jnp.float32, jnp.bfloat16
    half = CHUNK // 2 * z.rows
    power, edges, pr, band, msg, tables, trial, owner, width = pl.pallas_call(
        functools.partial(channelize, z),
        out_shape=(
            pltpu.VMEM((z.spec, z.rows, LANES), f32),
            pltpu.VMEM((z.spec, LANES), f32),
            pltpu.VMEM((taps, 1, channels), f32),
            pltpu.VMEM((z.band_rows, LANES), f32),
            pltpu.VMEM((own_rows, LANES), bf16),
            pltpu.VMEM(tables.shape, bf16),
            pltpu.VMEM(delays.shape, jnp.int32),
            pltpu.SMEM((groups,), jnp.int32),
            pltpu.SMEM(widths.shape, jnp.int32),
        ),
        in_specs=[hbm_spec()] * 6,
        out_specs=[vmem_spec()] * 7 + [smem_spec()] * 2,
        scratch_shapes=[
            pltpu.VMEM((1, z.spec * channels), bf16),
            pltpu.VMEM((z.hist, DFT_A, LANES), f32),
            pltpu.VMEM((DFT_A, CHUNK * LANES), bf16),
            pltpu.VMEM((DFT_A, CHUNK * LANES), bf16),
            pltpu.VMEM((half, 2 * LANES), bf16),
            pltpu.VMEM((half + 16, 2 * LANES), bf16),
            pltpu.VMEM((half, 2 * LANES), bf16),
            pltpu.VMEM((half + 16, 2 * LANES), bf16),
            pltpu.VMEM((16, LANES), f32),
            pltpu.VMEM((16, LANES), f32),
            pltpu.VMEM((16, LANES), f32),
            pltpu.SemaphoreType.DMA((5,)),
        ],
        compiler_params=params,
        name="channelize",
    )(
        *kept(raw, proto, tables, delays, owners.reshape(groups), widths, space=pltpu.HBM)
    )
    if n_tm == 2:
        own, other = msg, lax.ppermute(msg, "tm", [(0, 1), (1, 0)])
    else:
        every = lax.all_gather(msg, "tm")
        lasts = every[:-1, : z.raw_rows].reshape(-1, LANES)
        firsts = every[1:, z.raw_rows : 2 * z.raw_rows].reshape(-1, LANES)
        rest = lax.psum(band, "tm") - band
        rest = jnp.concatenate([rest, jnp.zeros((z.deep - z.band_rows, LANES), f32)]).astype(bf16)
        own, other = jnp.concatenate([lasts, rest]), jnp.concatenate([firsts, rest])
    hits = pl.pallas_call(
        functools.partial(coarse, z),
        out_shape=pltpu.VMEM((groups, (MAXT + 1) * 8, 2 * LANES), bf16),
        in_specs=[vmem_spec()] * 2,
        out_specs=vmem_spec(),
        compiler_params=params,
        name="coarse",
    )(*kept(tables, trial))
    work = [
        pltpu.VMEM((z.band_rows, LANES), f32),
        pltpu.VMEM((CHUNK * 8, LANES), f32),
        pltpu.VMEM((z.spec, LANES), f32),
    ]
    prev, high, bound, sides, inv = pl.pallas_call(
        functools.partial(tails, z),
        out_shape=(
            pltpu.VMEM((groups * trials, LANES), bf16),
            pltpu.VMEM((2, z.high_rows * groups, LANES), f32),
            pltpu.VMEM((z.bounds * z.hist, z.rows, LANES), f32),
            pltpu.VMEM((z.bounds, 16, LANES), f32),
            pltpu.VMEM((z.band_rows, LANES), f32),
        ),
        in_specs=[vmem_spec()] * 8,
        out_specs=[vmem_spec()] * 5,
        scratch_shapes=[
            pltpu.VMEM((DFT_A, (z.hist + 1) * LANES), bf16),
            pltpu.VMEM((z.hist * z.rows + 16, 2 * LANES), bf16),
            pltpu.VMEM((16, LANES), f32),
            pltpu.VMEM((groups, trials, LANES), f32),
        ]
        + work,
        compiler_params=params,
        name="tails",
    )(*kept(power, edges, pr, band, own, other, tables, hits))
    before = lax.ppermute(prev, "tm", [(i, (i + 1) % n_tm) for i in range(n_tm)])
    main = pl.pallas_call(
        functools.partial(bulk, z),
        out_shape=pltpu.VMEM((groups, trials, LANES), f32),
        in_specs=[vmem_spec()] * 8,
        out_specs=vmem_spec(),
        scratch_shapes=work
        + [
            pltpu.VMEM((2, z.low_chunks * CHUNK * groups, LANES), f32),
            pltpu.VMEM((2, 8 * groups, LANES), f32),
        ],
        compiler_params=params,
        cost_estimate=pl.CostEstimate(flops=10**9, bytes_accessed=8 * 10**6, transcendentals=0),
        name="bulk",
    )(*kept(power, edges, bound, sides, inv, tables, hits, high))
    slots = (2, z.capacity, trials, LANES)
    parcel = (2 * z.capacity * trials, LANES)
    held, leaving = pl.pallas_call(
        functools.partial(parcels, z),
        out_shape=(pltpu.VMEM((n_dm // 2, 1, *parcel), bf16),) * 2,
        in_specs=[vmem_spec()] * 2 + [smem_spec()],
        out_specs=[vmem_spec()] * 2,
        scratch_shapes=[pltpu.VMEM((groups, trials, LANES), f32), pltpu.VMEM((n_dm, *slots), f32)],
        compiler_params=params,
        name="parcels",
    )(*kept(main, before), *kept(owner, space=pltpu.SMEM))
    bit = 1
    while True:
        got = lax.ppermute(leaving, "dm", [(i, i ^ bit) for i in range(n_dm)])
        bit *= 2
        if bit == n_dm:
            break
        held, leaving = pl.pallas_call(
            relay,
            out_shape=(pltpu.VMEM((n_dm // 2 // bit, bit, *parcel), bf16),) * 2,
            in_specs=[vmem_spec()] * 2,
            out_specs=[vmem_spec()] * 2,
            compiler_params=params,
            name="relay",
        )(*kept(held, got))
    return pl.pallas_call(
        functools.partial(boxes, z),
        out_shape=jax.ShapeDtypeStruct((z.capacity, n_dm, 1, trials, widths.shape[0], z.spec), bf16),
        in_specs=[smem_spec()] + [vmem_spec()] * 2,
        out_specs=vmem_spec(),
        scratch_shapes=[pltpu.VMEM((n_dm, WMAX, z.capacity * trials, LANES), f32)],
        compiler_params=params,
        name="boxes",
    )(*kept(width, space=pltpu.SMEM), *kept(held, got))


def solution(mesh):
    sizes = dict(mesh.shape)
    return jax.shard_map(
        functools.partial(shards, sizes["dm"], sizes["tm"]),
        mesh=mesh,
        in_specs=(P(("group", "dm", "beam"), "tm"), P(), P(), P(), P()),
        out_specs=P("dm", "group", "beam", None, None, "tm"),
        check_vma=False,
    )
```

```python
import functools
import math

import jax
import jax.numpy as jnp
import numpy as np
from jax import lax
from jax.experimental import pallas as pl
from jax.experimental.pallas import tpu as pltpu
from jax.sharding import PartitionSpec as P

DFT_A = 128
NBLK = 64
FD = 4
TT = 8
MAXT = 3
WMAX = 8
LANES = 128
CHUNK = 16
LIMIT = 32 * 1024 * 1024


def ceil_to(value, unit):
    return -(-value // unit) * unit


def angle_tables(rows, cols, total):
    product = np.arange(rows)[:, None] * np.arange(cols)[None, :] % total
    angle = product.astype(np.float64) * (2.0 * math.pi / total)
    return np.cos(angle), np.sin(angle)


class Sizes:
    def __init__(self, taps, channels, spec, groups, n_dm, n_tm):
        self.taps, self.channels, self.spec, self.groups = taps, channels, spec, groups
        self.n_dm, self.n_tm = n_dm, n_tm
        self.side = channels // DFT_A
        self.rows = DFT_A // 2
        self.deep = self.rows + 16
        self.band_rows = self.rows + 8
        self.hist = taps - 1
        self.raw_rows = self.hist * DFT_A
        self.bounds = n_tm - 1
        self.capacity = 2 * (groups // n_dm)
        self.low_chunks = (spec - (WMAX - 1) - MAXT * TT - (FD - 1)) // CHUNK
        self.high_rows = ceil_to(spec + FD - 1 - self.low_chunks * CHUNK, 16)


def constants(z):
    cos_a, sin_a = angle_tables(DFT_A, DFT_A, DFT_A)
    first = np.concatenate([cos_a[: z.rows], -sin_a[: z.rows]])
    first[z.rows] = cos_a[z.rows]
    tw_cos, tw_sin = angle_tables(z.rows + 1, z.side, z.channels)
    edge = np.zeros((16, z.side))
    edge[0], edge[1] = tw_cos[z.rows], -tw_sin[z.rows]
    tw_cos, tw_sin = tw_cos[: z.rows], tw_sin[: z.rows]
    hidden = tw_cos.copy()
    hidden[0] = 0
    cos_b, sin_b = angle_tables(z.side, z.side, z.side)
    width = z.channels // NBLK
    fine = np.arange(z.groups)[:, None] * FD * (width - 1 - np.arange(width))[None, :] // (z.groups * (width - 1))
    parities = width // DFT_A
    masks = np.zeros((2, FD, parities, z.groups, LANES))
    for step in range(FD):
        for parity in range(parities):
            hit = fine[:, parity * DFT_A : (parity + 1) * DFT_A] == step
            masks[0, step, parity, :, : z.rows] = hit[:, : z.rows]
            masks[0, step, parity, :, z.rows : z.deep] = hit[:, z.rows, None]
            masks[1, step, parity, :, 1 : z.rows] = hit[:, : z.rows : -1]
    weight = np.full((z.deep, LANES), 2.0 / z.channels)
    weight[0] = weight[z.rows] = 1.0 / z.channels
    expand = np.zeros((NBLK, 2 * z.side))
    lane = np.arange(z.side)
    expand[lane // parities, lane] = 1
    expand[(z.side - 1 - lane) // parities, z.side + lane] = 1
    tables = {
        "first": first,
        "cos": tw_cos,
        "hidden": hidden,
        "edge": edge,
        "sin": tw_sin,
        "second": np.concatenate([cos_b, sin_b]),
        "second_im": np.concatenate([-sin_b, cos_b]),
        "masks": masks,
        "weight": weight,
        "expand": expand[:, : z.side],
        "expand_im": expand[:, z.side :],
    }
    kept_masks, z.mask_rows = [], {}
    for key in np.ndindex(masks.shape[:3]):
        if masks[key].any():
            z.mask_rows[key] = len(kept_masks) * z.groups
            kept_masks.append(masks[key])
    tables["masks"] = np.concatenate(kept_masks)
    places, row = {}, 0
    for name, table in tables.items():
        places[name] = (row, row + table.shape[0])
        row += table.shape[0]
    return jnp.asarray(np.concatenate(list(tables.values())), jnp.bfloat16), places


def table(z, ref, name):
    first, last = z.places[name]
    return ref[first:last]


def wide_table(z, ref, name):
    return jnp.concatenate([table(z, ref, name), table(z, ref, name + "_im")], 1)


def fill_frames(z, history, load, pr_ref, y_ref, count, save=None):
    for block in range(DFT_A // 16):
        rows = pl.ds(block * 16, 16)
        taps = [
            jnp.concatenate(
                [
                    pr_ref[tap, :, (2 * block + part) * 8 * LANES : (2 * block + part + 1) * 8 * LANES].reshape(8, LANES)
                    for part in range(2)
                ]
            )
            for tap in range(z.taps)
        ]
        window = [history(k, block) for k in range(z.hist)]
        for k in range(count):
            window.append(load(k, block))
            acc = window[0] * taps[0]
            for tap in range(1, z.taps):
                acc = acc + window[tap] * taps[tap]
            y_ref[rows, k * LANES : (k + 1) * LANES] = acc.astype(jnp.bfloat16)
            window.pop(0)
        if save is not None:
            for k in range(z.hist):
                save(k, block, window[k])


def transform(z, y_ref, tab_ref, t_refs, edge_ref, count):
    cos, hidden, sin = (table(z, tab_ref, name) for name in ("cos", "hidden", "sin"))
    part = count // len(t_refs)
    out = []
    for index, t_ref in enumerate(t_refs):
        for at in range(0, part, 2):
            pair = min(2, part - at)
            lane = (index * part + at) * LANES
            a = jnp.dot(
                table(z, tab_ref, "first"), y_ref[:, lane : lane + pair * LANES], preferred_element_type=jnp.float32
            )
            for k in range(pair):
                lanes = slice(k * LANES, (k + 1) * LANES)
                edge_ref[index * part + at + k : index * part + at + k + 1] = a[z.rows : z.rows + 1, lanes]
                re, im = a[: z.rows, lanes].astype(jnp.bfloat16), a[z.rows :, lanes].astype(jnp.bfloat16)
                rows = slice((at + k) * z.rows, (at + k + 1) * z.rows)
                t_ref[rows, :LANES] = re * cos + im * sin
                t_ref[rows, LANES:] = im * hidden - re * sin
        last = index + 1 == len(t_refs)
        if last:
            turn = table(z, tab_ref, "edge").astype(jnp.float32)
            rows = slice(part * z.rows, part * z.rows + 16)
            t_ref[rows, :LANES] = (edge_ref[...] * turn[0:1]).astype(jnp.bfloat16)
            t_ref[rows, LANES:] = (edge_ref[...] * turn[1:2]).astype(jnp.bfloat16)
        c = jnp.dot(
            t_ref[: part * z.rows + (16 if last else 0)], wide_table(z, tab_ref, "second"),
            preferred_element_type=jnp.float32,
        )
        for k in range(part):
            rows = c[k * z.rows : (k + 1) * z.rows]
            re, im = rows[:, :LANES], rows[:, LANES:]
            out.append(re * re + im * im)
    re, im = c[part * z.rows :, :LANES], c[part * z.rows :, LANES:]
    return out, re * re + im * im


def channelize(z, raw_ref, proto_ref, tab_in, delays_ref, owners_in, widths_in,
               power_ref, edges_ref, pr_ref, band_ref, msg_ref, tab_ref, trial_ref, owners_ref, widths_ref,
               buf, hist_ref, y0_ref, y1_ref, t0_ref, t1_ref, t2_ref, t3_ref, e0_ref, e1_ref, sum_ref, sems):
    chunks = z.spec // CHUNK
    span = CHUNK * z.channels

    def raw_copy(first, last, side):
        part = pl.ds(first * span, (last - first) * span)
        return pltpu.make_async_copy(raw_ref.at[:, part], buf.at[:, part], sems.at[side])

    tab_copy = pltpu.make_async_copy(tab_in, tab_ref, sems.at[2])
    delays_copy = pltpu.make_async_copy(delays_ref, trial_ref, sems.at[1])
    owners_copy = pltpu.make_async_copy(owners_in, owners_ref, sems.at[3])
    widths_copy = pltpu.make_async_copy(widths_in, widths_ref, sems.at[2])
    early_copies = [raw_copy(0, 1, 0), raw_copy(1, 3, 1), raw_copy(3, 5, 2), raw_copy(5, chunks, 0)]
    early_copies[0].start()
    for tap in range(z.taps):
        pltpu.make_async_copy(proto_ref.at[tap : tap + 1], pr_ref.at[tap], sems.at[3]).start()
    tab_copy.start()
    early_copies[1].start()
    hist_ref[...] = jnp.zeros_like(hist_ref)
    band_ref[...] = jnp.zeros_like(band_ref)
    sum_ref[...] = jnp.zeros_like(sum_ref)
    early = lax.axis_index("tm") > 0
    place = lax.broadcasted_iota(jnp.int32, (16, LANES), 0)

    def frames(i, y_ref):
        base = i * span

        def load(k, block):
            parts = []
            for part in range(2):
                start = pl.multiple_of(base + k * z.channels + (2 * block + part) * 8 * LANES, 8 * LANES)
                parts.append(buf[:, pl.ds(start, 8 * LANES)].astype(jnp.float32).reshape(8, LANES))
            return jnp.concatenate(parts)

        def history(k, block):
            return hist_ref[k, block * 16 : block * 16 + 16, :]

        def save(k, block, value):
            hist_ref[k, block * 16 : block * 16 + 16, :] = value

        fill_frames(z, history, load, pr_ref, y_ref, CHUNK, save)

    def powers(i, y_ref, t_refs, e_ref):
        power, edges = transform(z, y_ref, tab_ref, t_refs, e_ref, CHUNK)
        late = power[z.hist]
        for k in range(z.hist + 1, CHUNK):
            late = late + power[k]
        head = power[0]
        for k in range(1, z.hist):
            head = head + power[k]
        skip = jnp.logical_and(i == 0, early)
        band_ref[: z.rows] = band_ref[: z.rows] + late + jnp.where(skip, 0.0, head)
        sum_ref[...] = sum_ref[...] + jnp.where(jnp.logical_and(skip, place < z.hist), 0.0, edges)
        edges_ref[pl.ds(pl.multiple_of(i * CHUNK, CHUNK), CHUNK)] = edges
        for k in range(CHUNK):
            power_ref[i * CHUNK + k] = power[k]

    pltpu.make_async_copy(pr_ref, pr_ref, sems.at[3]).wait()
    owners_copy.start()
    early_copies[0].wait()
    tab_copy.wait()
    early_copies[2].start()
    frames(0, y0_ref)
    early_copies[3].start()

    def step(j, carry):
        i = 2 * j
        for turn in range(3):

            @pl.when(j == turn)
            def _(turn=turn):
                early_copies[turn + 1].wait()
                if turn < 2:
                    (delays_copy, widths_copy)[turn].start()

        frames(i + 1, y1_ref)
        powers(i, y0_ref, [t0_ref, t1_ref], e0_ref)
        frames(i + 2, y0_ref)
        powers(i + 1, y1_ref, [t2_ref, t3_ref], e1_ref)
        return carry

    lax.fori_loop(0, chunks // 2 - 1, step, 0)
    owners_copy.wait()
    delays_copy.wait()
    frames(chunks - 1, y1_ref)
    powers(chunks - 2, y0_ref, [t0_ref, t1_ref], e0_ref)
    powers(chunks - 1, y1_ref, [t2_ref, t3_ref], e1_ref)
    def spectrum(start):
        start = pl.multiple_of(start, z.channels)
        return buf[:, pl.ds(start, z.channels)].astype(jnp.float32).reshape(DFT_A, LANES).astype(jnp.bfloat16)

    row = 0
    tail = (z.spec - z.hist) * z.channels
    starts = [jnp.where(early, 0, tail)] if z.n_tm == 2 else [tail, 0]
    for start in starts:
        for k in range(z.hist):
            msg_ref[row : row + DFT_A] = spectrum(start + k * z.channels)
            row += DFT_A
    total = jnp.sum(sum_ref[...], 0, keepdims=True)
    rest = jnp.concatenate([total, jnp.zeros((15, LANES), jnp.float32)])
    band_ref[z.rows :] = rest[: z.band_rows - z.rows]
    msg_ref[row : row + z.deep] = jnp.concatenate([band_ref[: z.rows], rest]).astype(jnp.bfloat16)
    widths_copy.wait()


def coarse(z, tab_ref, trial_ref, hits_ref):
    unit = 1.0 / (math.sqrt(z.channels // NBLK) * math.sqrt(NBLK))
    trials = trial_ref.shape[1]
    tall = jnp.concatenate(
        [
            jnp.concatenate([trial_ref[g].astype(jnp.float32), jnp.zeros((8 - trials, NBLK), jnp.float32)])
            for g in range(z.groups)
        ]
    )
    spread = jnp.dot(
        tall.astype(jnp.bfloat16), wide_table(z, tab_ref, "expand"), preferred_element_type=jnp.float32
    )
    for g in range(z.groups):
        mine = spread[g * 8 : g * 8 + 8]
        hits = jnp.concatenate([jnp.where(mine == value, unit, 0.0) for value in range(MAXT + 1)])
        hits_ref[g] = hits.astype(jnp.bfloat16)


def boundary(z, pr_ref, band_ref, own_ref, other_ref, tab_ref, y_ref, t_ref, e_ref, bound_ref, sides_ref, inv_ref):
    me = lax.axis_index("tm")
    lo = z.bounds * z.raw_rows
    rest = other_ref[lo : lo + z.deep].astype(jnp.float32)
    total = band_ref[: z.rows] + rest[: z.rows]
    edge = band_ref[z.rows :] + rest[z.rows : z.band_rows]
    e_ref[...] = jnp.zeros_like(e_ref)
    swap = jnp.logical_and(me > 0, z.n_tm == 2)
    y_ref[:, z.hist * LANES :] = jnp.zeros((DFT_A, LANES), jnp.bfloat16)
    for b in range(z.bounds):

        def take(k, block, first, b=b):
            start = b * z.raw_rows + k * DFT_A + block * 16
            own = own_ref[start : start + 16].astype(jnp.float32)
            other = other_ref[start : start + 16].astype(jnp.float32)
            return jnp.where(swap, other, own) if first else jnp.where(swap, own, other)

        fill_frames(
            z, lambda k, block: take(k, block, True), lambda k, block: take(k, block, False), pr_ref, y_ref, z.hist
        )
        power, edges = transform(z, y_ref, tab_ref, [t_ref], e_ref, z.hist)
        sides_ref[b] = edges
        edge = edge + jnp.sum(edges, 0, keepdims=True)
        for k in range(z.hist):
            total = total + power[k]
            bound_ref[b * z.hist + k] = power[k]
    scale = float(z.taps * z.channels)
    total = jnp.concatenate([total, edge])
    inv_ref[...] = 1.0 / (total * (1.0 / (z.spec * z.n_tm)) + 1e-6 * scale)


def subbands(
    z, first, last, power_ref, edges_ref, bound_ref, sides_ref, inv_ref, tab_ref, weighted_ref, sums_ref, mean_ref, sub_ref
):
    me = lax.axis_index("tm")
    groups = z.groups
    weighted_ref[...] = table(z, tab_ref, "weight").astype(jnp.float32)[: z.band_rows] * inv_ref[...]
    before = jnp.maximum(me - 1, 0)
    mine = before * z.hist
    place = lax.broadcasted_iota(jnp.int32, (CHUNK, LANES), 0)

    def edges_of(i):
        value = edges_ref[pl.ds(pl.multiple_of(i * CHUNK, CHUNK), CHUNK)]
        if first == 0:
            inside = jnp.logical_and(jnp.logical_and(me > 0, i == 0), place < z.hist)
            value = jnp.where(inside, sides_ref[before], value)
        return value

    empty = jnp.zeros((groups, LANES), jnp.float32)

    def power_of(i, k):
        value = power_ref[i * CHUNK + k]
        if first == 0 and k < z.hist:
            value = jnp.where(jnp.logical_and(me > 0, i == 0), bound_ref[mine + k], value)
        return value

    def means(i):
        for k in range(CHUNK):
            value = power_of(i, k) * weighted_ref[: z.rows]
            sums_ref[k * 8 : k * 8 + 8] = jnp.sum(value.reshape(z.rows // 8, 8, LANES), 0)
        acc = edges_of(i) * weighted_ref[z.rows : z.rows + 1]
        for j in range(8):
            acc = acc + sums_ref[pl.ds(j, CHUNK, stride=8)]
        at = pl.multiple_of(i * CHUNK, CHUNK)
        mean_ref[pl.ds(at, CHUNK)] = jnp.broadcast_to(jnp.sum(acc, 1, keepdims=True), (CHUNK, LANES))

    parities = z.channels // NBLK // DFT_A
    lane = lax.broadcasted_iota(jnp.int32, (groups, LANES), 1)

    def picked(m, step, value):
        rows = [z.mask_rows.get((m, step, parity)) for parity in range(parities)]
        part = None if None in rows else value[rows[0] : rows[0] + groups]
        for parity, row in enumerate(rows):
            if row is not None and (part is None or parity > 0):
                hit = (lane if m == 0 else LANES - 1 - lane) % parities == parity
                part = jnp.where(hit, value[row : row + groups], 0.0 if part is None else part)
        return part

    def plus(left, right):
        return left if right is None else right if left is None else left + right

    def flat_step(i, carry):
        flats = []
        at = pl.multiple_of(i * CHUNK, CHUNK)
        edges = edges_of(i) * inv_ref[z.rows : z.rows + 1] - mean_ref[pl.ds(at, CHUNK)]
        open_sums = [list(carry[m]) for m in range(2)]
        for k in range(CHUNK):
            flat = power_of(i, k) * inv_ref[: z.rows] - mean_ref[pl.ds(i * CHUNK + k, 1)]
            edge = jnp.where(place == k, edges, 0.0)
            flats.append(jnp.concatenate([flat, edge]).astype(jnp.bfloat16))
            if k % 2 == 0:
                continue
            masks = table(z, tab_ref, "masks")[:, : z.deep]
            found = jnp.dot(masks, jnp.concatenate(flats[-2:], 1), preferred_element_type=jnp.float32)
            for half in range(2):
                value = found[:, half * LANES : (half + 1) * LANES]
                at = pl.multiple_of(((i - first) * CHUNK + k - 1 + half) * groups, 8)
                for m in range(2):
                    parts = [picked(m, step, value) for step in range(FD)]
                    sub_ref[m, pl.ds(at, groups)] = plus(open_sums[m][0], parts[0])
                    later = open_sums[m][1:] + [None]
                    open_sums[m] = [plus(later[step], parts[step + 1]) for step in range(FD - 1)]
        means(jnp.minimum(i + 1, last - 1))
        return tuple(tuple(empty if part is None else part for part in value) for value in open_sums)

    means(first)
    return lax.fori_loop(first, last, flat_step, ((empty,) * (FD - 1),) * 2)


def delayed(z, hits, series):
    lane = lax.broadcasted_iota(jnp.int32, (8, LANES), 1)
    found = lax.dot_general(hits, series, (((1,), (1,)), ((), ())), preferred_element_type=jnp.float32)
    total = found[:8]
    for value in range(1, MAXT + 1):
        moved = pltpu.roll(found[value * 8 : value * 8 + 8], value * TT, 1)
        total = total + jnp.where(lane >= value * TT, moved, 0.0)
    return total


def tails(z, power_ref, edges_ref, pr_ref, band_ref, own_ref, other_ref, tab_ref, hits_ref,
          prev_ref, high_ref, bound_ref, sides_ref, inv_ref, y_ref, t_ref, e_ref, late_ref, weighted_ref, sums_ref, mean_ref):
    groups = z.groups
    boundary(z, pr_ref, band_ref, own_ref, other_ref, tab_ref, y_ref, t_ref, e_ref, bound_ref, sides_ref, inv_ref)
    carry = subbands(
        z, z.low_chunks, z.spec // CHUNK, power_ref, edges_ref, bound_ref, sides_ref, inv_ref, tab_ref,
        weighted_ref, sums_ref, mean_ref, high_ref,
    )
    count = z.high_rows
    done = z.spec - z.low_chunks * CHUNK
    for m in range(2):
        for step in range(FD - 1):
            high_ref[m, (done + step) * groups : (done + step + 1) * groups] = carry[m][step]
    high_ref[:, (done + FD - 1) * groups :] = jnp.zeros((2, (count + 1 - done - FD + 1) * groups, LANES), jnp.float32)
    blank = jnp.zeros((LANES - count, 2 * LANES), jnp.bfloat16)
    trials = late_ref.shape[1]
    lane = lax.broadcasted_iota(jnp.int32, (8, LANES), 1)
    start = done - (WMAX - 1)
    for g in range(groups):
        both = [high_ref[m, pl.ds(g, count, stride=groups)].astype(jnp.bfloat16) for m in range(2)]
        dd = delayed(z, hits_ref[g], jnp.concatenate([jnp.concatenate(both, 1), blank]))
        late = pltpu.roll(dd, LANES - start, 1)
        late_ref[g] = jnp.where(lane < WMAX - 1 + MAXT * TT + FD - 1, late, 0.0)[:trials]
    prev_ref[...] = late_ref[...].reshape(groups * trials, LANES).astype(jnp.bfloat16)


def bulk(z, power_ref, edges_ref, bound_ref, sides_ref, inv_ref, tab_ref, hits_ref, high_ref,
         main_ref, weighted_ref, sums_ref, mean_ref, low_ref, join_ref):
    groups = z.groups
    carry = subbands(
        z, 0, z.low_chunks, power_ref, edges_ref, bound_ref, sides_ref, inv_ref, tab_ref,
        weighted_ref, sums_ref, mean_ref, low_ref,
    )
    join_ref[...] = jnp.zeros_like(join_ref)
    for m in range(2):
        for step in range(FD - 1):
            join_ref[m, step * groups : (step + 1) * groups] = carry[m][step]
    low = z.low_chunks * CHUNK
    trials = main_ref.shape[1]
    for g in range(groups):
        both = []
        for m in range(2):
            edge = high_ref[m, pl.ds(g, 8, stride=groups)] + join_ref[m, pl.ds(g, 8, stride=groups)]
            rest = high_ref[m, pl.ds(8 * groups + g, z.spec - low - 8, stride=groups)]
            both.append(jnp.concatenate([low_ref[m, pl.ds(g, low, stride=groups)], edge, rest]).astype(jnp.bfloat16))
        main_ref[g] = delayed(z, hits_ref[g], jnp.concatenate(both, 1))[:trials]


def parcels(z, main_ref, prev_ref, owners_ref, stay_ref, leave_ref, late_ref, all_ref):
    me = lax.axis_index("dm")
    all_ref[...] = jnp.zeros_like(all_ref)
    late_ref[...] = prev_ref[...].astype(jnp.float32).reshape(late_ref.shape)
    for g in range(z.groups):
        owner = owners_ref[g]
        rank = jnp.int32(0)
        for earlier in range(g):
            rank = rank + jnp.where(owners_ref[earlier] == owner, 1, 0)
        all_ref[owner ^ me, 0, rank] = main_ref[g]
        all_ref[owner ^ me, 1, rank] = late_ref[g]
    for r in range(z.n_dm):
        value = all_ref[r].reshape(stay_ref.shape[2:]).astype(jnp.bfloat16)
        (leave_ref if r % 2 else stay_ref)[r // 2, 0] = value


def relay(held_ref, got_ref, stay_ref, leave_ref):
    count = held_ref.shape[1]
    for r in range(held_ref.shape[0]):
        target = leave_ref if r % 2 else stay_ref
        target[r // 2, :count] = held_ref[r]
        target[r // 2, count:] = got_ref[r]


def boxes(z, widths_ref, *refs):
    held_ref, got_ref, out_ref, d_ref = refs
    early = lax.axis_index("tm") == 0
    me = lax.axis_index("dm")
    trials = out_ref.shape[3]
    near = held_ref.shape[1]
    rank = lax.broadcasted_iota(jnp.int32, (8, LANES), 0)
    count = widths_ref.shape[0]
    width = jnp.zeros((8, LANES), jnp.int32)
    for w in range(count):
        width = jnp.where(rank == w, widths_ref[w], width)
    norm = 1.0 / jnp.sqrt(width.astype(jnp.float32))
    weights = [jnp.where(width > lag, norm, 0.0) for lag in range(WMAX)]
    prior = WMAX - 1
    rows = z.capacity * trials
    for r in range(z.n_dm):
        ref, at = (held_ref, r) if r < near else (got_ref, r - near)
        own = ref[0, at, :rows].astype(jnp.float32)
        past = jnp.where(early, 0.0, ref[0, at, rows:].astype(jnp.float32))
        wide = jnp.concatenate([own, jnp.zeros_like(own)], 1)
        wide = pltpu.roll(wide, prior, 1) + jnp.concatenate([past, jnp.zeros_like(past)], 1)
        for lag in range(WMAX):
            shift = prior - lag
            d_ref[r, lag] = (pltpu.roll(wide, 2 * LANES - shift, 1) if shift else wide)[:, :LANES]
        for s in range(z.capacity):
            for j in range(trials):
                acc = None
                for lag in range(WMAX):
                    part = d_ref[r, lag, s * trials + j : s * trials + j + 1, :] * weights[lag]
                    acc = part if acc is None else acc + part
                out_ref[s, me ^ r, 0, j] = acc[:count].astype(jnp.bfloat16)


def vmem_spec():
    return pl.BlockSpec(memory_space=pltpu.VMEM)


def smem_spec():
    return pl.BlockSpec(memory_space=pltpu.SMEM)


def hbm_spec():
    return pl.BlockSpec(memory_space=pltpu.HBM)


def kept(*values, space=pltpu.VMEM):
    return [pltpu.with_memory_space_constraint(value, space) for value in values]


def shards(n_dm, n_tm, raw, proto, delays, widths, owners):
    taps, channels = proto.shape
    groups, trials, _ = delays.shape
    z = Sizes(taps, channels, raw.shape[1] // channels, groups, n_dm, n_tm)
    tables, z.places = constants(z)
    params = pltpu.CompilerParams(vmem_limit_bytes=LIMIT)
    own_rows = z.raw_rows * (1 if n_tm == 2 else 2) + z.deep
    f32, bf16 = jnp.float32, jnp.bfloat16
    half = CHUNK // 2 * z.rows
    power, edges, pr, band, msg, tables, trial, owner, width = pl.pallas_call(
        functools.partial(channelize, z),
        out_shape=(
            pltpu.VMEM((z.spec, z.rows, LANES), f32),
            pltpu.VMEM((z.spec, LANES), f32),
            pltpu.VMEM((taps, 1, channels), f32),
            pltpu.VMEM((z.band_rows, LANES), f32),
            pltpu.VMEM((own_rows, LANES), bf16),
            pltpu.VMEM(tables.shape, bf16),
            pltpu.VMEM(delays.shape, jnp.int32),
            pltpu.SMEM((groups,), jnp.int32),
            pltpu.SMEM(widths.shape, jnp.int32),
        ),
        in_specs=[hbm_spec()] * 6,
        out_specs=[vmem_spec()] * 7 + [smem_spec()] * 2,
        scratch_shapes=[
            pltpu.VMEM((1, z.spec * channels), bf16),
            pltpu.VMEM((z.hist, DFT_A, LANES), f32),
            pltpu.VMEM((DFT_A, CHUNK * LANES), bf16),
            pltpu.VMEM((DFT_A, CHUNK * LANES), bf16),
            pltpu.VMEM((half, 2 * LANES), bf16),
            pltpu.VMEM((half + 16, 2 * LANES), bf16),
            pltpu.VMEM((half, 2 * LANES), bf16),
            pltpu.VMEM((half + 16, 2 * LANES), bf16),
            pltpu.VMEM((16, LANES), f32),
            pltpu.VMEM((16, LANES), f32),
            pltpu.VMEM((16, LANES), f32),
            pltpu.SemaphoreType.DMA((4,)),
        ],
        compiler_params=params,
        name="channelize",
    )(
        *kept(raw, proto, tables, delays, owners.reshape(groups), widths, space=pltpu.HBM)
    )
    if n_tm == 2:
        own, other = msg, lax.ppermute(msg, "tm", [(0, 1), (1, 0)])
    else:
        every = lax.all_gather(msg, "tm")
        lasts = every[:-1, : z.raw_rows].reshape(-1, LANES)
        firsts = every[1:, z.raw_rows : 2 * z.raw_rows].reshape(-1, LANES)
        rest = lax.psum(band, "tm") - band
        rest = jnp.concatenate([rest, jnp.zeros((z.deep - z.band_rows, LANES), f32)]).astype(bf16)
        own, other = jnp.concatenate([lasts, rest]), jnp.concatenate([firsts, rest])
    hits = pl.pallas_call(
        functools.partial(coarse, z),
        out_shape=pltpu.VMEM((groups, (MAXT + 1) * 8, 2 * LANES), bf16),
        in_specs=[vmem_spec()] * 2,
        out_specs=vmem_spec(),
        compiler_params=params,
        name="coarse",
    )(*kept(tables, trial))
    work = [
        pltpu.VMEM((z.band_rows, LANES), f32),
        pltpu.VMEM((CHUNK * 8 + 8, LANES), f32),
        pltpu.VMEM((z.spec, LANES), f32),
    ]
    prev, high, bound, sides, inv = pl.pallas_call(
        functools.partial(tails, z),
        out_shape=(
            pltpu.VMEM((groups * trials, LANES), bf16),
            pltpu.VMEM((2, (z.high_rows + 1) * groups, LANES), f32),
            pltpu.VMEM((z.bounds * z.hist, z.rows, LANES), f32),
            pltpu.VMEM((z.bounds, 16, LANES), f32),
            pltpu.VMEM((z.band_rows, LANES), f32),
        ),
        in_specs=[vmem_spec()] * 8,
        out_specs=[vmem_spec()] * 5,
        scratch_shapes=[
            pltpu.VMEM((DFT_A, (z.hist + 1) * LANES), bf16),
            pltpu.VMEM((z.hist * z.rows + 16, 2 * LANES), bf16),
            pltpu.VMEM((16, LANES), f32),
            pltpu.VMEM((groups, trials, LANES), f32),
        ]
        + work,
        compiler_params=params,
        name="tails",
    )(*kept(power, edges, pr, band, own, other, tables, hits))
    before = lax.ppermute(prev, "tm", [(i, (i + 1) % n_tm) for i in range(n_tm)])
    main = pl.pallas_call(
        functools.partial(bulk, z),
        out_shape=pltpu.VMEM((groups, trials, LANES), f32),
        in_specs=[vmem_spec()] * 8,
        out_specs=vmem_spec(),
        scratch_shapes=work
        + [
            pltpu.VMEM((2, (z.low_chunks * CHUNK + 1) * groups, LANES), f32),
            pltpu.VMEM((2, 9 * groups, LANES), f32),
        ],
        compiler_params=params,
        cost_estimate=pl.CostEstimate(flops=10**9, bytes_accessed=8 * 10**6, transcendentals=0),
        name="bulk",
    )(*kept(power, edges, bound, sides, inv, tables, hits, high))
    slots = (2, z.capacity, trials, LANES)
    parcel = (2 * z.capacity * trials, LANES)
    held, leaving = pl.pallas_call(
        functools.partial(parcels, z),
        out_shape=(pltpu.VMEM((n_dm // 2, 1, *parcel), bf16),) * 2,
        in_specs=[vmem_spec()] * 2 + [smem_spec()],
        out_specs=[vmem_spec()] * 2,
        scratch_shapes=[pltpu.VMEM((groups, trials, LANES), f32), pltpu.VMEM((n_dm, *slots), f32)],
        compiler_params=params,
        name="parcels",
    )(*kept(main, before), *kept(owner, space=pltpu.SMEM))
    bit = 1
    while True:
        got = lax.ppermute(leaving, "dm", [(i, i ^ bit) for i in range(n_dm)])
        bit *= 2
        if bit == n_dm:
            break
        held, leaving = pl.pallas_call(
            relay,
            out_shape=(pltpu.VMEM((n_dm // 2 // bit, bit, *parcel), bf16),) * 2,
            in_specs=[vmem_spec()] * 2,
            out_specs=[vmem_spec()] * 2,
            compiler_params=params,
            name="relay",
        )(*kept(held, got))
    return pl.pallas_call(
        functools.partial(boxes, z),
        out_shape=jax.ShapeDtypeStruct((z.capacity, n_dm, 1, trials, widths.shape[0], z.spec), bf16),
        in_specs=[smem_spec()] + [vmem_spec()] * 2,
        out_specs=vmem_spec(),
        scratch_shapes=[pltpu.VMEM((n_dm, WMAX, z.capacity * trials, LANES), f32)],
        compiler_params=params,
        name="boxes",
    )(*kept(width, space=pltpu.SMEM), *kept(held, got))


def solution(mesh):
    sizes = dict(mesh.shape)
    return jax.shard_map(
        functools.partial(shards, sizes["dm"], sizes["tm"]),
        mesh=mesh,
        in_specs=(P(("group", "dm", "beam"), "tm"), P(), P(), P(), P()),
        out_specs=P("dm", "group", "beam", None, None, "tm"),
        check_vma=False,
    )
```

```python
import functools
import math

import jax
import jax.numpy as jnp
import numpy as np
from jax import lax
from jax.experimental import pallas as pl
from jax.experimental.pallas import tpu as pltpu
from jax.sharding import PartitionSpec as P

DFT_A = 128
NBLK = 64
FD = 4
TT = 8
MAXT = 3
WMAX = 8
LANES = 128
CHUNK = 16
LIMIT = 32 * 1024 * 1024


def ceil_to(value, unit):
    return -(-value // unit) * unit


def angle_tables(rows, cols, total):
    product = np.arange(rows)[:, None] * np.arange(cols)[None, :] % total
    angle = product.astype(np.float64) * (2.0 * math.pi / total)
    return np.cos(angle), np.sin(angle)


class Sizes:
    def __init__(self, taps, channels, spec, groups, n_dm, n_tm):
        self.taps, self.channels, self.spec, self.groups = taps, channels, spec, groups
        self.n_dm, self.n_tm = n_dm, n_tm
        self.side = channels // DFT_A
        self.rows = DFT_A // 2
        self.deep = self.rows + 16
        self.band_rows = self.rows + 8
        self.hist = taps - 1
        self.raw_rows = self.hist * DFT_A
        self.bounds = n_tm - 1
        self.capacity = 2 * (groups // n_dm)
        self.low_chunks = (spec - (WMAX - 1) - MAXT * TT - (FD - 1)) // CHUNK
        self.high_rows = ceil_to(spec + FD - 1 - self.low_chunks * CHUNK, 16)


def constants(z):
    cos_a, sin_a = angle_tables(DFT_A, DFT_A, DFT_A)
    first = np.concatenate([cos_a[: z.rows], -sin_a[: z.rows]])
    first[z.rows] = cos_a[z.rows]
    tw_cos, tw_sin = angle_tables(z.rows + 1, z.side, z.channels)
    edge = np.zeros((16, z.side))
    edge[0], edge[1] = tw_cos[z.rows], -tw_sin[z.rows]
    tw_cos, tw_sin = tw_cos[: z.rows], tw_sin[: z.rows]
    hidden = tw_cos.copy()
    hidden[0] = 0
    cos_b, sin_b = angle_tables(z.side, z.side, z.side)
    width = z.channels // NBLK
    fine = np.arange(z.groups)[:, None] * FD * (width - 1 - np.arange(width))[None, :] // (z.groups * (width - 1))
    parities = width // DFT_A
    masks = np.zeros((2, FD, parities, z.groups, LANES))
    for step in range(FD):
        for parity in range(parities):
            hit = fine[:, parity * DFT_A : (parity + 1) * DFT_A] == step
            masks[0, step, parity, :, : z.rows] = hit[:, : z.rows]
            masks[0, step, parity, :, z.rows : z.deep] = hit[:, z.rows, None]
            masks[1, step, parity, :, 1 : z.rows] = hit[:, : z.rows : -1]
    weight = np.full((z.deep, LANES), 2.0 / z.channels)
    weight[0] = weight[z.rows] = 1.0 / z.channels
    expand = np.zeros((NBLK, 2 * z.side))
    lane = np.arange(z.side)
    expand[lane // parities, lane] = 1
    expand[(z.side - 1 - lane) // parities, z.side + lane] = 1
    tables = {
        "first": first,
        "cos": tw_cos,
        "hidden": hidden,
        "edge": edge,
        "sin": tw_sin,
        "second": np.concatenate([cos_b, sin_b]),
        "second_im": np.concatenate([-sin_b, cos_b]),
        "masks": masks,
        "weight": weight,
        "expand": expand[:, : z.side],
        "expand_im": expand[:, z.side :],
    }
    kept_masks, z.mask_rows = [], {}
    for key in np.ndindex(masks.shape[:3]):
        if masks[key].any():
            z.mask_rows[key] = len(kept_masks) * z.groups
            kept_masks.append(masks[key])
    tables["masks"] = np.concatenate(kept_masks)
    places, row = {}, 0
    for name, table in tables.items():
        places[name] = (row, row + table.shape[0])
        row += table.shape[0]
    return jnp.asarray(np.concatenate(list(tables.values())), jnp.bfloat16), places


def table(z, ref, name):
    first, last = z.places[name]
    return ref[first:last]


def wide_table(z, ref, name):
    return jnp.concatenate([table(z, ref, name), table(z, ref, name + "_im")], 1)


def fill_frames(z, history, load, pr_ref, y_ref, count, save=None):
    for block in range(DFT_A // 16):
        rows = pl.ds(block * 16, 16)
        taps = [
            jnp.concatenate(
                [
                    pr_ref[tap, :, (2 * block + part) * 8 * LANES : (2 * block + part + 1) * 8 * LANES].reshape(8, LANES)
                    for part in range(2)
                ]
            )
            for tap in range(z.taps)
        ]
        window = [history(k, block) for k in range(z.hist)]
        for k in range(count):
            window.append(load(k, block))
            acc = window[0] * taps[0]
            for tap in range(1, z.taps):
                acc = acc + window[tap] * taps[tap]
            y_ref[rows, k * LANES : (k + 1) * LANES] = acc.astype(jnp.bfloat16)
            window.pop(0)
        if save is not None:
            for k in range(z.hist):
                save(k, block, window[k])


def transform(z, y_ref, tab_ref, t_refs, edge_ref, count):
    cos, hidden, sin = (table(z, tab_ref, name) for name in ("cos", "hidden", "sin"))
    part = count // len(t_refs)
    out = []
    for index, t_ref in enumerate(t_refs):
        for at in range(0, part, 2):
            pair = min(2, part - at)
            lane = (index * part + at) * LANES
            a = jnp.dot(
                table(z, tab_ref, "first"), y_ref[:, lane : lane + pair * LANES], preferred_element_type=jnp.float32
            )
            for k in range(pair):
                lanes = slice(k * LANES, (k + 1) * LANES)
                edge_ref[index * part + at + k : index * part + at + k + 1] = a[z.rows : z.rows + 1, lanes]
                re, im = a[: z.rows, lanes].astype(jnp.bfloat16), a[z.rows :, lanes].astype(jnp.bfloat16)
                rows = slice((at + k) * z.rows, (at + k + 1) * z.rows)
                t_ref[rows, :LANES] = re * cos + im * sin
                t_ref[rows, LANES:] = im * hidden - re * sin
        last = index + 1 == len(t_refs)
        if last:
            turn = table(z, tab_ref, "edge").astype(jnp.float32)
            rows = slice(part * z.rows, part * z.rows + 16)
            t_ref[rows, :LANES] = (edge_ref[...] * turn[0:1]).astype(jnp.bfloat16)
            t_ref[rows, LANES:] = (edge_ref[...] * turn[1:2]).astype(jnp.bfloat16)
        c = jnp.dot(
            t_ref[: part * z.rows + (16 if last else 0)], wide_table(z, tab_ref, "second"),
            preferred_element_type=jnp.float32,
        )
        for k in range(part):
            rows = c[k * z.rows : (k + 1) * z.rows]
            re, im = rows[:, :LANES], rows[:, LANES:]
            out.append(re * re + im * im)
    re, im = c[part * z.rows :, :LANES], c[part * z.rows :, LANES:]
    return out, re * re + im * im


def channelize(z, raw_ref, proto_ref, tab_in, delays_ref, owners_in, widths_in,
               power_ref, edges_ref, pr_ref, band_ref, msg_ref, tab_ref, trial_ref, owners_ref, widths_ref,
               buf, hist_ref, y0_ref, y1_ref, t0_ref, t1_ref, e0_ref, e1_ref, sum_ref, sems):
    chunks = z.spec // CHUNK
    span = CHUNK * z.channels

    def raw_copy(first, last, side):
        part = pl.ds(first * span, (last - first) * span)
        return pltpu.make_async_copy(raw_ref.at[:, part], buf.at[:, part], sems.at[side])

    tab_copy = pltpu.make_async_copy(tab_in, tab_ref, sems.at[2])
    delays_copy = pltpu.make_async_copy(delays_ref, trial_ref, sems.at[1])
    owners_copy = pltpu.make_async_copy(owners_in, owners_ref, sems.at[3])
    widths_copy = pltpu.make_async_copy(widths_in, widths_ref, sems.at[2])
    early_copies = [raw_copy(0, 1, 0), raw_copy(1, 3, 1), raw_copy(3, 5, 2), raw_copy(5, chunks, 0)]
    early_copies[0].start()
    for tap in range(z.taps):
        pltpu.make_async_copy(proto_ref.at[tap : tap + 1], pr_ref.at[tap], sems.at[3]).start()
    tab_copy.start()
    early_copies[1].start()
    hist_ref[...] = jnp.zeros_like(hist_ref)
    band_ref[...] = jnp.zeros_like(band_ref)
    sum_ref[...] = jnp.zeros_like(sum_ref)
    early = lax.axis_index("tm") > 0
    place = lax.broadcasted_iota(jnp.int32, (16, LANES), 0)

    def frames(i, y_ref):
        base = i * span

        def load(k, block):
            parts = []
            for part in range(2):
                start = pl.multiple_of(base + k * z.channels + (2 * block + part) * 8 * LANES, 8 * LANES)
                parts.append(buf[:, pl.ds(start, 8 * LANES)].astype(jnp.float32).reshape(8, LANES))
            return jnp.concatenate(parts)

        def history(k, block):
            return hist_ref[k, block * 16 : block * 16 + 16, :]

        def save(k, block, value):
            hist_ref[k, block * 16 : block * 16 + 16, :] = value

        fill_frames(z, history, load, pr_ref, y_ref, CHUNK, save)

    def powers(i, y_ref, t_refs, e_ref):
        power, edges = transform(z, y_ref, tab_ref, t_refs, e_ref, CHUNK)
        late = power[z.hist]
        for k in range(z.hist + 1, CHUNK):
            late = late + power[k]
        head = power[0]
        for k in range(1, z.hist):
            head = head + power[k]
        skip = jnp.logical_and(i == 0, early)
        band_ref[: z.rows] = band_ref[: z.rows] + late + jnp.where(skip, 0.0, head)
        sum_ref[...] = sum_ref[...] + jnp.where(jnp.logical_and(skip, place < z.hist), 0.0, edges)
        edges_ref[pl.ds(pl.multiple_of(i * CHUNK, CHUNK), CHUNK)] = edges
        for k in range(CHUNK):
            power_ref[i * CHUNK + k] = power[k]

    pltpu.make_async_copy(pr_ref, pr_ref, sems.at[3]).wait()
    owners_copy.start()
    early_copies[0].wait()
    tab_copy.wait()
    early_copies[2].start()
    frames(0, y0_ref)
    early_copies[3].start()

    def step(j, carry):
        i = 2 * j
        for turn in range(3):

            @pl.when(j == turn)
            def _(turn=turn):
                early_copies[turn + 1].wait()
                if turn < 2:
                    (delays_copy, widths_copy)[turn].start()

        frames(i + 1, y1_ref)
        powers(i, y0_ref, [t0_ref], e0_ref)
        frames(i + 2, y0_ref)
        powers(i + 1, y1_ref, [t1_ref], e1_ref)
        return carry

    lax.fori_loop(0, chunks // 2 - 1, step, 0)
    owners_copy.wait()
    delays_copy.wait()
    frames(chunks - 1, y1_ref)
    powers(chunks - 2, y0_ref, [t0_ref], e0_ref)
    powers(chunks - 1, y1_ref, [t1_ref], e1_ref)
    def spectrum(start):
        start = pl.multiple_of(start, z.channels)
        return buf[:, pl.ds(start, z.channels)].astype(jnp.float32).reshape(DFT_A, LANES).astype(jnp.bfloat16)

    row = 0
    tail = (z.spec - z.hist) * z.channels
    starts = [jnp.where(early, 0, tail)] if z.n_tm == 2 else [tail, 0]
    for start in starts:
        for k in range(z.hist):
            msg_ref[row : row + DFT_A] = spectrum(start + k * z.channels)
            row += DFT_A
    total = jnp.sum(sum_ref[...], 0, keepdims=True)
    rest = jnp.concatenate([total, jnp.zeros((15, LANES), jnp.float32)])
    band_ref[z.rows :] = rest[: z.band_rows - z.rows]
    msg_ref[row : row + z.deep] = jnp.concatenate([band_ref[: z.rows], rest]).astype(jnp.bfloat16)
    widths_copy.wait()


def coarse(z, tab_ref, trial_ref, hits_ref):
    unit = 1.0 / (math.sqrt(z.channels // NBLK) * math.sqrt(NBLK))
    trials = trial_ref.shape[1]
    tall = jnp.concatenate(
        [
            jnp.concatenate([trial_ref[g].astype(jnp.float32), jnp.zeros((8 - trials, NBLK), jnp.float32)])
            for g in range(z.groups)
        ]
    )
    spread = jnp.dot(
        tall.astype(jnp.bfloat16), wide_table(z, tab_ref, "expand"), preferred_element_type=jnp.float32
    )
    for g in range(z.groups):
        mine = spread[g * 8 : g * 8 + 8]
        hits = jnp.concatenate([jnp.where(mine == value, unit, 0.0) for value in range(MAXT + 1)])
        hits_ref[g] = hits.astype(jnp.bfloat16)


def boundary(z, pr_ref, band_ref, own_ref, other_ref, tab_ref, y_ref, t_ref, e_ref, bound_ref, sides_ref, inv_ref):
    me = lax.axis_index("tm")
    lo = z.bounds * z.raw_rows
    rest = other_ref[lo : lo + z.deep].astype(jnp.float32)
    total = band_ref[: z.rows] + rest[: z.rows]
    edge = band_ref[z.rows :] + rest[z.rows : z.band_rows]
    e_ref[...] = jnp.zeros_like(e_ref)
    swap = jnp.logical_and(me > 0, z.n_tm == 2)
    y_ref[:, z.hist * LANES :] = jnp.zeros((DFT_A, LANES), jnp.bfloat16)
    for b in range(z.bounds):

        def take(k, block, first, b=b):
            start = b * z.raw_rows + k * DFT_A + block * 16
            own = own_ref[start : start + 16].astype(jnp.float32)
            other = other_ref[start : start + 16].astype(jnp.float32)
            return jnp.where(swap, other, own) if first else jnp.where(swap, own, other)

        fill_frames(
            z, lambda k, block: take(k, block, True), lambda k, block: take(k, block, False), pr_ref, y_ref, z.hist
        )
        power, edges = transform(z, y_ref, tab_ref, [t_ref], e_ref, z.hist)
        sides_ref[b] = edges
        edge = edge + jnp.sum(edges, 0, keepdims=True)
        for k in range(z.hist):
            total = total + power[k]
            bound_ref[b * z.hist + k] = power[k]
    scale = float(z.taps * z.channels)
    total = jnp.concatenate([total, edge])
    inv_ref[...] = 1.0 / (total * (1.0 / (z.spec * z.n_tm)) + 1e-6 * scale)


def subbands(
    z, first, last, power_ref, edges_ref, bound_ref, sides_ref, inv_ref, tab_ref, weighted_ref, sums_ref, mean_ref, sub_ref
):
    me = lax.axis_index("tm")
    groups = z.groups
    weighted_ref[...] = table(z, tab_ref, "weight").astype(jnp.float32)[: z.band_rows] * inv_ref[...]
    before = jnp.maximum(me - 1, 0)
    mine = before * z.hist
    place = lax.broadcasted_iota(jnp.int32, (CHUNK, LANES), 0)

    def edges_of(i):
        value = edges_ref[pl.ds(pl.multiple_of(i * CHUNK, CHUNK), CHUNK)]
        if first == 0:
            inside = jnp.logical_and(jnp.logical_and(me > 0, i == 0), place < z.hist)
            value = jnp.where(inside, sides_ref[before], value)
        return value

    empty = jnp.zeros((groups, LANES), jnp.float32)

    def power_of(i, k):
        value = power_ref[i * CHUNK + k]
        if first == 0 and k < z.hist:
            value = jnp.where(jnp.logical_and(me > 0, i == 0), bound_ref[mine + k], value)
        return value

    def means(i):
        for k in range(CHUNK):
            value = power_of(i, k) * weighted_ref[: z.rows]
            sums_ref[k * 8 : k * 8 + 8] = jnp.sum(value.reshape(z.rows // 8, 8, LANES), 0)
        acc = edges_of(i) * weighted_ref[z.rows : z.rows + 1]
        for j in range(8):
            acc = acc + sums_ref[pl.ds(j, CHUNK, stride=8)]
        at = pl.multiple_of(i * CHUNK, CHUNK)
        mean_ref[pl.ds(at, CHUNK)] = jnp.broadcast_to(jnp.sum(acc, 1, keepdims=True), (CHUNK, LANES))

    parities = z.channels // NBLK // DFT_A
    lane = lax.broadcasted_iota(jnp.int32, (groups, LANES), 1)

    def picked(m, step, value):
        rows = [z.mask_rows.get((m, step, parity)) for parity in range(parities)]
        part = None if None in rows else value[rows[0] : rows[0] + groups]
        for parity, row in enumerate(rows):
            if row is not None and (part is None or parity > 0):
                hit = (lane if m == 0 else LANES - 1 - lane) % parities == parity
                part = jnp.where(hit, value[row : row + groups], 0.0 if part is None else part)
        return part

    def plus(left, right):
        return left if right is None else right if left is None else left + right

    def flat_step(i, carry):
        flats = []
        at = pl.multiple_of(i * CHUNK, CHUNK)
        edges = edges_of(i) * inv_ref[z.rows : z.rows + 1] - mean_ref[pl.ds(at, CHUNK)]
        open_sums = [list(carry[m]) for m in range(2)]
        for k in range(CHUNK):
            flat = power_of(i, k) * inv_ref[: z.rows] - mean_ref[pl.ds(i * CHUNK + k, 1)]
            edge = jnp.where(place == k, edges, 0.0)
            flats.append(jnp.concatenate([flat, edge]).astype(jnp.bfloat16))
            if k % 2 == 0:
                continue
            masks = table(z, tab_ref, "masks")[:, : z.deep]
            found = jnp.dot(masks, jnp.concatenate(flats[-2:], 1), preferred_element_type=jnp.float32)
            for half in range(2):
                value = found[:, half * LANES : (half + 1) * LANES]
                at = pl.multiple_of(((i - first) * CHUNK + k - 1 + half) * groups, 8)
                for m in range(2):
                    parts = [picked(m, step, value) for step in range(FD)]
                    sub_ref[m, pl.ds(at, groups)] = plus(open_sums[m][0], parts[0])
                    later = open_sums[m][1:] + [None]
                    open_sums[m] = [plus(later[step], parts[step + 1]) for step in range(FD - 1)]
        means(jnp.minimum(i + 1, last - 1))
        return tuple(tuple(empty if part is None else part for part in value) for value in open_sums)

    means(first)
    return lax.fori_loop(first, last, flat_step, ((empty,) * (FD - 1),) * 2)


def delayed(z, hits, series):
    lane = lax.broadcasted_iota(jnp.int32, (8, LANES), 1)
    found = lax.dot_general(hits, series, (((1,), (1,)), ((), ())), preferred_element_type=jnp.float32)
    total = found[:8]
    for value in range(1, MAXT + 1):
        moved = pltpu.roll(found[value * 8 : value * 8 + 8], value * TT, 1)
        total = total + jnp.where(lane >= value * TT, moved, 0.0)
    return total


def tails(z, power_ref, edges_ref, pr_ref, band_ref, own_ref, other_ref, tab_ref, hits_ref,
          prev_ref, high_ref, bound_ref, sides_ref, inv_ref, y_ref, t_ref, e_ref, late_ref, weighted_ref, sums_ref, mean_ref):
    groups = z.groups
    boundary(z, pr_ref, band_ref, own_ref, other_ref, tab_ref, y_ref, t_ref, e_ref, bound_ref, sides_ref, inv_ref)
    carry = subbands(
        z, z.low_chunks, z.spec // CHUNK, power_ref, edges_ref, bound_ref, sides_ref, inv_ref, tab_ref,
        weighted_ref, sums_ref, mean_ref, high_ref,
    )
    count = z.high_rows
    done = z.spec - z.low_chunks * CHUNK
    for m in range(2):
        for step in range(FD - 1):
            high_ref[m, (done + step) * groups : (done + step + 1) * groups] = carry[m][step]
    high_ref[:, (done + FD - 1) * groups :] = jnp.zeros((2, (count + 1 - done - FD + 1) * groups, LANES), jnp.float32)
    blank = jnp.zeros((LANES - count, 2 * LANES), jnp.bfloat16)
    trials = late_ref.shape[1]
    lane = lax.broadcasted_iota(jnp.int32, (8, LANES), 1)
    start = done - (WMAX - 1)
    for g in range(groups):
        both = [high_ref[m, pl.ds(g, count, stride=groups)].astype(jnp.bfloat16) for m in range(2)]
        dd = delayed(z, hits_ref[g], jnp.concatenate([jnp.concatenate(both, 1), blank]))
        late = pltpu.roll(dd, LANES - start, 1)
        late_ref[g] = jnp.where(lane < WMAX - 1 + MAXT * TT + FD - 1, late, 0.0)[:trials]
    prev_ref[...] = late_ref[...].reshape(groups * trials, LANES).astype(jnp.bfloat16)


def bulk(z, power_ref, edges_ref, bound_ref, sides_ref, inv_ref, tab_ref, hits_ref, high_ref,
         main_ref, weighted_ref, sums_ref, mean_ref, low_ref, join_ref):
    groups = z.groups
    carry = subbands(
        z, 0, z.low_chunks, power_ref, edges_ref, bound_ref, sides_ref, inv_ref, tab_ref,
        weighted_ref, sums_ref, mean_ref, low_ref,
    )
    join_ref[...] = jnp.zeros_like(join_ref)
    for m in range(2):
        for step in range(FD - 1):
            join_ref[m, step * groups : (step + 1) * groups] = carry[m][step]
    low = z.low_chunks * CHUNK
    trials = main_ref.shape[1]
    for g in range(groups):
        both = []
        for m in range(2):
            edge = high_ref[m, pl.ds(g, 8, stride=groups)] + join_ref[m, pl.ds(g, 8, stride=groups)]
            rest = high_ref[m, pl.ds(8 * groups + g, z.spec - low - 8, stride=groups)]
            both.append(jnp.concatenate([low_ref[m, pl.ds(g, low, stride=groups)], edge, rest]).astype(jnp.bfloat16))
        main_ref[g] = delayed(z, hits_ref[g], jnp.concatenate(both, 1))[:trials]


def parcels(z, main_ref, prev_ref, owners_ref, stay_ref, leave_ref, late_ref, all_ref):
    me = lax.axis_index("dm")
    all_ref[...] = jnp.zeros_like(all_ref)
    late_ref[...] = prev_ref[...].astype(jnp.float32).reshape(late_ref.shape)
    for g in range(z.groups):
        owner = owners_ref[g]
        rank = jnp.int32(0)
        for earlier in range(g):
            rank = rank + jnp.where(owners_ref[earlier] == owner, 1, 0)
        all_ref[owner ^ me, 0, rank] = main_ref[g]
        all_ref[owner ^ me, 1, rank] = late_ref[g]
    half = z.n_dm // 2
    for r in range(z.n_dm):
        value = all_ref[r].reshape(stay_ref.shape[2:]).astype(jnp.bfloat16)
        (stay_ref if r < half else leave_ref)[r % half, 0] = value


def relay(held_ref, got_ref, stay_ref, leave_ref):
    count = held_ref.shape[1]
    half = held_ref.shape[0] // 2
    for r in range(2 * half):
        target = stay_ref if r < half else leave_ref
        target[r % half, :count] = held_ref[r]
        target[r % half, count:] = got_ref[r]


def boxes(z, widths_ref, *refs):
    held_ref, got_ref, out_ref, d_ref = refs
    early = lax.axis_index("tm") == 0
    me = lax.axis_index("dm")
    trials = out_ref.shape[3]
    near = held_ref.shape[1]
    rank = lax.broadcasted_iota(jnp.int32, (8, LANES), 0)
    count = widths_ref.shape[0]
    width = jnp.zeros((8, LANES), jnp.int32)
    for w in range(count):
        width = jnp.where(rank == w, widths_ref[w], width)
    norm = 1.0 / jnp.sqrt(width.astype(jnp.float32))
    weights = [jnp.where(width > lag, norm, 0.0) for lag in range(WMAX)]
    prior = WMAX - 1
    rows = z.capacity * trials
    order, bit = [0], z.n_dm // 2
    while bit:
        order, bit = order + [r + bit for r in order], bit // 2
    for place, r in enumerate(order):
        ref, at = (held_ref, place) if place < near else (got_ref, place - near)
        own = ref[0, at, :rows].astype(jnp.float32)
        past = jnp.where(early, 0.0, ref[0, at, rows:].astype(jnp.float32))
        wide = jnp.concatenate([own, jnp.zeros_like(own)], 1)
        wide = pltpu.roll(wide, prior, 1) + jnp.concatenate([past, jnp.zeros_like(past)], 1)
        for lag in range(WMAX):
            shift = prior - lag
            d_ref[r, lag] = (pltpu.roll(wide, 2 * LANES - shift, 1) if shift else wide)[:, :LANES]
        for s in range(z.capacity):
            for j in range(trials):
                acc = None
                for lag in range(WMAX):
                    part = d_ref[r, lag, s * trials + j : s * trials + j + 1, :] * weights[lag]
                    acc = part if acc is None else acc + part
                out_ref[s, me ^ r, 0, j] = acc[:count].astype(jnp.bfloat16)


def vmem_spec():
    return pl.BlockSpec(memory_space=pltpu.VMEM)


def smem_spec():
    return pl.BlockSpec(memory_space=pltpu.SMEM)


def hbm_spec():
    return pl.BlockSpec(memory_space=pltpu.HBM)


def kept(*values, space=pltpu.VMEM):
    return [pltpu.with_memory_space_constraint(value, space) for value in values]


def shards(n_dm, n_tm, raw, proto, delays, widths, owners):
    taps, channels = proto.shape
    groups, trials, _ = delays.shape
    z = Sizes(taps, channels, raw.shape[1] // channels, groups, n_dm, n_tm)
    tables, z.places = constants(z)
    params = pltpu.CompilerParams(vmem_limit_bytes=LIMIT)
    own_rows = z.raw_rows * (1 if n_tm == 2 else 2) + z.deep
    f32, bf16 = jnp.float32, jnp.bfloat16
    half = CHUNK // 2 * z.rows
    power, edges, pr, band, msg, tables, trial, owner, width = pl.pallas_call(
        functools.partial(channelize, z),
        out_shape=(
            pltpu.VMEM((z.spec, z.rows, LANES), f32),
            pltpu.VMEM((z.spec, LANES), f32),
            pltpu.VMEM((taps, 1, channels), f32),
            pltpu.VMEM((z.band_rows, LANES), f32),
            pltpu.VMEM((own_rows, LANES), bf16),
            pltpu.VMEM(tables.shape, bf16),
            pltpu.VMEM(delays.shape, jnp.int32),
            pltpu.SMEM((groups,), jnp.int32),
            pltpu.SMEM(widths.shape, jnp.int32),
        ),
        in_specs=[hbm_spec()] * 6,
        out_specs=[vmem_spec()] * 7 + [smem_spec()] * 2,
        scratch_shapes=[
            pltpu.VMEM((1, z.spec * channels), bf16),
            pltpu.VMEM((z.hist, DFT_A, LANES), f32),
            pltpu.VMEM((DFT_A, CHUNK * LANES), bf16),
            pltpu.VMEM((DFT_A, CHUNK * LANES), bf16),
            pltpu.VMEM((2 * half + 16, 2 * LANES), bf16),
            pltpu.VMEM((2 * half + 16, 2 * LANES), bf16),
            pltpu.VMEM((16, LANES), f32),
            pltpu.VMEM((16, LANES), f32),
            pltpu.VMEM((16, LANES), f32),
            pltpu.SemaphoreType.DMA((4,)),
        ],
        compiler_params=params,
        name="channelize",
    )(
        *kept(raw, proto, tables, delays, owners.reshape(groups), widths, space=pltpu.HBM)
    )
    if n_tm == 2:
        own, other = msg, lax.ppermute(msg, "tm", [(0, 1), (1, 0)])
    else:
        every = lax.all_gather(msg, "tm")
        lasts = every[:-1, : z.raw_rows].reshape(-1, LANES)
        firsts = every[1:, z.raw_rows : 2 * z.raw_rows].reshape(-1, LANES)
        rest = lax.psum(band, "tm") - band
        rest = jnp.concatenate([rest, jnp.zeros((z.deep - z.band_rows, LANES), f32)]).astype(bf16)
        own, other = jnp.concatenate([lasts, rest]), jnp.concatenate([firsts, rest])
    hits = pl.pallas_call(
        functools.partial(coarse, z),
        out_shape=pltpu.VMEM((groups, (MAXT + 1) * 8, 2 * LANES), bf16),
        in_specs=[vmem_spec()] * 2,
        out_specs=vmem_spec(),
        compiler_params=params,
        name="coarse",
    )(*kept(tables, trial))
    work = [
        pltpu.VMEM((z.band_rows, LANES), f32),
        pltpu.VMEM((CHUNK * 8 + 8, LANES), f32),
        pltpu.VMEM((z.spec, LANES), f32),
    ]
    prev, high, bound, sides, inv = pl.pallas_call(
        functools.partial(tails, z),
        out_shape=(
            pltpu.VMEM((groups * trials, LANES), bf16),
            pltpu.VMEM((2, (z.high_rows + 1) * groups, LANES), f32),
            pltpu.VMEM((z.bounds * z.hist, z.rows, LANES), f32),
            pltpu.VMEM((z.bounds, 16, LANES), f32),
            pltpu.VMEM((z.band_rows, LANES), f32),
        ),
        in_specs=[vmem_spec()] * 8,
        out_specs=[vmem_spec()] * 5,
        scratch_shapes=[
            pltpu.VMEM((DFT_A, (z.hist + 1) * LANES), bf16),
            pltpu.VMEM((z.hist * z.rows + 16, 2 * LANES), bf16),
            pltpu.VMEM((16, LANES), f32),
            pltpu.VMEM((groups, trials, LANES), f32),
        ]
        + work,
        compiler_params=params,
        name="tails",
    )(*kept(power, edges, pr, band, own, other, tables, hits))
    before = lax.ppermute(prev, "tm", [(i, (i + 1) % n_tm) for i in range(n_tm)])
    main = pl.pallas_call(
        functools.partial(bulk, z),
        out_shape=pltpu.VMEM((groups, trials, LANES), f32),
        in_specs=[vmem_spec()] * 8,
        out_specs=vmem_spec(),
        scratch_shapes=work
        + [
            pltpu.VMEM((2, (z.low_chunks * CHUNK + 1) * groups, LANES), f32),
            pltpu.VMEM((2, 9 * groups, LANES), f32),
        ],
        compiler_params=params,
        cost_estimate=pl.CostEstimate(flops=10**9, bytes_accessed=8 * 10**6, transcendentals=0),
        name="bulk",
    )(*kept(power, edges, bound, sides, inv, tables, hits, high))
    slots = (2, z.capacity, trials, LANES)
    parcel = (2 * z.capacity * trials, LANES)
    held, leaving = pl.pallas_call(
        functools.partial(parcels, z),
        out_shape=(pltpu.VMEM((n_dm // 2, 1, *parcel), bf16),) * 2,
        in_specs=[vmem_spec()] * 2 + [smem_spec()],
        out_specs=[vmem_spec()] * 2,
        scratch_shapes=[pltpu.VMEM((groups, trials, LANES), f32), pltpu.VMEM((n_dm, *slots), f32)],
        compiler_params=params,
        name="parcels",
    )(*kept(main, before), *kept(owner, space=pltpu.SMEM))
    bit = n_dm // 2
    while True:
        got = lax.ppermute(leaving, "dm", [(i, i ^ bit) for i in range(n_dm)])
        bit //= 2
        if bit == 0:
            break
        held, leaving = pl.pallas_call(
            relay,
            out_shape=(pltpu.VMEM((bit, n_dm // 2 // bit, *parcel), bf16),) * 2,
            in_specs=[vmem_spec()] * 2,
            out_specs=[vmem_spec()] * 2,
            compiler_params=params,
            name="relay",
        )(*kept(held, got))
    return pl.pallas_call(
        functools.partial(boxes, z),
        out_shape=jax.ShapeDtypeStruct((z.capacity, n_dm, 1, trials, widths.shape[0], z.spec), bf16),
        in_specs=[smem_spec()] + [vmem_spec()] * 2,
        out_specs=vmem_spec(),
        scratch_shapes=[pltpu.VMEM((n_dm, WMAX, z.capacity * trials, LANES), f32)],
        compiler_params=params,
        name="boxes",
    )(*kept(width, space=pltpu.SMEM), *kept(held, got))


def solution(mesh):
    sizes = dict(mesh.shape)
    return jax.shard_map(
        functools.partial(shards, sizes["dm"], sizes["tm"]),
        mesh=mesh,
        in_specs=(P(("group", "dm", "beam"), "tm"), P(), P(), P(), P()),
        out_specs=P("dm", "group", "beam", None, None, "tm"),
        check_vma=False,
    )
```

```python
import functools
import math

import jax
import jax.numpy as jnp
import numpy as np
from jax import lax
from jax.experimental import pallas as pl
from jax.experimental.pallas import tpu as pltpu
from jax.sharding import PartitionSpec as P

DFT_A = 128
NBLK = 64
FD = 4
TT = 8
MAXT = 3
WMAX = 8
LANES = 128
CHUNK = 16
SIDE = 4
LIMIT = 32 * 1024 * 1024


def ceil_to(value, unit):
    return -(-value // unit) * unit


def angle_tables(rows, cols, total):
    product = np.arange(rows)[:, None] * np.arange(cols)[None, :] % total
    angle = product.astype(np.float64) * (2.0 * math.pi / total)
    return np.cos(angle), np.sin(angle)


class Sizes:
    def __init__(self, taps, channels, spec, groups, n_dm, n_tm):
        self.taps, self.channels, self.spec, self.groups = taps, channels, spec, groups
        self.n_dm, self.n_tm = n_dm, n_tm
        self.side = channels // DFT_A
        self.rows = DFT_A // 2
        self.deep = self.rows + 16
        self.band_rows = self.rows + 8
        self.hist = taps - 1
        self.raw_rows = self.hist * DFT_A
        self.bounds = n_tm - 1
        self.capacity = 2 * (groups // n_dm)
        self.low_chunks = (spec - (WMAX - 1) - MAXT * TT - (FD - 1)) // CHUNK
        self.high_rows = ceil_to(spec + FD - 1 - self.low_chunks * CHUNK, 16)


def constants(z):
    cos_a, sin_a = angle_tables(DFT_A, DFT_A, DFT_A)
    first = np.concatenate([cos_a[: z.rows], -sin_a[: z.rows]])
    first[z.rows] = cos_a[z.rows]
    tw_cos, tw_sin = angle_tables(z.rows + 1, z.side, z.channels)
    edge = np.zeros((16, z.side))
    edge[0], edge[1] = tw_cos[z.rows], -tw_sin[z.rows]
    tw_cos, tw_sin = tw_cos[: z.rows], tw_sin[: z.rows]
    hidden = tw_cos.copy()
    hidden[0] = 0
    cos_b, sin_b = angle_tables(z.side, z.side, z.side)
    width = z.channels // NBLK
    fine = np.arange(z.groups)[:, None] * FD * (width - 1 - np.arange(width))[None, :] // (z.groups * (width - 1))
    parities = width // DFT_A
    masks = np.zeros((2, FD, parities, z.groups, LANES))
    for step in range(FD):
        for parity in range(parities):
            hit = fine[:, parity * DFT_A : (parity + 1) * DFT_A] == step
            masks[0, step, parity, :, : z.rows] = hit[:, : z.rows]
            masks[0, step, parity, :, z.rows : z.deep] = hit[:, z.rows, None]
            masks[1, step, parity, :, 1 : z.rows] = hit[:, : z.rows : -1]
    weight = np.full((z.deep, LANES), 2.0 / z.channels)
    weight[0] = weight[z.rows] = 1.0 / z.channels
    expand = np.zeros((NBLK, 2 * z.side))
    lane = np.arange(z.side)
    expand[lane // parities, lane] = 1
    expand[(z.side - 1 - lane) // parities, z.side + lane] = 1
    tables = {
        "first": first,
        "cos": tw_cos,
        "hidden": hidden,
        "edge": edge,
        "sin": tw_sin,
        "second": np.concatenate([cos_b, sin_b]),
        "second_im": np.concatenate([-sin_b, cos_b]),
        "masks": masks,
        "weight": weight,
        "expand": expand[:, : z.side],
        "expand_im": expand[:, z.side :],
    }
    kept_masks, z.mask_rows = [], {}
    for key in np.ndindex(masks.shape[:3]):
        if masks[key].any():
            z.mask_rows[key] = len(kept_masks) * z.groups
            kept_masks.append(masks[key])
    tables["masks"] = np.concatenate(kept_masks)
    places, row = {}, 0
    for name, table in tables.items():
        places[name] = (row, row + table.shape[0])
        row += table.shape[0]
    return jnp.asarray(np.concatenate(list(tables.values())), jnp.bfloat16), places


def table(z, ref, name):
    first, last = z.places[name]
    return ref[first:last]


def wide_table(z, ref, name):
    return jnp.concatenate([table(z, ref, name), table(z, ref, name + "_im")], 1)


def fill_frames(z, history, load, pr_ref, y_ref, count, save=None):
    for block in range(DFT_A // 16):
        rows = pl.ds(block * 16, 16)
        taps = [
            jnp.concatenate(
                [
                    pr_ref[tap, :, (2 * block + part) * 8 * LANES : (2 * block + part + 1) * 8 * LANES].reshape(8, LANES)
                    for part in range(2)
                ]
            )
            for tap in range(z.taps)
        ]
        window = [history(k, block) for k in range(z.hist)]
        for k in range(count):
            window.append(load(k, block))
            acc = window[0] * taps[0]
            for tap in range(1, z.taps):
                acc = acc + window[tap] * taps[tap]
            y_ref[rows, k * LANES : (k + 1) * LANES] = acc.astype(jnp.bfloat16)
            window.pop(0)
        if save is not None:
            for k in range(z.hist):
                save(k, block, window[k])


def transform(z, y_ref, tab_ref, t_refs, edge_ref, count):
    cos, hidden, sin = (table(z, tab_ref, name) for name in ("cos", "hidden", "sin"))
    part = count // len(t_refs)
    out = []
    for index, t_ref in enumerate(t_refs):
        for at in range(0, part, SIDE):
            pair = min(SIDE, part - at)
            lane = (index * part + at) * LANES
            a = jnp.dot(
                table(z, tab_ref, "first"), y_ref[:, lane : lane + pair * LANES], preferred_element_type=jnp.float32
            )
            for k in range(pair):
                lanes = slice(k * LANES, (k + 1) * LANES)
                edge_ref[index * part + at + k : index * part + at + k + 1] = a[z.rows : z.rows + 1, lanes]
                re, im = a[: z.rows, lanes].astype(jnp.bfloat16), a[z.rows :, lanes].astype(jnp.bfloat16)
                rows = slice((at + k) * z.rows, (at + k + 1) * z.rows)
                t_ref[rows, :LANES] = re * cos + im * sin
                t_ref[rows, LANES:] = im * hidden - re * sin
        last = index + 1 == len(t_refs)
        if last:
            turn = table(z, tab_ref, "edge").astype(jnp.float32)
            rows = slice(part * z.rows, part * z.rows + 16)
            t_ref[rows, :LANES] = (edge_ref[...] * turn[0:1]).astype(jnp.bfloat16)
            t_ref[rows, LANES:] = (edge_ref[...] * turn[1:2]).astype(jnp.bfloat16)
        c = jnp.dot(
            t_ref[: part * z.rows + (16 if last else 0)], wide_table(z, tab_ref, "second"),
            preferred_element_type=jnp.float32,
        )
        for k in range(part):
            rows = c[k * z.rows : (k + 1) * z.rows]
            re, im = rows[:, :LANES], rows[:, LANES:]
            out.append(re * re + im * im)
    re, im = c[part * z.rows :, :LANES], c[part * z.rows :, LANES:]
    return out, re * re + im * im


def channelize(z, raw_ref, proto_ref, tab_in, delays_ref, owners_in, widths_in,
               power_ref, edges_ref, pr_ref, band_ref, msg_ref, tab_ref, trial_ref, owners_ref, widths_ref,
               buf, hist_ref, y0_ref, y1_ref, t0_ref, t1_ref, e0_ref, e1_ref, sum_ref, sems):
    chunks = z.spec // CHUNK
    span = CHUNK * z.channels

    def raw_copy(first, last, side):
        part = pl.ds(first * span, (last - first) * span)
        return pltpu.make_async_copy(raw_ref.at[:, part], buf.at[:, part], sems.at[side])

    tab_copy = pltpu.make_async_copy(tab_in, tab_ref, sems.at[2])
    delays_copy = pltpu.make_async_copy(delays_ref, trial_ref, sems.at[1])
    owners_copy = pltpu.make_async_copy(owners_in, owners_ref, sems.at[3])
    widths_copy = pltpu.make_async_copy(widths_in, widths_ref, sems.at[2])
    early_copies = [raw_copy(0, 1, 0), raw_copy(1, 3, 1), raw_copy(3, 5, 2), raw_copy(5, chunks, 0)]
    early_copies[0].start()
    for tap in range(z.taps):
        pltpu.make_async_copy(proto_ref.at[tap : tap + 1], pr_ref.at[tap], sems.at[3]).start()
    tab_copy.start()
    early_copies[1].start()
    hist_ref[...] = jnp.zeros_like(hist_ref)
    band_ref[...] = jnp.zeros_like(band_ref)
    sum_ref[...] = jnp.zeros_like(sum_ref)
    early = lax.axis_index("tm") > 0
    place = lax.broadcasted_iota(jnp.int32, (16, LANES), 0)

    def frames(i, y_ref):
        base = i * span

        def load(k, block):
            parts = []
            for part in range(2):
                start = pl.multiple_of(base + k * z.channels + (2 * block + part) * 8 * LANES, 8 * LANES)
                parts.append(buf[:, pl.ds(start, 8 * LANES)].astype(jnp.float32).reshape(8, LANES))
            return jnp.concatenate(parts)

        def history(k, block):
            return hist_ref[k, block * 16 : block * 16 + 16, :]

        def save(k, block, value):
            hist_ref[k, block * 16 : block * 16 + 16, :] = value

        fill_frames(z, history, load, pr_ref, y_ref, CHUNK, save)

    def powers(i, y_ref, t_refs, e_ref):
        power, edges = transform(z, y_ref, tab_ref, t_refs, e_ref, CHUNK)
        late = power[z.hist]
        for k in range(z.hist + 1, CHUNK):
            late = late + power[k]
        head = power[0]
        for k in range(1, z.hist):
            head = head + power[k]
        skip = jnp.logical_and(i == 0, early)
        band_ref[: z.rows] = band_ref[: z.rows] + late + jnp.where(skip, 0.0, head)
        sum_ref[...] = sum_ref[...] + jnp.where(jnp.logical_and(skip, place < z.hist), 0.0, edges)
        edges_ref[pl.ds(pl.multiple_of(i * CHUNK, CHUNK), CHUNK)] = edges
        for k in range(CHUNK):
            power_ref[i * CHUNK + k] = power[k]

    pltpu.make_async_copy(pr_ref, pr_ref, sems.at[3]).wait()
    owners_copy.start()
    early_copies[0].wait()
    tab_copy.wait()
    early_copies[2].start()
    frames(0, y0_ref)
    early_copies[3].start()

    def step(j, carry):
        i = 2 * j
        for turn in range(3):

            @pl.when(j == turn)
            def _(turn=turn):
                early_copies[turn + 1].wait()
                if turn < 2:
                    (delays_copy, widths_copy)[turn].start()

        frames(i + 1, y1_ref)
        powers(i, y0_ref, [t0_ref], e0_ref)
        frames(i + 2, y0_ref)
        powers(i + 1, y1_ref, [t1_ref], e1_ref)
        return carry

    lax.fori_loop(0, chunks // 2 - 1, step, 0)
    owners_copy.wait()
    delays_copy.wait()
    frames(chunks - 1, y1_ref)
    powers(chunks - 2, y0_ref, [t0_ref], e0_ref)
    powers(chunks - 1, y1_ref, [t1_ref], e1_ref)
    def spectrum(start):
        start = pl.multiple_of(start, z.channels)
        return buf[:, pl.ds(start, z.channels)].astype(jnp.float32).reshape(DFT_A, LANES).astype(jnp.bfloat16)

    row = 0
    tail = (z.spec - z.hist) * z.channels
    starts = [jnp.where(early, 0, tail)] if z.n_tm == 2 else [tail, 0]
    for start in starts:
        for k in range(z.hist):
            msg_ref[row : row + DFT_A] = spectrum(start + k * z.channels)
            row += DFT_A
    total = jnp.sum(sum_ref[...], 0, keepdims=True)
    rest = jnp.concatenate([total, jnp.zeros((15, LANES), jnp.float32)])
    band_ref[z.rows :] = rest[: z.band_rows - z.rows]
    msg_ref[row : row + z.deep] = jnp.concatenate([band_ref[: z.rows], rest]).astype(jnp.bfloat16)
    widths_copy.wait()


def coarse(z, tab_ref, trial_ref, hits_ref):
    unit = 1.0 / (math.sqrt(z.channels // NBLK) * math.sqrt(NBLK))
    trials = trial_ref.shape[1]
    tall = jnp.concatenate(
        [
            jnp.concatenate([trial_ref[g].astype(jnp.float32), jnp.zeros((8 - trials, NBLK), jnp.float32)])
            for g in range(z.groups)
        ]
    )
    spread = jnp.dot(
        tall.astype(jnp.bfloat16), wide_table(z, tab_ref, "expand"), preferred_element_type=jnp.float32
    )
    for g in range(z.groups):
        mine = spread[g * 8 : g * 8 + 8]
        hits = jnp.concatenate([jnp.where(mine == value, unit, 0.0) for value in range(MAXT + 1)])
        hits_ref[g] = hits.astype(jnp.bfloat16)


def boundary(z, pr_ref, band_ref, own_ref, other_ref, tab_ref, y_ref, t_ref, e_ref, bound_ref, sides_ref, inv_ref):
    me = lax.axis_index("tm")
    lo = z.bounds * z.raw_rows
    rest = other_ref[lo : lo + z.deep].astype(jnp.float32)
    total = band_ref[: z.rows] + rest[: z.rows]
    edge = band_ref[z.rows :] + rest[z.rows : z.band_rows]
    e_ref[...] = jnp.zeros_like(e_ref)
    swap = jnp.logical_and(me > 0, z.n_tm == 2)
    y_ref[:, z.hist * LANES :] = jnp.zeros((DFT_A, LANES), jnp.bfloat16)
    for b in range(z.bounds):

        def take(k, block, first, b=b):
            start = b * z.raw_rows + k * DFT_A + block * 16
            own = own_ref[start : start + 16].astype(jnp.float32)
            other = other_ref[start : start + 16].astype(jnp.float32)
            return jnp.where(swap, other, own) if first else jnp.where(swap, own, other)

        fill_frames(
            z, lambda k, block: take(k, block, True), lambda k, block: take(k, block, False), pr_ref, y_ref, z.hist
        )
        power, edges = transform(z, y_ref, tab_ref, [t_ref], e_ref, z.hist)
        sides_ref[b] = edges
        edge = edge + jnp.sum(edges, 0, keepdims=True)
        for k in range(z.hist):
            total = total + power[k]
            bound_ref[b * z.hist + k] = power[k]
    scale = float(z.taps * z.channels)
    total = jnp.concatenate([total, edge])
    inv_ref[...] = 1.0 / (total * (1.0 / (z.spec * z.n_tm)) + 1e-6 * scale)


def subbands(
    z, first, last, power_ref, edges_ref, bound_ref, sides_ref, inv_ref, tab_ref, weighted_ref, sums_ref, mean_ref, sub_ref
):
    me = lax.axis_index("tm")
    groups = z.groups
    weighted_ref[...] = table(z, tab_ref, "weight").astype(jnp.float32)[: z.band_rows] * inv_ref[...]
    before = jnp.maximum(me - 1, 0)
    mine = before * z.hist
    place = lax.broadcasted_iota(jnp.int32, (CHUNK, LANES), 0)

    def edges_of(i):
        value = edges_ref[pl.ds(pl.multiple_of(i * CHUNK, CHUNK), CHUNK)]
        if first == 0:
            inside = jnp.logical_and(jnp.logical_and(me > 0, i == 0), place < z.hist)
            value = jnp.where(inside, sides_ref[before], value)
        return value

    empty = jnp.zeros((groups, LANES), jnp.float32)

    def power_of(i, k):
        value = power_ref[i * CHUNK + k]
        if first == 0 and k < z.hist:
            value = jnp.where(jnp.logical_and(me > 0, i == 0), bound_ref[mine + k], value)
        return value

    def means(i):
        for k in range(CHUNK):
            value = power_of(i, k) * weighted_ref[: z.rows]
            sums_ref[k * 8 : k * 8 + 8] = jnp.sum(value.reshape(z.rows // 8, 8, LANES), 0)
        acc = edges_of(i) * weighted_ref[z.rows : z.rows + 1]
        for j in range(8):
            acc = acc + sums_ref[pl.ds(j, CHUNK, stride=8)]
        at = pl.multiple_of(i * CHUNK, CHUNK)
        mean_ref[pl.ds(at, CHUNK)] = jnp.broadcast_to(jnp.sum(acc, 1, keepdims=True), (CHUNK, LANES))

    parities = z.channels // NBLK // DFT_A
    lane = lax.broadcasted_iota(jnp.int32, (groups, LANES), 1)

    def picked(m, step, value):
        rows = [z.mask_rows.get((m, step, parity)) for parity in range(parities)]
        part = None if None in rows else value[rows[0] : rows[0] + groups]
        for parity, row in enumerate(rows):
            if row is not None and (part is None or parity > 0):
                hit = (lane if m == 0 else LANES - 1 - lane) % parities == parity
                part = jnp.where(hit, value[row : row + groups], 0.0 if part is None else part)
        return part

    def plus(left, right):
        return left if right is None else right if left is None else left + right

    def flat_step(i, carry):
        flats = []
        at = pl.multiple_of(i * CHUNK, CHUNK)
        edges = edges_of(i) * inv_ref[z.rows : z.rows + 1] - mean_ref[pl.ds(at, CHUNK)]
        open_sums = [list(carry[m]) for m in range(2)]
        for k in range(CHUNK):
            flat = power_of(i, k) * inv_ref[: z.rows] - mean_ref[pl.ds(i * CHUNK + k, 1)]
            edge = jnp.where(place == k, edges, 0.0)
            flats.append(jnp.concatenate([flat, edge]).astype(jnp.bfloat16))
            if (k + 1) % SIDE:
                continue
            masks = table(z, tab_ref, "masks")[:, : z.deep]
            found = jnp.dot(masks, jnp.concatenate(flats[-SIDE:], 1), preferred_element_type=jnp.float32)
            for half in range(SIDE):
                value = found[:, half * LANES : (half + 1) * LANES]
                at = pl.multiple_of(((i - first) * CHUNK + k + 1 - SIDE + half) * groups, 8)
                for m in range(2):
                    parts = [picked(m, step, value) for step in range(FD)]
                    sub_ref[m, pl.ds(at, groups)] = plus(open_sums[m][0], parts[0])
                    later = open_sums[m][1:] + [None]
                    open_sums[m] = [plus(later[step], parts[step + 1]) for step in range(FD - 1)]
        means(jnp.minimum(i + 1, last - 1))
        return tuple(tuple(empty if part is None else part for part in value) for value in open_sums)

    means(first)
    return lax.fori_loop(first, last, flat_step, ((empty,) * (FD - 1),) * 2)


def delayed(z, hits, series):
    lane = lax.broadcasted_iota(jnp.int32, (8, LANES), 1)
    found = lax.dot_general(hits, series, (((1,), (1,)), ((), ())), preferred_element_type=jnp.float32)
    total = found[:8]
    for value in range(1, MAXT + 1):
        moved = pltpu.roll(found[value * 8 : value * 8 + 8], value * TT, 1)
        total = total + jnp.where(lane >= value * TT, moved, 0.0)
    return total


def tails(z, power_ref, edges_ref, pr_ref, band_ref, own_ref, other_ref, tab_ref, hits_ref,
          prev_ref, high_ref, bound_ref, sides_ref, inv_ref, y_ref, t_ref, e_ref, late_ref, weighted_ref, sums_ref, mean_ref):
    groups = z.groups
    boundary(z, pr_ref, band_ref, own_ref, other_ref, tab_ref, y_ref, t_ref, e_ref, bound_ref, sides_ref, inv_ref)
    carry = subbands(
        z, z.low_chunks, z.spec // CHUNK, power_ref, edges_ref, bound_ref, sides_ref, inv_ref, tab_ref,
        weighted_ref, sums_ref, mean_ref, high_ref,
    )
    count = z.high_rows
    done = z.spec - z.low_chunks * CHUNK
    for m in range(2):
        for step in range(FD - 1):
            high_ref[m, (done + step) * groups : (done + step + 1) * groups] = carry[m][step]
    high_ref[:, (done + FD - 1) * groups :] = jnp.zeros((2, (count + 1 - done - FD + 1) * groups, LANES), jnp.float32)
    blank = jnp.zeros((LANES - count, 2 * LANES), jnp.bfloat16)
    trials = late_ref.shape[1]
    lane = lax.broadcasted_iota(jnp.int32, (8, LANES), 1)
    start = done - (WMAX - 1)
    for g in range(groups):
        both = [high_ref[m, pl.ds(g, count, stride=groups)].astype(jnp.bfloat16) for m in range(2)]
        dd = delayed(z, hits_ref[g], jnp.concatenate([jnp.concatenate(both, 1), blank]))
        late = pltpu.roll(dd, LANES - start, 1)
        late_ref[g] = jnp.where(lane < WMAX - 1 + MAXT * TT + FD - 1, late, 0.0)[:trials]
    prev_ref[...] = late_ref[...].reshape(groups * trials, LANES).astype(jnp.bfloat16)


def bulk(z, power_ref, edges_ref, bound_ref, sides_ref, inv_ref, tab_ref, hits_ref, high_ref,
         main_ref, weighted_ref, sums_ref, mean_ref, low_ref, join_ref):
    groups = z.groups
    carry = subbands(
        z, 0, z.low_chunks, power_ref, edges_ref, bound_ref, sides_ref, inv_ref, tab_ref,
        weighted_ref, sums_ref, mean_ref, low_ref,
    )
    join_ref[...] = jnp.zeros_like(join_ref)
    for m in range(2):
        for step in range(FD - 1):
            join_ref[m, step * groups : (step + 1) * groups] = carry[m][step]
    low = z.low_chunks * CHUNK
    trials = main_ref.shape[1]
    for g in range(groups):
        both = []
        for m in range(2):
            edge = high_ref[m, pl.ds(g, 8, stride=groups)] + join_ref[m, pl.ds(g, 8, stride=groups)]
            rest = high_ref[m, pl.ds(8 * groups + g, z.spec - low - 8, stride=groups)]
            both.append(jnp.concatenate([low_ref[m, pl.ds(g, low, stride=groups)], edge, rest]).astype(jnp.bfloat16))
        main_ref[g] = delayed(z, hits_ref[g], jnp.concatenate(both, 1))[:trials]


def parcels(z, main_ref, prev_ref, owners_ref, stay_ref, leave_ref, late_ref, all_ref):
    me = lax.axis_index("dm")
    all_ref[...] = jnp.zeros_like(all_ref)
    late_ref[...] = prev_ref[...].astype(jnp.float32).reshape(late_ref.shape)
    for g in range(z.groups):
        owner = owners_ref[g]
        rank = jnp.int32(0)
        for earlier in range(g):
            rank = rank + jnp.where(owners_ref[earlier] == owner, 1, 0)
        all_ref[owner ^ me, 0, rank] = main_ref[g]
        all_ref[owner ^ me, 1, rank] = late_ref[g]
    half = z.n_dm // 2
    for r in range(z.n_dm):
        value = all_ref[r].reshape(stay_ref.shape[2:]).astype(jnp.bfloat16)
        (stay_ref if r < half else leave_ref)[r % half, 0] = value


def relay(held_ref, got_ref, stay_ref, leave_ref):
    count = held_ref.shape[1]
    half = held_ref.shape[0] // 2
    for r in range(2 * half):
        target = stay_ref if r < half else leave_ref
        target[r % half, :count] = held_ref[r]
        target[r % half, count:] = got_ref[r]


def boxes(z, widths_ref, *refs):
    held_ref, got_ref, out_ref, d_ref = refs
    early = lax.axis_index("tm") == 0
    me = lax.axis_index("dm")
    trials = out_ref.shape[3]
    near = held_ref.shape[1]
    rank = lax.broadcasted_iota(jnp.int32, (8, LANES), 0)
    count = widths_ref.shape[0]
    width = jnp.zeros((8, LANES), jnp.int32)
    for w in range(count):
        width = jnp.where(rank == w, widths_ref[w], width)
    norm = 1.0 / jnp.sqrt(width.astype(jnp.float32))
    weights = [jnp.where(width > lag, norm, 0.0) for lag in range(WMAX)]
    prior = WMAX - 1
    rows = z.capacity * trials
    order, bit = [0], z.n_dm // 2
    while bit:
        order, bit = order + [r + bit for r in order], bit // 2
    for place, r in enumerate(order):
        ref, at = (held_ref, place) if place < near else (got_ref, place - near)
        own = ref[0, at, :rows].astype(jnp.float32)
        past = jnp.where(early, 0.0, ref[0, at, rows:].astype(jnp.float32))
        wide = jnp.concatenate([own, jnp.zeros_like(own)], 1)
        wide = pltpu.roll(wide, prior, 1) + jnp.concatenate([past, jnp.zeros_like(past)], 1)
        for lag in range(WMAX):
            shift = prior - lag
            d_ref[r, lag] = (pltpu.roll(wide, 2 * LANES - shift, 1) if shift else wide)[:, :LANES]
        for s in range(z.capacity):
            for j in range(trials):
                acc = None
                for lag in range(WMAX):
                    part = d_ref[r, lag, s * trials + j : s * trials + j + 1, :] * weights[lag]
                    acc = part if acc is None else acc + part
                out_ref[s, me ^ r, 0, j] = acc[:count].astype(jnp.bfloat16)


def vmem_spec():
    return pl.BlockSpec(memory_space=pltpu.VMEM)


def smem_spec():
    return pl.BlockSpec(memory_space=pltpu.SMEM)


def hbm_spec():
    return pl.BlockSpec(memory_space=pltpu.HBM)


def kept(*values, space=pltpu.VMEM):
    return [pltpu.with_memory_space_constraint(value, space) for value in values]


def shards(n_dm, n_tm, raw, proto, delays, widths, owners):
    taps, channels = proto.shape
    groups, trials, _ = delays.shape
    z = Sizes(taps, channels, raw.shape[1] // channels, groups, n_dm, n_tm)
    tables, z.places = constants(z)
    params = pltpu.CompilerParams(vmem_limit_bytes=LIMIT)
    own_rows = z.raw_rows * (1 if n_tm == 2 else 2) + z.deep
    f32, bf16 = jnp.float32, jnp.bfloat16
    half = CHUNK // 2 * z.rows
    power, edges, pr, band, msg, tables, trial, owner, width = pl.pallas_call(
        functools.partial(channelize, z),
        out_shape=(
            pltpu.VMEM((z.spec, z.rows, LANES), f32),
            pltpu.VMEM((z.spec, LANES), f32),
            pltpu.VMEM((taps, 1, channels), f32),
            pltpu.VMEM((z.band_rows, LANES), f32),
            pltpu.VMEM((own_rows, LANES), bf16),
            pltpu.VMEM(tables.shape, bf16),
            pltpu.VMEM(delays.shape, jnp.int32),
            pltpu.SMEM((groups,), jnp.int32),
            pltpu.SMEM(widths.shape, jnp.int32),
        ),
        in_specs=[hbm_spec()] * 6,
        out_specs=[vmem_spec()] * 7 + [smem_spec()] * 2,
        scratch_shapes=[
            pltpu.VMEM((1, z.spec * channels), bf16),
            pltpu.VMEM((z.hist, DFT_A, LANES), f32),
            pltpu.VMEM((DFT_A, CHUNK * LANES), bf16),
            pltpu.VMEM((DFT_A, CHUNK * LANES), bf16),
            pltpu.VMEM((2 * half + 16, 2 * LANES), bf16),
            pltpu.VMEM((2 * half + 16, 2 * LANES), bf16),
            pltpu.VMEM((16, LANES), f32),
            pltpu.VMEM((16, LANES), f32),
            pltpu.VMEM((16, LANES), f32),
            pltpu.SemaphoreType.DMA((4,)),
        ],
        compiler_params=params,
        name="channelize",
    )(
        *kept(raw, proto, tables, delays, owners.reshape(groups), widths, space=pltpu.HBM)
    )
    if n_tm == 2:
        own, other = msg, lax.ppermute(msg, "tm", [(0, 1), (1, 0)])
    else:
        every = lax.all_gather(msg, "tm")
        lasts = every[:-1, : z.raw_rows].reshape(-1, LANES)
        firsts = every[1:, z.raw_rows : 2 * z.raw_rows].reshape(-1, LANES)
        rest = lax.psum(band, "tm") - band
        rest = jnp.concatenate([rest, jnp.zeros((z.deep - z.band_rows, LANES), f32)]).astype(bf16)
        own, other = jnp.concatenate([lasts, rest]), jnp.concatenate([firsts, rest])
    hits = pl.pallas_call(
        functools.partial(coarse, z),
        out_shape=pltpu.VMEM((groups, (MAXT + 1) * 8, 2 * LANES), bf16),
        in_specs=[vmem_spec()] * 2,
        out_specs=vmem_spec(),
        compiler_params=params,
        name="coarse",
    )(*kept(tables, trial))
    work = [
        pltpu.VMEM((z.band_rows, LANES), f32),
        pltpu.VMEM((CHUNK * 8 + 8, LANES), f32),
        pltpu.VMEM((z.spec, LANES), f32),
    ]
    prev, high, bound, sides, inv = pl.pallas_call(
        functools.partial(tails, z),
        out_shape=(
            pltpu.VMEM((groups * trials, LANES), bf16),
            pltpu.VMEM((2, (z.high_rows + 1) * groups, LANES), f32),
            pltpu.VMEM((z.bounds * z.hist, z.rows, LANES), f32),
            pltpu.VMEM((z.bounds, 16, LANES), f32),
            pltpu.VMEM((z.band_rows, LANES), f32),
        ),
        in_specs=[vmem_spec()] * 8,
        out_specs=[vmem_spec()] * 5,
        scratch_shapes=[
            pltpu.VMEM((DFT_A, (z.hist + 1) * LANES), bf16),
            pltpu.VMEM((z.hist * z.rows + 16, 2 * LANES), bf16),
            pltpu.VMEM((16, LANES), f32),
            pltpu.VMEM((groups, trials, LANES), f32),
        ]
        + work,
        compiler_params=params,
        name="tails",
    )(*kept(power, edges, pr, band, own, other, tables, hits))
    before = lax.ppermute(prev, "tm", [(i, (i + 1) % n_tm) for i in range(n_tm)])
    main = pl.pallas_call(
        functools.partial(bulk, z),
        out_shape=pltpu.VMEM((groups, trials, LANES), f32),
        in_specs=[vmem_spec()] * 8,
        out_specs=vmem_spec(),
        scratch_shapes=work
        + [
            pltpu.VMEM((2, (z.low_chunks * CHUNK + 1) * groups, LANES), f32),
            pltpu.VMEM((2, 9 * groups, LANES), f32),
        ],
        compiler_params=params,
        cost_estimate=pl.CostEstimate(flops=10**9, bytes_accessed=8 * 10**6, transcendentals=0),
        name="bulk",
    )(*kept(power, edges, bound, sides, inv, tables, hits, high))
    slots = (2, z.capacity, trials, LANES)
    parcel = (2 * z.capacity * trials, LANES)
    held, leaving = pl.pallas_call(
        functools.partial(parcels, z),
        out_shape=(pltpu.VMEM((n_dm // 2, 1, *parcel), bf16),) * 2,
        in_specs=[vmem_spec()] * 2 + [smem_spec()],
        out_specs=[vmem_spec()] * 2,
        scratch_shapes=[pltpu.VMEM((groups, trials, LANES), f32), pltpu.VMEM((n_dm, *slots), f32)],
        compiler_params=params,
        name="parcels",
    )(*kept(main, before), *kept(owner, space=pltpu.SMEM))
    bit = n_dm // 2
    while True:
        got = lax.ppermute(leaving, "dm", [(i, i ^ bit) for i in range(n_dm)])
        bit //= 2
        if bit == 0:
            break
        held, leaving = pl.pallas_call(
            relay,
            out_shape=(pltpu.VMEM((bit, n_dm // 2 // bit, *parcel), bf16),) * 2,
            in_specs=[vmem_spec()] * 2,
            out_specs=[vmem_spec()] * 2,
            compiler_params=params,
            name="relay",
        )(*kept(held, got))
    return pl.pallas_call(
        functools.partial(boxes, z),
        out_shape=jax.ShapeDtypeStruct((z.capacity, n_dm, 1, trials, widths.shape[0], z.spec), bf16),
        in_specs=[smem_spec()] + [vmem_spec()] * 2,
        out_specs=vmem_spec(),
        scratch_shapes=[pltpu.VMEM((n_dm, WMAX, z.capacity * trials, LANES), f32)],
        compiler_params=params,
        name="boxes",
    )(*kept(width, space=pltpu.SMEM), *kept(held, got))


def solution(mesh):
    sizes = dict(mesh.shape)
    return jax.shard_map(
        functools.partial(shards, sizes["dm"], sizes["tm"]),
        mesh=mesh,
        in_specs=(P(("group", "dm", "beam"), "tm"), P(), P(), P(), P()),
        out_specs=P("dm", "group", "beam", None, None, "tm"),
        check_vma=False,
    )
```
